32 devices in a mesh: roll: 2 (over y), dom: 4 (over z), blk: 4 (over x, core).
Axes of the slice: x: 2, y: 2, z: 4, core: 2. Of those that a mesh axis runs over, the one named last changes fastest.
Arguments:
- basis: bfloat16 [256, 4, 128, 128], P('blk', 'dom', 'roll'), parts along dimension 2
- zone: int32 [4, 128, 128], P('dom', 'roll'), parts along dimension 1, may hold values from 0 to 15
- cond_table: float32 [16], replicated, may hold values from 0.1 to 0.4
- heat_table: float32 [16], replicated, may hold values from 0.25 to 1
Outputs:
- applied: bfloat16 [512, 4, 64, 128], P('roll', 'dom', 'blk'), parts along dimension 0
- reduced: float32 [256, 512], P(('dom', 'blk'), 'roll'), parts along dimension 1
The draws below stay inside these ranges and needn't reach their ends.
There are 2 independent parts, one for each index of `roll`. The reference program is written for one: setup_inputs(seed, part) draws one part's arguments, and reference() takes and returns one part's arrays. A program takes and returns all parts, laid end to end along the dimension named above; an argument that names none is the same for every part. Nothing has to cross between parts.
All inputs are finite; a program needn't handle non-finite values.
Results may differ from the reference program's by a relative error of at most 0.0035.
Values may be sent and summed in bfloat16 or wider, within the bound.
No kernel may reach another device: no remote copies, remote signals or barrier semaphores. Data moves between devices by JAX's collectives and lax.ppermute only.
A program may use at most 64 MiB of HBM per device.

```python
import math
import jax
import jax.numpy as jnp
from jax import lax

K = 256
ZONES = 16
CX = 1
NY = 64
NZ = 128
NX = 4
N_DOM = 4
N_BLK = 4


def draw_basis(key, part):
    key = jax.random.fold_in(key, 11)
    keys = jax.random.split(key, 5)
    shape = (K, NX, NY, NZ)
    mixing = 0.7 * jax.random.normal(keys[0], (4, K), jnp.float32)
    value = jnp.zeros(shape, jnp.float32)
    for which in range(4):
        field = jax.random.normal(jax.random.fold_in(keys[1], which), (NX, NY, NZ), jnp.float32)
        value = value + mixing[which][:, None, None, None] * field[None]
    noise = jax.random.normal(keys[2], shape, jnp.float32)
    regions = N_DOM * N_BLK
    order = jax.random.permutation(keys[4], regions)
    owner = order[jnp.arange(K) % regions]
    xs = jnp.arange(NX) // CX
    ys = jnp.arange(NY) // (NY // N_BLK)
    here = xs[:, None] * N_BLK + ys[None, :]
    boost = jnp.where(here[None] == owner[:, None, None], 4.0, 1.0)[..., None]
    value = (value + noise) * boost
    return value.astype(jnp.bfloat16)


def draw_zone(key, part):
    key = jax.random.fold_in(key, 23)
    keys = jax.random.split(key, 3)
    span = max(NX // 16, 1)
    blocks = (NX + span - 1) // span
    block_zone = jax.random.randint(keys[0], (blocks, 2), 0, ZONES)
    xs = jnp.arange(NX) // span
    ys = jnp.arange(NY) * 2 // NY
    base = block_zone[xs[:, None], ys[None, :]]
    stray = jax.random.randint(keys[1], (NX, NY, NZ), 0, ZONES)
    picker = jax.random.randint(keys[2], (NX, NY, NZ), 0, 5)
    return jnp.where(picker == 0, stray, base[:, :, None]).astype(jnp.int32)


def setup_inputs(seed: int = 0, part: int = 0) -> dict:
    arg_keys = jax.random.split(jax.random.key(seed), 5)
    part_splits = jax.random.split(jax.random.fold_in(arg_keys[4], part), 5)
    basis = draw_basis(jax.random.fold_in(jax.random.fold_in(arg_keys[4], part), 71), part)
    zone = draw_zone(jax.random.fold_in(jax.random.fold_in(arg_keys[4], part), 71), part)
    cond_table = jnp.clip(jnp.exp(jax.random.uniform(arg_keys[2], (ZONES,), jnp.float32, math.log(0.1), math.log(0.4))), 0.1, 0.4)
    heat_table = jnp.clip(jnp.exp(jax.random.uniform(arg_keys[3], (ZONES,), jnp.float32, math.log(0.25), math.log(1.0))), 0.25, 1.0)
    return dict(basis=basis, zone=zone, cond_table=cond_table, heat_table=heat_table)


def table_lookup(zone, table):
    result = jnp.zeros(zone.shape, jnp.float32)
    for which in range(ZONES):
        result = jnp.where(zone == which, table[which], result)
    return result


def shifted(grid, axis, start):
    result = grid
    for which in range(3):
        dim = grid.ndim - 3 + which
        extent = grid.shape[dim]
        lower = start if which == axis else 1
        result = lax.slice_in_dim(result, lower, lower + extent - 2, axis=dim)
    return result


def apply_operator(padded, cond, heat):
    values = padded.astype(jnp.float32)
    center = values[:, 1:-1, 1:-1, 1:-1]
    own = cond[1:-1, 1:-1, 1:-1]
    total = heat * center
    for axis in range(3):
        for start in (0, 2):
            face = 0.5 * (own + shifted(cond, axis, start))
            total = total + face * (center - shifted(values, axis, start))
    return total


def reference(basis, zone, cond_table, heat_table):
    cond = lax.optimization_barrier(table_lookup(zone, cond_table).astype(jnp.bfloat16)).astype(jnp.float32)
    heat = table_lookup(zone, heat_table)
    value_padded = jnp.pad(basis, ((0, 0), (1, 1), (1, 1), (1, 1)))
    cpad = jnp.pad(cond, 1)

    def plane(gram, index_value):
        block_slice = lax.dynamic_slice_in_dim(value_padded, index_value, 3, 1)
        kblock = lax.dynamic_slice_in_dim(cpad, index_value, 3, 0)
        hrow = lax.dynamic_slice_in_dim(heat, index_value, 1, 0)
        image = apply_operator(block_slice, kblock, hrow).astype(jnp.bfloat16)
        own = lax.dynamic_slice_in_dim(basis, index_value, 1, 1)
        gram = gram + lax.dot_general(own.reshape(K, -1), image.reshape(K, -1), (((1,), (1,)), ((), ())), preferred_element_type=jnp.float32)
        return gram, image[:, 0]

    gram, images = lax.scan(plane, jnp.zeros((K, K), jnp.float32), jnp.arange(NX, dtype=jnp.int32))
    applied = jnp.transpose(images, (1, 0, 2, 3))
    weight = 1.0 / (NX * NY * NZ)
    return applied, gram * weight
```

```python
import functools

import jax
import jax.numpy as jnp
from jax import lax
from jax.experimental import pallas as pl
from jax.experimental.pallas import tpu as pltpu
from jax.sharding import PartitionSpec as P

ZONES = 16
F32 = jnp.float32
BF16 = jnp.bfloat16


def lookup(zone, table_ref):
    result = jnp.zeros(zone.shape, F32)
    for which in range(ZONES):
        result = jnp.where(zone == which, table_ref[which], result)
    return result


def cond_of(zone, table_ref):
    return lookup(zone, table_ref).astype(BF16).astype(F32)


def prepare_kernel(blocks, basis_ref, zone_ref, cond_ref, *refs):
    centers, slabs, mains, edges, (wide, turned, cond_pad, sems) = (
        refs[0:2], refs[2:4], refs[4:2 + blocks], refs[2 + blocks:2 * blocks], refs[2 * blocks:],
    )
    columns, _, ny, nz = basis_ref.shape
    rows = ny // blocks
    me = lax.axis_index("blk")
    for c in range(columns):
        wide[c * ny:(c + 1) * ny, :] = basis_ref[c, 0].astype(F32)
    zero = jnp.zeros((columns, nz), BF16)
    turned[0] = zero
    turned[ny + 1] = zero
    for y in range(ny):
        turned[y + 1] = wide[pl.ds(y, columns, stride=ny), :].astype(BF16)
    mine = zone_ref[0, pl.ds(pl.multiple_of(me * rows, rows), rows), :]
    own = cond_of(mine, cond_ref)
    cond_pad[...] = jnp.concatenate([own, jnp.zeros((columns - rows, nz), F32)], 0).astype(BF16)

    copies = []

    def send(source, target):
        copy = pltpu.make_async_copy(source, target, sems.at[len(copies)])
        copy.start()
        copies.append(copy)

    for s in range(blocks):
        first = (me ^ s) * rows
        if s < 2:
            send(turned.at[pl.ds(first, rows + 2)], centers[s])
            send(turned.at[pl.ds(first + 1, rows)], slabs[s].at[pl.ds(0, rows)])
        else:
            send(turned.at[pl.ds(first + 1, rows)], mains[s - 2])
            send(turned.at[pl.ds(first, 1)], edges[s - 2].at[pl.ds(0, 1)])
            send(turned.at[pl.ds(first + rows + 1, 1)], edges[s - 2].at[pl.ds(1, 1)])
    send(cond_pad, slabs[0].at[rows])
    for copy in copies:
        copy.wait()


def prepare(basis, zone, cond_table, blocks):
    columns, _, ny, nz = basis.shape
    rows = ny // blocks

    def out(n):
        return jax.ShapeDtypeStruct((n, columns, nz), BF16)

    vmem = pl.BlockSpec(memory_space=pltpu.VMEM)
    smem = pl.BlockSpec(memory_space=pltpu.SMEM)
    shapes = [out(rows + 2)] * 2 + [out(rows + 1), out(rows)] + [out(rows)] * (blocks - 2) + [out(2)] * (blocks - 2)
    results = pl.pallas_call(
        functools.partial(prepare_kernel, blocks),
        out_shape=shapes,
        in_specs=[vmem, vmem, smem],
        out_specs=[pl.BlockSpec(memory_space=pl.ANY)] * len(shapes),
        scratch_shapes=[
            pltpu.VMEM((columns * ny, nz), F32),
            pltpu.VMEM((ny + 2, columns, nz), BF16),
            pltpu.VMEM((columns, nz), BF16),
            pltpu.SemaphoreType.DMA((3 * blocks,)),
        ],
        compiler_params=pltpu.CompilerParams(vmem_limit_bytes=16 << 20),
    )(basis, zone, cond_table)
    return results[0:2], results[2:4], results[4:2 + blocks], results[2 + blocks:]


def apply_kernel(blocks, weight, zone_ref, cond_ref, heat_ref, *refs):
    centers, mains, edges, ups, downs = (
        refs[0:2], refs[2:blocks], refs[blocks:2 * blocks - 2],
        refs[2 * blocks - 2:3 * blocks - 2], refs[3 * blocks - 2:4 * blocks - 2],
    )
    applied_ref, gram_ref, cond_pad, coef, left, right, wide = refs[4 * blocks - 2:]
    _, columns, nz = ups[1].shape
    rows = ups[1].shape[0]
    ny = zone_ref.shape[1]
    me = lax.axis_index("blk")
    slab = lax.axis_index("dom")
    slabs = lax.axis_size("dom")

    cond_pad[0:8, :] = jnp.zeros((8, nz), F32)
    cond_pad[8:8 + ny, :] = cond_of(zone_ref[0], cond_ref)
    cond_pad[8 + ny:16 + ny, :] = jnp.zeros((8, nz), F32)
    base = pl.multiple_of(me * rows, 8)
    near = cond_pad[pl.ds(base, rows + 16), :]
    own = near[8:8 + rows]
    lane = lax.broadcasted_iota(jnp.int32, (rows, nz), 1)
    above = jnp.where(slab == slabs - 1, 0.0, ups[0][rows].astype(F32)[:rows])
    below = jnp.where(slab == 0, 0.0, downs[0][rows].astype(F32)[:rows])
    beside = (
        jnp.where(lane == 0, 0.0, pltpu.roll(own, 1, 1)),
        jnp.where(lane == nz - 1, 0.0, pltpu.roll(own, nz - 1, 1)),
    )
    coef[0] = lookup(zone_ref[0, pl.ds(base, rows), :], heat_ref)
    for which, other in enumerate((below, above, near[7:7 + rows], near[9:9 + rows], *beside)):
        coef[1 + which] = 0.5 * (own + other)

    lane = lax.broadcasted_iota(jnp.int32, (columns, nz), 1)
    first, last = lane == 0, lane == nz - 1
    for y in range(rows):
        face = [jnp.broadcast_to(coef[k, y:y + 1, :], (columns, nz)) for k in range(7)]
        for s in range(blocks):
            def row(at):
                if s < 2:
                    return centers[s][at + 1]
                if at < 0:
                    return edges[s - 2][0]
                return mains[s - 2][at] if at < rows else edges[s - 2][1]

            raw = row(y)
            v = raw.astype(F32)
            total = face[0] * v
            total += face[1] * (v - downs[s][y].astype(F32))
            total += face[2] * (v - ups[s][y].astype(F32))
            total += face[3] * (v - row(y - 1).astype(F32))
            total += face[4] * (v - row(y + 1).astype(F32))
            total += face[5] * (v - jnp.where(first, 0.0, pltpu.roll(v, 1, 1)))
            total += face[6] * (v - jnp.where(last, 0.0, pltpu.roll(v, nz - 1, 1)))
            image = total.astype(BF16)
            start = (me ^ s) * columns
            where = pl.ds(pl.multiple_of(start, columns), columns)
            left[where, y * nz:(y + 1) * nz] = raw
            right[where, y * nz:(y + 1) * nz] = image
            wide[pl.ds(start * rows + y, columns, stride=rows), :] = image.astype(F32)
    gram_ref[...] = weight * lax.dot_general(
        left[...], right[...], (((1,), (1,)), ((), ())), preferred_element_type=F32
    )
    for c in range(blocks * columns):
        applied_ref[c, 0] = wide[c * rows:(c + 1) * rows, :].astype(BF16)


def apply(zone, cond_table, heat_table, centers, mains, edges, ups, downs, weight):
    blocks = len(ups)
    rows, columns, nz = ups[1].shape
    ny = zone.shape[1]
    total = blocks * columns
    vmem = pl.BlockSpec(memory_space=pltpu.VMEM)
    smem = pl.BlockSpec(memory_space=pltpu.SMEM)
    pieces = (*centers, *mains, *edges, *ups, *downs)
    return pl.pallas_call(
        functools.partial(apply_kernel, blocks, weight),
        out_shape=(
            jax.ShapeDtypeStruct((total, 1, rows, nz), BF16),
            jax.ShapeDtypeStruct((total, total), F32),
        ),
        in_specs=[vmem, smem, smem] + [vmem] * len(pieces),
        out_specs=(vmem, vmem),
        scratch_shapes=[
            pltpu.VMEM((ny + 16, nz), F32),
            pltpu.VMEM((7, rows, nz), F32),
            pltpu.VMEM((total, rows * nz), BF16),
            pltpu.VMEM((total, rows * nz), BF16),
            pltpu.VMEM((total * rows, nz), F32),
        ],
        compiler_params=pltpu.CompilerParams(vmem_limit_bytes=32 << 20),
    )(zone, cond_table, heat_table, *pieces)


def per_device(basis, zone, cond_table, heat_table):
    blocks = lax.axis_size("blk")
    slabs = lax.axis_size("dom")
    columns = basis.shape[0] * blocks
    weight = 1.0 / (slabs * basis.shape[1] * basis.shape[2] * basis.shape[3])
    axes = ("dom", "blk")

    def across(array, s):
        return lax.ppermute(array, "blk", [(i, i ^ s) for i in range(blocks)])

    def along(array, step, s):
        pairs = [
            (d * blocks + b, (d + step) * blocks + (b ^ s))
            for d in range(slabs) if 0 <= d + step < slabs for b in range(blocks)
        ]
        return lax.ppermute(array, axes, pairs)

    centers, slab_rows, mains, edges = prepare(basis, zone, cond_table, blocks)
    mains = [across(main, s + 2) for s, main in enumerate(mains)]
    ups = [along(array, -1, s) for s, array in enumerate(slab_rows)]
    downs = [along(array, 1, s) for s, array in enumerate(slab_rows)]
    centers = [centers[0], across(centers[1], 1)]
    edges = [across(edge, s + 2) for s, edge in enumerate(edges)]
    ups += [along(main, -1, 0) for main in mains]
    downs += [along(main, 1, 0) for main in mains]
    applied, gram = apply(zone, cond_table, heat_table, centers, mains, edges, ups, downs, weight)
    parts = slabs * blocks
    shares = gram.reshape(parts, columns // parts, columns)
    shares = lax.all_to_all(shares, axes, split_axis=0, concat_axis=0, tiled=True)
    return applied, shares.sum(0)


def solution(mesh):
    placed = (P("blk", "dom", "roll", None), P("dom", "roll", None), P(), P())
    return jax.shard_map(
        per_device,
        mesh=mesh,
        in_specs=placed,
        out_specs=(P("roll", "dom", "blk", None), P(("dom", "blk"), "roll")),
        check_vma=False,
    )
```

```python
import functools

import jax
import jax.numpy as jnp
from jax import lax
from jax.experimental import pallas as pl
from jax.experimental.pallas import tpu as pltpu
from jax.sharding import PartitionSpec as P

ZONES = 16
CORES = 2
F32 = jnp.float32
BF16 = jnp.bfloat16
VMEM = pl.BlockSpec(memory_space=pltpu.VMEM)
SMEM = pl.BlockSpec(memory_space=pltpu.SMEM)
HBM = pl.BlockSpec(memory_space=pltpu.HBM)


def lookup(zone, table_ref):
    result = jnp.zeros(zone.shape, F32)
    for which in range(ZONES):
        result = jnp.where(zone == which, table_ref[which], result)
    return result


def cond_of(zone, table_ref):
    return lookup(zone, table_ref).astype(BF16).astype(F32)


def prepare_kernel(chips, basis_hbm, zone_hbm, cond_hbm, *refs):
    outs, (basis, zone, table, wide, turned, cond_pad, in_sems, out_sems) = refs[:chips + 1], refs[chips + 1:]
    columns, _, ny, nz = basis.shape
    rows = ny // chips
    chip = lax.axis_index("blk") // CORES
    step = 16
    chunks = columns // step
    loads = [
        pltpu.make_async_copy(basis_hbm.at[pl.ds(i * step, step)], basis.at[pl.ds(i * step, step)], in_sems.at[i])
        for i in range(chunks)
    ]
    loads.append(pltpu.make_async_copy(zone_hbm, zone, in_sems.at[chunks]))
    loads.append(pltpu.make_async_copy(cond_hbm, table, in_sems.at[chunks + 1]))
    for load in loads:
        load.start()
    turned[0] = jnp.zeros((columns, nz), BF16)
    turned[ny + 1] = jnp.zeros((columns, nz), BF16)
    for i in range(chunks):
        loads[i].wait()
        for c in range(i * step, (i + 1) * step):
            wide[c * ny:(c + 1) * ny, :] = basis[c, 0].astype(F32)
        for y in range(ny):
            block = wide[pl.ds(i * step * ny + y, step, stride=ny), :]
            turned[y + 1, i * step:(i + 1) * step, :] = block.astype(BF16)
    loads[chunks].wait()
    loads[chunks + 1].wait()
    mine = zone[0, pl.ds(pl.multiple_of(chip * rows, rows), rows), :]
    own = cond_of(mine, table)
    cond_pad[...] = jnp.concatenate([own, jnp.zeros((columns - rows, nz), F32)], 0).astype(BF16)

    stores = [
        pltpu.make_async_copy(turned.at[pl.ds((chip ^ k) * rows, rows + 2)], outs[1 + k], out_sems.at[k])
        for k in range(chips)
    ]
    stores.append(
        pltpu.make_async_copy(turned.at[pl.ds(chip * rows + 1, rows)], outs[0].at[pl.ds(0, rows)], out_sems.at[chips])
    )
    stores.append(pltpu.make_async_copy(cond_pad, outs[0].at[rows], out_sems.at[chips + 1]))
    for store in stores:
        store.start()
    for store in stores:
        store.wait()


def prepare(basis, zone, cond_table, chips):
    columns, _, ny, nz = basis.shape
    rows = ny // chips
    shapes = [jax.ShapeDtypeStruct((rows + 1, columns, nz), BF16)]
    shapes += [jax.ShapeDtypeStruct((rows + 2, columns, nz), BF16)] * chips
    results = pl.pallas_call(
        functools.partial(prepare_kernel, chips),
        out_shape=shapes,
        in_specs=[HBM, HBM, HBM],
        out_specs=[pl.BlockSpec(memory_space=pl.ANY)] * len(shapes),
        scratch_shapes=[
            pltpu.VMEM(basis.shape, BF16),
            pltpu.VMEM(zone.shape, jnp.int32),
            pltpu.SMEM((ZONES,), F32),
            pltpu.VMEM((columns * ny, nz), F32),
            pltpu.VMEM((ny + 2, columns, nz), BF16),
            pltpu.VMEM((columns, nz), BF16),
            pltpu.SemaphoreType.DMA((columns // 16 + 2,)),
            pltpu.SemaphoreType.DMA((chips + 2,)),
        ],
        compiler_params=pltpu.CompilerParams(vmem_limit_bytes=16 << 20),
    )(basis, zone, cond_table)
    return results[0], results[1], results[2:]


def image_rows(coef, center, one, two, skip, mine, theirs, flat):
    rows = coef.shape[1]
    columns, nz = center.shape[1:]
    half = rows // CORES
    core = lax.axis_index("blk") % CORES
    lane = lax.broadcasted_iota(jnp.int32, (columns, nz), 1)
    first, last = lane == 0, lane == nz - 1
    for y in range(rows):
        face = [jnp.broadcast_to(coef[k, y:y + 1, :], (columns, nz)) for k in range(7)]
        v = center[y + 1].astype(F32)
        total = face[0] * v
        total += face[1] * (v - one[y + skip].astype(F32))
        total += face[2] * (v - two[y + skip].astype(F32))
        total += face[3] * (v - center[y].astype(F32))
        total += face[4] * (v - center[y + 2].astype(F32))
        total += face[5] * (v - jnp.where(first, 0.0, pltpu.roll(v, 1, 1)))
        total += face[6] * (v - jnp.where(last, 0.0, pltpu.roll(v, nz - 1, 1)))
        flat[:, y * nz:(y + 1) * nz] = total.astype(BF16)
    for y in range(half):
        low = flat[:, y * nz:(y + 1) * nz]
        high = flat[:, (half + y) * nz:(half + y + 1) * nz]
        mine[y] = jnp.where(core == 0, low, high)
        theirs[y] = jnp.where(core == 0, high, low)


def gram_of(left, flat):
    return lax.dot_general(left[...], flat[...], (((1,), (1,)), ((), ())), preferred_element_type=F32)


def near_kernel(chips, weight, zone_ref, cond_ref, heat_ref, center, one, two, *refs):
    others, (mine, theirs, coef, left, gram, cond_pad, flat) = refs[:2 * chips - 1], refs[2 * chips - 1:]
    rows = center.shape[0] - 2
    columns, nz = center.shape[1:]
    ny = zone_ref.shape[1]
    me = lax.axis_index("blk")
    chip = me // CORES

    cond_pad[0:8, :] = jnp.zeros((8, nz), F32)
    cond_pad[8:8 + ny, :] = cond_of(zone_ref[0], cond_ref)
    cond_pad[8 + ny:16 + ny, :] = jnp.zeros((8, nz), F32)
    base = pl.multiple_of(chip * rows, 8)
    near = cond_pad[pl.ds(base, rows + 16), :]
    own = near[8:8 + rows]
    lane = lax.broadcasted_iota(jnp.int32, (rows, nz), 1)
    coef[0] = lookup(zone_ref[0, pl.ds(base, rows), :], heat_ref)
    beside = (
        one[rows].astype(F32)[:rows],
        two[rows].astype(F32)[:rows],
        near[7:7 + rows],
        near[9:9 + rows],
        jnp.where(lane == 0, 0.0, pltpu.roll(own, 1, 1)),
        jnp.where(lane == nz - 1, 0.0, pltpu.roll(own, nz - 1, 1)),
    )
    for which, other in enumerate(beside):
        coef[1 + which] = 0.5 * (own + other)

    image_rows(coef, center, one, two, 0, mine, theirs, flat)
    pieces = [(center, 0)]
    pieces += [(ref, CORES * (k + 1)) for k, ref in enumerate(others[:chips - 1])]
    pieces += [(ref, CORES * k + 1) for k, ref in enumerate(others[chips - 1:])]
    for ref, partner in pieces:
        where = pl.ds(pl.multiple_of((me ^ partner) * columns, columns), columns)
        for y in range(rows):
            left[where, y * nz:(y + 1) * nz] = ref[y + 1]
    gram[...] = weight * gram_of(left, flat)


def far_kernel(chips, weight, coef, left, near_gram, *refs):
    count = chips - 1
    centers, ones, twos, mine, theirs = (refs[i * count:(i + 1) * count] for i in range(5))
    gram, flat = refs[5 * count:]
    columns = centers[0].shape[1]
    gram[:, 0:columns] = near_gram[...]
    for k in range(count):
        image_rows(coef, centers[k], ones[k], twos[k], 1, mine[k], theirs[k], flat)
        gram[:, (k + 1) * columns:(k + 2) * columns] = weight * gram_of(left, flat)


def finish_kernel(blocks, *refs):
    images, (applied, wide) = refs[:blocks], refs[blocks:]
    rows, columns, nz = images[0].shape
    me = lax.axis_index("blk")
    for s, image in enumerate(images):
        for y in range(rows):
            wide[pl.ds(y, columns, stride=rows), :] = image[y].astype(F32)
        start = (me ^ s) * columns
        for c in range(columns):
            applied[start + c, 0] = wide[c * rows:(c + 1) * rows, :].astype(BF16)


def sum_kernel(slabs, blocks, shares, out):
    chips = blocks // CORES
    columns = shares.shape[2] // chips
    for core in range(CORES):
        sums = []
        for chip in range(chips):
            total = shares[CORES * chip + core]
            for slab in range(1, slabs):
                total += shares[slab * blocks + CORES * chip + core]
            sums.append(total)
        for target in range(chips):
            parts = [sums[chip][:, (chip ^ target) * columns:((chip ^ target) + 1) * columns] for chip in range(chips)]
            start = (CORES * target + core) * columns
            out[:, start:start + columns] = functools.reduce(jnp.add, parts)


def per_device(basis, zone, cond_table, heat_table):
    blocks = lax.axis_size("blk")
    slabs = lax.axis_size("dom")
    chips = blocks // CORES
    columns, planes, ny, nz = basis.shape
    rows = ny // chips
    half = ny // blocks
    total = columns * blocks
    weight = 1.0 / (slabs * planes * ny * nz)

    def swap(array, s):
        return lax.ppermute(array, "blk", [(i, i ^ s) for i in range(blocks)])

    def along(array):
        result = []
        for offset in (0, 1):
            partner = [((d + offset) ^ 1) - offset for d in range(slabs)]
            pairs = [(d, to) for d, to in enumerate(partner) if 0 <= to < slabs]
            result.append(lax.ppermute(array, "dom", pairs))
        return result

    sent, center, others = prepare(basis, zone, cond_table, chips)
    others = [swap(other, CORES * (k + 1)) for k, other in enumerate(others)]
    one, two = along(sent)
    theirs = [swap(center, 1)]
    far = [along(other) for other in others]
    theirs += [swap(other, 1) for other in others]

    image = jax.ShapeDtypeStruct((half, columns, nz), BF16)
    left = jax.ShapeDtypeStruct((total, rows * nz), BF16)
    flat = pltpu.VMEM((columns, rows * nz), BF16)
    params = pltpu.CompilerParams(vmem_limit_bytes=32 << 20)
    near_mine, near_theirs, coef, left, near_gram = pl.pallas_call(
        functools.partial(near_kernel, chips, weight),
        out_shape=(
            image, image, jax.ShapeDtypeStruct((7, rows, nz), F32), left, jax.ShapeDtypeStruct((total, columns), F32),
        ),
        in_specs=[VMEM, SMEM, SMEM] + [VMEM] * (2 * chips + 2),
        out_specs=[VMEM] * 5,
        scratch_shapes=[pltpu.VMEM((ny + 16, nz), F32), flat],
        compiler_params=params,
    )(zone, cond_table, heat_table, center, one, two, *others, *theirs)

    count = chips - 1
    *images, gram = pl.pallas_call(
        functools.partial(far_kernel, chips, weight),
        out_shape=[image] * (2 * count) + [jax.ShapeDtypeStruct((total, chips * columns), F32)],
        in_specs=[VMEM] * (3 + 3 * count),
        out_specs=[VMEM] * (2 * count + 1),
        scratch_shapes=[flat],
        compiler_params=params,
    )(coef, left, near_gram, *others, *(one for one, _ in far), *(two for _, two in far))

    near_theirs = swap(near_theirs, 1)
    far_theirs = [swap(array, 1) for array in images[count:]]
    pieces = [near_mine, near_theirs]
    for k in range(count):
        pieces += [images[k], far_theirs[k]]
    applied = pl.pallas_call(
        functools.partial(finish_kernel, blocks),
        out_shape=jax.ShapeDtypeStruct((total, 1, half, nz), BF16),
        in_specs=[VMEM] * blocks,
        out_specs=VMEM,
        scratch_shapes=[pltpu.VMEM((columns * half, nz), F32)],
        compiler_params=params,
    )(*pieces)

    parts = slabs * blocks
    shares = gram.reshape(parts, total // parts, chips * columns)
    shares = lax.all_to_all(shares, ("dom", "blk"), split_axis=0, concat_axis=0, tiled=True)
    reduced = pl.pallas_call(
        functools.partial(sum_kernel, slabs, blocks),
        out_shape=jax.ShapeDtypeStruct((total // parts, total), F32),
        in_specs=[VMEM],
        out_specs=VMEM,
    )(shares)
    return applied, reduced


def solution(mesh):
    placed = (P("blk", "dom", "roll", None), P("dom", "roll", None), P(), P())
    return jax.shard_map(
        per_device,
        mesh=mesh,
        in_specs=placed,
        out_specs=(P("roll", "dom", "blk", None), P(("dom", "blk"), "roll")),
        check_vma=False,
    )
```

```python
import functools

import jax
import jax.numpy as jnp
from jax import lax
from jax.experimental import pallas as pl
from jax.experimental.pallas import tpu as pltpu
from jax.sharding import PartitionSpec as P

ZONES = 16
CORES = 2
F32 = jnp.float32
BF16 = jnp.bfloat16
VMEM = pl.BlockSpec(memory_space=pltpu.VMEM)
SMEM = pl.BlockSpec(memory_space=pltpu.SMEM)
HBM = pl.BlockSpec(memory_space=pltpu.HBM)


def lookup(zone, table_ref):
    result = jnp.zeros(zone.shape, F32)
    for which in range(ZONES):
        result = jnp.where(zone == which, table_ref[which], result)
    return result


def cond_of(zone, table_ref):
    return lookup(zone, table_ref).astype(BF16).astype(F32)


def prepare_kernel(chips, basis_hbm, zone_hbm, cond_hbm, *refs):
    outs, (basis, zone, table, wide, turned, cond_pad, in_sems, out_sems) = refs[:chips + 1], refs[chips + 1:]
    columns, _, ny, nz = basis.shape
    rows = ny // chips
    chip = lax.axis_index("blk") // CORES
    step = 16
    chunks = columns // step
    loads = [
        pltpu.make_async_copy(basis_hbm.at[pl.ds(i * step, step)], basis.at[pl.ds(i * step, step)], in_sems.at[i])
        for i in range(chunks)
    ]
    loads.append(pltpu.make_async_copy(zone_hbm, zone, in_sems.at[chunks]))
    loads.append(pltpu.make_async_copy(cond_hbm, table, in_sems.at[chunks + 1]))
    for load in loads:
        load.start()
    turned[0] = jnp.zeros((columns, nz), BF16)
    turned[ny + 1] = jnp.zeros((columns, nz), BF16)
    for i in range(chunks):
        loads[i].wait()
        for c in range(i * step, (i + 1) * step):
            wide[c * ny:(c + 1) * ny, :] = basis[c, 0].astype(F32)
        for y in range(ny):
            block = wide[pl.ds(i * step * ny + y, step, stride=ny), :]
            turned[y + 1, i * step:(i + 1) * step, :] = block.astype(BF16)
    loads[chunks].wait()
    loads[chunks + 1].wait()
    mine = zone[0, pl.ds(pl.multiple_of(chip * rows, rows), rows), :]
    own = cond_of(mine, table)
    cond_pad[...] = jnp.concatenate([own, jnp.zeros((columns - rows, nz), F32)], 0).astype(BF16)

    stores = [
        pltpu.make_async_copy(turned.at[pl.ds((chip ^ k) * rows, rows + 2)], outs[1 + k], out_sems.at[k])
        for k in range(chips)
    ]
    stores.append(
        pltpu.make_async_copy(turned.at[pl.ds(chip * rows + 1, rows)], outs[0].at[pl.ds(0, rows)], out_sems.at[chips])
    )
    stores.append(pltpu.make_async_copy(cond_pad, outs[0].at[rows], out_sems.at[chips + 1]))
    for store in stores:
        store.start()
    for store in stores:
        store.wait()


def prepare(basis, zone, cond_table, chips):
    columns, _, ny, nz = basis.shape
    rows = ny // chips
    shapes = [jax.ShapeDtypeStruct((rows + 1, columns, nz), BF16)]
    shapes += [jax.ShapeDtypeStruct((rows + 2, columns, nz), BF16)] * chips
    results = pl.pallas_call(
        functools.partial(prepare_kernel, chips),
        out_shape=shapes,
        in_specs=[HBM, HBM, HBM],
        out_specs=[pl.BlockSpec(memory_space=pl.ANY)] * len(shapes),
        scratch_shapes=[
            pltpu.VMEM(basis.shape, BF16),
            pltpu.VMEM(zone.shape, jnp.int32),
            pltpu.SMEM((ZONES,), F32),
            pltpu.VMEM((columns * ny, nz), F32),
            pltpu.VMEM((ny + 2, columns, nz), BF16),
            pltpu.VMEM((columns, nz), BF16),
            pltpu.SemaphoreType.DMA((columns // 16 + 2,)),
            pltpu.SemaphoreType.DMA((chips + 2,)),
        ],
        compiler_params=pltpu.CompilerParams(vmem_limit_bytes=60 << 20),
    )(basis, zone, cond_table)
    return results[0], results[1], results[2:]


def image_rows(coef, center, one, two, skip, mine, theirs, flat):
    rows = coef.shape[1]
    columns, nz = center.shape[1:]
    half = rows // CORES
    core = lax.axis_index("blk") % CORES
    lane = lax.broadcasted_iota(jnp.int32, (columns, nz), 1)
    first, last = lane == 0, lane == nz - 1
    for y in range(rows):
        face = [jnp.broadcast_to(coef[k, y:y + 1, :], (columns, nz)) for k in range(7)]
        v = center[y + 1].astype(F32)
        total = face[0] * v
        total += face[1] * (v - one[y + skip].astype(F32))
        total += face[2] * (v - two[y + skip].astype(F32))
        total += face[3] * (v - center[y].astype(F32))
        total += face[4] * (v - center[y + 2].astype(F32))
        total += face[5] * (v - jnp.where(first, 0.0, pltpu.roll(v, 1, 1)))
        total += face[6] * (v - jnp.where(last, 0.0, pltpu.roll(v, nz - 1, 1)))
        flat[:, y * nz:(y + 1) * nz] = total.astype(BF16)
    for y in range(half):
        low = flat[:, y * nz:(y + 1) * nz]
        high = flat[:, (half + y) * nz:(half + y + 1) * nz]
        mine[y] = jnp.where(core == 0, low, high)
        theirs[y] = jnp.where(core == 0, high, low)


def gram_of(left, flat):
    return lax.dot_general(left[...], flat[...], (((1,), (1,)), ((), ())), preferred_element_type=F32)


def near_kernel(chips, weight, zone_ref, cond_ref, heat_ref, center, one, two, *refs):
    others, (mine, theirs, coef, left, gram, cond_pad, flat) = refs[:2 * chips - 1], refs[2 * chips - 1:]
    rows = center.shape[0] - 2
    columns, nz = center.shape[1:]
    ny = zone_ref.shape[1]
    me = lax.axis_index("blk")
    chip = me // CORES

    cond_pad[0:8, :] = jnp.zeros((8, nz), F32)
    cond_pad[8:8 + ny, :] = cond_of(zone_ref[0], cond_ref)
    cond_pad[8 + ny:16 + ny, :] = jnp.zeros((8, nz), F32)
    base = pl.multiple_of(chip * rows, 8)
    near = cond_pad[pl.ds(base, rows + 16), :]
    own = near[8:8 + rows]
    lane = lax.broadcasted_iota(jnp.int32, (rows, nz), 1)
    coef[0] = lookup(zone_ref[0, pl.ds(base, rows), :], heat_ref)
    beside = (
        one[rows].astype(F32)[:rows],
        two[rows].astype(F32)[:rows],
        near[7:7 + rows],
        near[9:9 + rows],
        jnp.where(lane == 0, 0.0, pltpu.roll(own, 1, 1)),
        jnp.where(lane == nz - 1, 0.0, pltpu.roll(own, nz - 1, 1)),
    )
    for which, other in enumerate(beside):
        coef[1 + which] = 0.5 * (own + other)

    image_rows(coef, center, one, two, 0, mine, theirs, flat)
    pieces = [(center, 0)]
    pieces += [(ref, CORES * (k + 1)) for k, ref in enumerate(others[:chips - 1])]
    pieces += [(ref, CORES * k + 1) for k, ref in enumerate(others[chips - 1:])]
    for ref, partner in pieces:
        where = pl.ds(pl.multiple_of((me ^ partner) * columns, columns), columns)
        for y in range(rows):
            left[where, y * nz:(y + 1) * nz] = ref[y + 1]
    gram[...] = weight * gram_of(left, flat)


def far_kernel(chips, weight, coef, left, near_gram, *refs):
    count = chips - 1
    centers, ones, twos, mine, theirs = (refs[i * count:(i + 1) * count] for i in range(5))
    gram, flat = refs[5 * count:]
    columns = centers[0].shape[1]
    gram[:, 0:columns] = near_gram[...]
    for k in range(count):
        image_rows(coef, centers[k], ones[k], twos[k], 1, mine[k], theirs[k], flat)
        gram[:, (k + 1) * columns:(k + 2) * columns] = weight * gram_of(left, flat)


def finish_kernel(blocks, *refs):
    images, (applied, wide) = refs[:blocks], refs[blocks:]
    rows, columns, nz = images[0].shape
    me = lax.axis_index("blk")
    for s, image in enumerate(images):
        for y in range(rows):
            wide[pl.ds(y, columns, stride=rows), :] = image[y].astype(F32)
        start = (me ^ s) * columns
        for c in range(columns):
            applied[start + c, 0] = wide[c * rows:(c + 1) * rows, :].astype(BF16)


def sum_kernel(slabs, blocks, shares, out):
    chips = blocks // CORES
    columns = shares.shape[2] // chips
    for core in range(CORES):
        sums = []
        for chip in range(chips):
            total = shares[CORES * chip + core]
            for slab in range(1, slabs):
                total += shares[slab * blocks + CORES * chip + core]
            sums.append(total)
        for target in range(chips):
            parts = [sums[chip][:, (chip ^ target) * columns:((chip ^ target) + 1) * columns] for chip in range(chips)]
            start = (CORES * target + core) * columns
            out[:, start:start + columns] = functools.reduce(jnp.add, parts)


def per_device(basis, zone, cond_table, heat_table):
    blocks = lax.axis_size("blk")
    slabs = lax.axis_size("dom")
    chips = blocks // CORES
    columns, planes, ny, nz = basis.shape
    rows = ny // chips
    half = ny // blocks
    total = columns * blocks
    weight = 1.0 / (slabs * planes * ny * nz)

    def swap(array, s):
        return lax.ppermute(array, "blk", [(i, i ^ s) for i in range(blocks)])

    def exchange(array, offset):
        partner = [((d + offset) ^ 1) - offset for d in range(slabs)]
        return lax.ppermute(array, "dom", [(d, to) for d, to in enumerate(partner) if 0 <= to < slabs])

    sent, center, others = prepare(basis, zone, cond_table, chips)
    others = [swap(other, CORES * (k + 1)) for k, other in enumerate(others)]
    one, two = exchange(sent, 0), exchange(sent, 1)
    theirs = [swap(center, 1)]
    far = []
    for other in others:
        far.append([
            exchange(lax.optimization_barrier((other, near))[0], offset) for offset, near in enumerate((one, two))
        ])
    theirs += [swap(other, 1) for other in others]

    image = jax.ShapeDtypeStruct((half, columns, nz), BF16)
    left = jax.ShapeDtypeStruct((total, rows * nz), BF16)
    flat = pltpu.VMEM((columns, rows * nz), BF16)
    params = pltpu.CompilerParams(vmem_limit_bytes=32 << 20)
    near_mine, near_theirs, coef, left, near_gram = pl.pallas_call(
        functools.partial(near_kernel, chips, weight),
        out_shape=(
            image, image, jax.ShapeDtypeStruct((7, rows, nz), F32), left, jax.ShapeDtypeStruct((total, columns), F32),
        ),
        in_specs=[VMEM, SMEM, SMEM] + [VMEM] * (2 * chips + 2),
        out_specs=[VMEM] * 5,
        scratch_shapes=[pltpu.VMEM((ny + 16, nz), F32), flat],
        compiler_params=params,
    )(zone, cond_table, heat_table, center, one, two, *others, *theirs)

    count = chips - 1
    *images, gram = pl.pallas_call(
        functools.partial(far_kernel, chips, weight),
        out_shape=[image] * (2 * count) + [jax.ShapeDtypeStruct((total, chips * columns), F32)],
        in_specs=[VMEM] * (3 + 3 * count),
        out_specs=[VMEM] * (2 * count + 1),
        scratch_shapes=[flat],
        compiler_params=params,
    )(coef, left, near_gram, *others, *(one for one, _ in far), *(two for _, two in far))

    near_theirs = swap(near_theirs, 1)
    far_theirs = [swap(array, 1) for array in images[count:]]
    pieces = [near_mine, near_theirs]
    for k in range(count):
        pieces += [images[k], far_theirs[k]]
    applied = pl.pallas_call(
        functools.partial(finish_kernel, blocks),
        out_shape=jax.ShapeDtypeStruct((total, 1, half, nz), BF16),
        in_specs=[VMEM] * blocks,
        out_specs=VMEM,
        scratch_shapes=[pltpu.VMEM((columns * half, nz), F32)],
        compiler_params=params,
    )(*pieces)

    parts = slabs * blocks
    shares = gram.reshape(parts, total // parts, chips * columns)
    shares = lax.all_to_all(shares, ("dom", "blk"), split_axis=0, concat_axis=0, tiled=True)
    reduced = pl.pallas_call(
        functools.partial(sum_kernel, slabs, blocks),
        out_shape=jax.ShapeDtypeStruct((total // parts, total), F32),
        in_specs=[VMEM],
        out_specs=VMEM,
    )(shares)
    return applied, reduced


def solution(mesh):
    placed = (P("blk", "dom", "roll", None), P("dom", "roll", None), P(), P())
    return jax.shard_map(
        per_device,
        mesh=mesh,
        in_specs=placed,
        out_specs=(P("roll", "dom", "blk", None), P(("dom", "blk"), "roll")),
        check_vma=False,
    )
```

```python
import functools

import jax
import jax.numpy as jnp
from jax import lax
from jax.experimental import pallas as pl
from jax.experimental.pallas import tpu as pltpu
from jax.sharding import PartitionSpec as P

ZONES = 16
CORES = 2
COST = 1 << 30
F32 = jnp.float32
BF16 = jnp.bfloat16
VMEM = pl.BlockSpec(memory_space=pltpu.VMEM)
SMEM = pl.BlockSpec(memory_space=pltpu.SMEM)
HBM = pl.BlockSpec(memory_space=pltpu.HBM)


def lookup(zone, table_ref):
    result = jnp.zeros(zone.shape, F32)
    for which in range(ZONES):
        result = jnp.where(zone == which, table_ref[which], result)
    return result


def cond_of(zone, table_ref):
    return lookup(zone, table_ref).astype(BF16).astype(F32)


def prepare_kernel(chips, basis_hbm, zone_hbm, cond_hbm, *refs):
    outs, (basis, zone, table, wide, turned, cond_pad, in_sems, out_sems) = refs[:chips + 1], refs[chips + 1:]
    columns, _, ny, nz = basis.shape
    rows = ny // chips
    chip = lax.axis_index("blk") // CORES
    step = 16
    chunks = columns // step
    loads = [
        pltpu.make_async_copy(basis_hbm.at[pl.ds(i * step, step)], basis.at[pl.ds(i * step, step)], in_sems.at[i])
        for i in range(chunks)
    ]
    loads.append(pltpu.make_async_copy(zone_hbm, zone, in_sems.at[chunks]))
    loads.append(pltpu.make_async_copy(cond_hbm, table, in_sems.at[chunks + 1]))
    for load in loads:
        load.start()
    turned[0] = jnp.zeros((columns, nz), BF16)
    turned[ny + 1] = jnp.zeros((columns, nz), BF16)
    stores = []

    def store(source, target):
        copy = pltpu.make_async_copy(source, target, out_sems.at[len(stores)])
        copy.start()
        stores.append(copy)

    loads[chunks].wait()
    loads[chunks + 1].wait()
    mine = zone[0, pl.ds(pl.multiple_of(chip * rows, rows), rows), :]
    own = cond_of(mine, table)
    cond_pad[...] = jnp.concatenate([own, jnp.zeros((columns - rows, nz), F32)], 0).astype(BF16)
    store(cond_pad, outs[0].at[rows])
    for i in range(chunks):
        loads[i].wait()
        some = pl.ds(i * step, step)
        for c in range(i * step, (i + 1) * step):
            wide[c * ny:(c + 1) * ny, :] = basis[c, 0].astype(F32)
        for y in range(ny):
            turned[y + 1, some, :] = wide[pl.ds(i * step * ny + y, step, stride=ny), :].astype(BF16)
        for k in reversed(range(chips)):
            store(turned.at[pl.ds((chip ^ k) * rows, rows + 2), some], outs[1 + k].at[:, some])
        store(turned.at[pl.ds(chip * rows + 1, rows), some], outs[0].at[pl.ds(0, rows), some])
    for copy in stores:
        copy.wait()


def prepare(basis, zone, cond_table, chips):
    columns, _, ny, nz = basis.shape
    rows = ny // chips
    shapes = [jax.ShapeDtypeStruct((rows + 1, columns, nz), BF16)]
    shapes += [jax.ShapeDtypeStruct((rows + 2, columns, nz), BF16)] * chips
    results = pl.pallas_call(
        functools.partial(prepare_kernel, chips),
        out_shape=shapes,
        in_specs=[HBM, HBM, HBM],
        out_specs=[pl.BlockSpec(memory_space=pl.ANY)] * len(shapes),
        scratch_shapes=[
            pltpu.VMEM(basis.shape, BF16),
            pltpu.VMEM(zone.shape, jnp.int32),
            pltpu.SMEM((ZONES,), F32),
            pltpu.VMEM((columns * ny, nz), F32),
            pltpu.VMEM((ny + 2, columns, nz), BF16),
            pltpu.VMEM((columns, nz), BF16),
            pltpu.SemaphoreType.DMA((columns // 16 + 2,)),
            pltpu.SemaphoreType.DMA((1 + (chips + 1) * (columns // 16),)),
        ],
        compiler_params=pltpu.CompilerParams(vmem_limit_bytes=16 << 20),
    )(*[pltpu.with_memory_space_constraint(x, pltpu.HBM) for x in (basis, zone, cond_table)])
    return results[0], results[1], results[2:]


def plane_kernel(chips, zone_ref, cond_ref, heat_ref, center, coef, partial, cond_pad):
    rows = partial.shape[0]
    nz = center.shape[2]
    ny = zone_ref.shape[1]
    chip = lax.axis_index("blk") // CORES
    cond_pad[0:8, :] = jnp.zeros((8, nz), F32)
    cond_pad[8:8 + ny, :] = cond_of(zone_ref[0], cond_ref)
    cond_pad[8 + ny:16 + ny, :] = jnp.zeros((8, nz), F32)
    base = pl.multiple_of(chip * rows, 8)
    near = cond_pad[pl.ds(base, rows + 16), :]
    own = near[8:8 + rows]
    lane = lax.broadcasted_iota(jnp.int32, (rows, nz), 1)
    coef[0] = lookup(zone_ref[0, pl.ds(base, rows), :], heat_ref)
    beside = (
        near[7:7 + rows],
        near[9:9 + rows],
        jnp.where(lane == 0, 0.0, pltpu.roll(own, 1, 1)),
        jnp.where(lane == nz - 1, 0.0, pltpu.roll(own, nz - 1, 1)),
    )
    for which, other in enumerate(beside):
        coef[1 + which] = 0.5 * (own + other)
    coef[5] = own
    plane_rows(coef, center, partial)


def plane_rows(coef, center, partial):
    columns, nz = center.shape[1:]
    lane = lax.broadcasted_iota(jnp.int32, (columns, nz), 1)
    first, last = lane == 0, lane == nz - 1
    for y in range(partial.shape[0]):
        face = [jnp.broadcast_to(coef[k, y:y + 1, :], (columns, nz)) for k in range(5)]
        v = center[y + 1].astype(F32)
        total = face[0] * v
        total += face[1] * (v - center[y].astype(F32))
        total += face[2] * (v - center[y + 2].astype(F32))
        total += face[3] * (v - jnp.where(first, 0.0, pltpu.roll(v, 1, 1)))
        total += face[4] * (v - jnp.where(last, 0.0, pltpu.roll(v, nz - 1, 1)))
        partial[y] = total


def image_rows(coef, partial, center, one, two, skip, mine, theirs, flat):
    rows, columns, nz = partial.shape
    half = rows // CORES
    core = lax.axis_index("blk") % CORES
    for y in range(rows):
        face = [jnp.broadcast_to(coef[k, y:y + 1, :], (columns, nz)) for k in range(2)]
        v = center[y + 1].astype(F32)
        total = partial[y]
        total += face[0] * (v - one[y + skip].astype(F32))
        total += face[1] * (v - two[y + skip].astype(F32))
        image = total.astype(BF16)
        flat[:, y * nz:(y + 1) * nz] = image

        @pl.when(core == y // half)
        def _():
            mine[y % half] = image

        @pl.when(core != y // half)
        def _():
            theirs[y % half] = image


def gram_of(left, flat):
    return lax.dot_general(left[...], flat[...], (((1,), (1,)), ((), ())), preferred_element_type=F32)


def near_kernel(coef, partial, center, one, two, mine, theirs, faces, flat):
    rows = partial.shape[0]
    for which, ref in enumerate((one, two)):
        faces[which] = 0.5 * (coef[5] + ref[rows].astype(F32)[:rows])
    image_rows(faces, partial, center, one, two, 0, mine, theirs, flat)


def left_kernel(chips, weight, coef, flat, center, *refs):
    others, theirs, partials = refs[:chips - 1], refs[chips - 1:2 * chips - 1], refs[2 * chips - 1:3 * chips - 2]
    left, gram = refs[3 * chips - 2:]
    rows, columns, nz = partials[0].shape
    me = lax.axis_index("blk")
    for k, ref in enumerate((center, *others)):
        for core in range(CORES):
            where = pl.ds(pl.multiple_of((me ^ (CORES * k + core)) * columns, columns), columns)
            for y in range(rows):
                left[where, y * nz:(y + 1) * nz] = theirs[k][y] if core else ref[y + 1]
    gram[...] = weight * gram_of(left, flat)
    for k in range(chips - 1):
        plane_rows(coef, others[k], partials[k])


def far_kernel(chips, weight, faces, left, near_gram, *refs):
    count = chips - 1
    partials, centers, twos, ones, mine, theirs = (refs[i * count:(i + 1) * count] for i in range(6))
    gram, flat = refs[6 * count:]
    columns = centers[0].shape[1]
    gram[:, 0:columns] = near_gram[...]
    for k in range(count):
        image_rows(faces, partials[k], centers[k], ones[k], twos[k], 1, mine[k], theirs[k], flat)
        gram[:, (k + 1) * columns:(k + 2) * columns] = weight * gram_of(left, flat)


def finish_kernel(blocks, *refs):
    images, (applied, wide) = refs[:blocks], refs[blocks:]
    rows, columns, nz = images[0].shape
    me = lax.axis_index("blk")
    for s, image in enumerate(images):
        for y in range(rows):
            wide[pl.ds(y, columns, stride=rows), :] = image[y].astype(F32)
        start = (me ^ s) * columns
        for c in range(columns):
            applied[start + c, 0] = wide[c * rows:(c + 1) * rows, :].astype(BF16)


def sum_kernel(slabs, blocks, shares, out):
    chips = blocks // CORES
    columns = shares.shape[2] // chips
    for core in range(CORES):
        sums = []
        for chip in range(chips):
            total = shares[CORES * chip + core]
            for slab in range(1, slabs):
                total += shares[slab * blocks + CORES * chip + core]
            sums.append(total)
        for target in range(chips):
            parts = [sums[chip][:, (chip ^ target) * columns:((chip ^ target) + 1) * columns] for chip in range(chips)]
            start = (CORES * target + core) * columns
            out[:, start:start + columns] = functools.reduce(jnp.add, parts)


def per_device(basis, zone, cond_table, heat_table):
    blocks = lax.axis_size("blk")
    slabs = lax.axis_size("dom")
    chips = blocks // CORES
    columns, planes, ny, nz = basis.shape
    rows = ny // chips
    half = ny // blocks
    total = columns * blocks
    weight = 1.0 / (slabs * planes * ny * nz)

    def swap(array, s):
        return lax.ppermute(array, "blk", [(i, i ^ s) for i in range(blocks)])

    def exchange(array, offset):
        partner = [((d + offset) ^ 1) - offset for d in range(slabs)]
        return lax.ppermute(array, "dom", [(d, to) for d, to in enumerate(partner) if 0 <= to < slabs])

    sent, center, others = prepare(basis, zone, cond_table, chips)
    others = [swap(other, CORES * (k + 1)) for k, other in enumerate(others)]
    count = chips - 1
    image = jax.ShapeDtypeStruct((half, columns, nz), BF16)
    partial = jax.ShapeDtypeStruct((rows, columns, nz), F32)
    flat = pltpu.VMEM((columns, rows * nz), BF16)
    params = pltpu.CompilerParams(vmem_limit_bytes=32 << 20)
    two = exchange(sent, 1)
    one = exchange(sent, 0)
    coef, near_partial = pl.pallas_call(
        functools.partial(plane_kernel, chips),
        out_shape=(jax.ShapeDtypeStruct((6, rows, nz), F32), partial),
        in_specs=[VMEM, SMEM, SMEM, VMEM],
        out_specs=[VMEM] * 2,
        scratch_shapes=[pltpu.VMEM((ny + 16, nz), F32)],
        compiler_params=params,
        cost_estimate=pl.CostEstimate(flops=COST, bytes_accessed=COST // 8, transcendentals=0),
    )(zone, cond_table, heat_table, center)
    far = []
    for other in others:
        far_two = exchange(lax.optimization_barrier((other, one))[0], 1)
        far.append((exchange(lax.optimization_barrier((other, two))[0], 0), far_two))
    near_mine, near_theirs, faces, near_flat = pl.pallas_call(
        near_kernel,
        out_shape=(
            image,
            image,
            jax.ShapeDtypeStruct((2, rows, nz), F32),
            jax.ShapeDtypeStruct((columns, rows * nz), BF16),
        ),
        in_specs=[VMEM] * 5,
        out_specs=[VMEM] * 4,
        compiler_params=params,
        cost_estimate=pl.CostEstimate(flops=1, bytes_accessed=1, transcendentals=0),
    )(coef, near_partial, center, one, two)
    late = lax.optimization_barrier((center, others, faces))
    theirs = [swap(array[1:-1], 1) for array in (late[0], *late[1])]
    *far_partials, left, near_gram = pl.pallas_call(
        functools.partial(left_kernel, chips, weight),
        out_shape=[partial] * count + [
            jax.ShapeDtypeStruct((total, rows * nz), BF16),
            jax.ShapeDtypeStruct((total, columns), F32),
        ],
        in_specs=[VMEM] * (2 * chips + 2),
        out_specs=[VMEM] * (count + 2),
        compiler_params=params,
        cost_estimate=pl.CostEstimate(flops=1, bytes_accessed=1, transcendentals=0),
    )(coef, near_flat, center, *others, *theirs)

    *images, gram = pl.pallas_call(
        functools.partial(far_kernel, chips, weight),
        out_shape=[image] * (2 * count) + [jax.ShapeDtypeStruct((total, chips * columns), F32)],
        in_specs=[VMEM] * (3 + 4 * count),
        out_specs=[VMEM] * (2 * count + 1),
        scratch_shapes=[flat],
        compiler_params=params,
    )(faces, left, near_gram, *far_partials, *others, *(two for _, two in far), *(one for one, _ in far))

    near_theirs = swap(near_theirs, 1)
    far_theirs = [swap(array, 1) for array in images[count:]]
    pieces = [near_mine, near_theirs]
    for k in range(count):
        pieces += [images[k], far_theirs[k]]
    applied = pl.pallas_call(
        functools.partial(finish_kernel, blocks),
        out_shape=jax.ShapeDtypeStruct((total, 1, half, nz), BF16),
        in_specs=[VMEM] * blocks,
        out_specs=VMEM,
        scratch_shapes=[pltpu.VMEM((columns * half, nz), F32)],
        compiler_params=params,
    )(*pieces)

    parts = slabs * blocks
    shares = gram.reshape(parts, total // parts, chips * columns)
    shares = lax.all_to_all(shares, ("dom", "blk"), split_axis=0, concat_axis=0, tiled=True)
    reduced = pl.pallas_call(
        functools.partial(sum_kernel, slabs, blocks),
        out_shape=jax.ShapeDtypeStruct((total // parts, total), F32),
        in_specs=[VMEM],
        out_specs=VMEM,
    )(shares)
    return applied, reduced


def solution(mesh):
    placed = (P("blk", "dom", "roll", None), P("dom", "roll", None), P(), P())
    return jax.shard_map(
        per_device,
        mesh=mesh,
        in_specs=placed,
        out_specs=(P("roll", "dom", "blk", None), P(("dom", "blk"), "roll")),
        check_vma=False,
    )
```

```python
import functools

import jax
import jax.numpy as jnp
from jax import lax
from jax.experimental import pallas as pl
from jax.experimental.pallas import tpu as pltpu
from jax.sharding import PartitionSpec as P

ZONES = 16
CORES = 2
COST = 1 << 30
F32 = jnp.float32
BF16 = jnp.bfloat16
VMEM = pl.BlockSpec(memory_space=pltpu.VMEM)
SMEM = pl.BlockSpec(memory_space=pltpu.SMEM)
HBM = pl.BlockSpec(memory_space=pltpu.HBM)


def lookup(zone, table_ref):
    result = jnp.zeros(zone.shape, F32)
    for which in range(ZONES):
        result = jnp.where(zone == which, table_ref[which], result)
    return result


def cond_of(zone, table_ref):
    return lookup(zone, table_ref).astype(BF16).astype(F32)


def prepare_kernel(chips, basis_hbm, zone_hbm, cond_hbm, *refs):
    outs, (basis, zone, table, wide, turned, cond_pad, in_sems, out_sems) = refs[:chips + 1], refs[chips + 1:]
    columns, _, ny, nz = basis.shape
    rows = ny // chips
    chip = lax.axis_index("blk") // CORES
    step = 16
    chunks = columns // step
    loads = [
        pltpu.make_async_copy(basis_hbm.at[pl.ds(i * step, step)], basis.at[pl.ds(i * step, step)], in_sems.at[i])
        for i in range(chunks)
    ]
    loads.append(pltpu.make_async_copy(zone_hbm, zone, in_sems.at[chunks]))
    loads.append(pltpu.make_async_copy(cond_hbm, table, in_sems.at[chunks + 1]))
    for load in loads:
        load.start()
    turned[0] = jnp.zeros((columns, nz), BF16)
    turned[ny + 1] = jnp.zeros((columns, nz), BF16)
    stores = []

    def store(source, target):
        copy = pltpu.make_async_copy(source, target, out_sems.at[len(stores)])
        copy.start()
        stores.append(copy)

    loads[chunks].wait()
    loads[chunks + 1].wait()
    mine = zone[0, pl.ds(pl.multiple_of(chip * rows, rows), rows), :]
    own = cond_of(mine, table)
    cond_pad[...] = jnp.concatenate([own, jnp.zeros((columns - rows, nz), F32)], 0).astype(BF16)
    store(cond_pad, outs[0].at[rows])
    for i in range(chunks):
        loads[i].wait()
        some = pl.ds(i * step, step)
        for c in range(i * step, (i + 1) * step):
            wide[c * ny:(c + 1) * ny, :] = basis[c, 0].astype(F32)
        for y in range(ny):
            turned[y + 1, some, :] = wide[pl.ds(i * step * ny + y, step, stride=ny), :].astype(BF16)
        for k in reversed(range(chips)):
            store(turned.at[pl.ds((chip ^ k) * rows, rows + 2), some], outs[1 + k].at[:, some])
        store(turned.at[pl.ds(chip * rows + 1, rows), some], outs[0].at[pl.ds(0, rows), some])
    for copy in stores:
        copy.wait()


def prepare(basis, zone, cond_table, chips):
    columns, _, ny, nz = basis.shape
    rows = ny // chips
    shapes = [jax.ShapeDtypeStruct((rows + 1, columns, nz), BF16)]
    shapes += [jax.ShapeDtypeStruct((rows + 2, columns, nz), BF16)] * chips
    results = pl.pallas_call(
        functools.partial(prepare_kernel, chips),
        out_shape=shapes,
        in_specs=[HBM, HBM, HBM],
        out_specs=[pl.BlockSpec(memory_space=pl.ANY)] * len(shapes),
        scratch_shapes=[
            pltpu.VMEM(basis.shape, BF16),
            pltpu.VMEM(zone.shape, jnp.int32),
            pltpu.SMEM((ZONES,), F32),
            pltpu.VMEM((columns * ny, nz), F32),
            pltpu.VMEM((ny + 2, columns, nz), BF16),
            pltpu.VMEM((columns, nz), BF16),
            pltpu.SemaphoreType.DMA((columns // 16 + 2,)),
            pltpu.SemaphoreType.DMA((1 + (chips + 1) * (columns // 16),)),
        ],
        compiler_params=pltpu.CompilerParams(vmem_limit_bytes=16 << 20),
    )(*[pltpu.with_memory_space_constraint(x, pltpu.HBM) for x in (basis, zone, cond_table)])
    return results[0], results[1], results[2:]


def plane_kernel(chips, zone_ref, cond_ref, heat_ref, center, coef, partial, cond_pad):
    rows = partial.shape[0]
    nz = center.shape[2]
    ny = zone_ref.shape[1]
    chip = lax.axis_index("blk") // CORES
    cond_pad[0:8, :] = jnp.zeros((8, nz), F32)
    cond_pad[8:8 + ny, :] = cond_of(zone_ref[0], cond_ref)
    cond_pad[8 + ny:16 + ny, :] = jnp.zeros((8, nz), F32)
    base = pl.multiple_of(chip * rows, 8)
    near = cond_pad[pl.ds(base, rows + 16), :]
    own = near[8:8 + rows]
    lane = lax.broadcasted_iota(jnp.int32, (rows, nz), 1)
    coef[0] = lookup(zone_ref[0, pl.ds(base, rows), :], heat_ref)
    beside = (
        near[7:7 + rows],
        near[9:9 + rows],
        jnp.where(lane == 0, 0.0, pltpu.roll(own, 1, 1)),
        jnp.where(lane == nz - 1, 0.0, pltpu.roll(own, nz - 1, 1)),
    )
    for which, other in enumerate(beside):
        coef[1 + which] = 0.5 * (own + other)
    coef[5] = own
    plane_rows(coef, center, partial)


def plane_rows(coef, center, partial):
    columns, nz = center.shape[1:]
    lane = lax.broadcasted_iota(jnp.int32, (columns, nz), 1)
    first, last = lane == 0, lane == nz - 1
    for y in range(partial.shape[0]):
        face = [jnp.broadcast_to(coef[k, y:y + 1, :], (columns, nz)) for k in range(5)]
        v = center[y + 1].astype(F32)
        total = face[0] * v
        total += face[1] * (v - center[y].astype(F32))
        total += face[2] * (v - center[y + 2].astype(F32))
        total += face[3] * (v - jnp.where(first, 0.0, pltpu.roll(v, 1, 1)))
        total += face[4] * (v - jnp.where(last, 0.0, pltpu.roll(v, nz - 1, 1)))
        partial[y] = total


def image_rows(coef, partial, center, one, two, skip, mine, theirs, flat):
    rows, columns, nz = partial.shape
    half = rows // CORES
    core = lax.axis_index("blk") % CORES
    for y in range(rows):
        face = [jnp.broadcast_to(coef[k, y:y + 1, :], (columns, nz)) for k in range(2)]
        v = center[y + 1].astype(F32)
        total = partial[y]
        total += face[0] * (v - one[y + skip].astype(F32))
        total += face[1] * (v - two[y + skip].astype(F32))
        image = total.astype(BF16)
        flat[:, y * nz:(y + 1) * nz] = image

        @pl.when(core == y // half)
        def _():
            mine[y % half] = image

        @pl.when(core != y // half)
        def _():
            theirs[y % half] = image


def gram_of(left, flat):
    return lax.dot_general(left[...], flat[...], (((1,), (1,)), ((), ())), preferred_element_type=F32)


def near_kernel(coef, partial, center, one, two, mine, theirs, faces, flat):
    rows = partial.shape[0]
    for which, ref in enumerate((one, two)):
        faces[which] = 0.5 * (coef[5] + ref[rows].astype(F32)[:rows])
    image_rows(faces, partial, center, one, two, 0, mine, theirs, flat)


def left_kernel(chips, weight, coef, flat, center, *refs):
    others, theirs, partials = refs[:chips - 1], refs[chips - 1:2 * chips - 1], refs[2 * chips - 1:3 * chips - 2]
    left, gram = refs[3 * chips - 2:]
    rows, columns, nz = partials[0].shape
    me = lax.axis_index("blk")
    for k, ref in enumerate((center, *others)):
        for core in range(CORES):
            where = pl.ds(pl.multiple_of((me ^ (CORES * k + core)) * columns, columns), columns)
            for y in range(rows):
                left[where, y * nz:(y + 1) * nz] = theirs[k][y] if core else ref[y + 1]
    gram[...] = weight * gram_of(left, flat)
    for k in range(chips - 1):
        plane_rows(coef, others[k], partials[k])


def far_kernel(chips, weight, faces, left, near_gram, *refs):
    count = chips - 1
    partials, centers, twos, ones, mine, theirs = (refs[i * count:(i + 1) * count] for i in range(6))
    gram, flat = refs[6 * count:]
    columns = centers[0].shape[1]
    gram[:, 0:columns] = near_gram[...]
    for k in range(count):
        image_rows(faces, partials[k], centers[k], ones[k], twos[k], 1, mine[k], theirs[k], flat)
        gram[:, (k + 1) * columns:(k + 2) * columns] = weight * gram_of(left, flat)


def turn_out(image, start, applied, wide, turned, sem):
    rows, columns, _ = image.shape
    for y in range(rows):
        wide[pl.ds(y, columns, stride=rows), :] = image[y].astype(F32)
    for c in range(columns):
        turned[c, 0] = wide[c * rows:(c + 1) * rows, :].astype(BF16)
    copy = pltpu.make_async_copy(turned, applied.at[pl.ds(start, columns)], sem)
    copy.start()
    return copy


def first_kernel(mine, theirs, applied, wide, turned, sems):
    me = lax.axis_index("blk")
    columns = mine.shape[1]
    copies = [
        turn_out(image, (me ^ s) * columns, applied, wide.at[s], turned.at[s], sems.at[s])
        for s, image in enumerate((mine, theirs))
    ]
    for copy in copies:
        copy.wait()


def last_kernel(slabs, blocks, shares, _, *refs):
    images, (applied, reduced, wide, turned, sems) = refs[:blocks - CORES], refs[blocks - CORES:]
    me = lax.axis_index("blk")
    columns = images[0].shape[1]
    copies = [
        turn_out(image, (me ^ (s + CORES)) * columns, applied, wide.at[s], turned.at[s], sems.at[s])
        for s, image in enumerate(images)
    ]
    chips = blocks // CORES
    for core in range(CORES):
        sums = []
        for chip in range(chips):
            total = shares[CORES * chip + core]
            for slab in range(1, slabs):
                total += shares[slab * blocks + CORES * chip + core]
            sums.append(total)
        for target in range(chips):
            parts = [sums[chip][:, (chip ^ target) * columns:((chip ^ target) + 1) * columns] for chip in range(chips)]
            start = (CORES * target + core) * columns
            reduced[:, start:start + columns] = functools.reduce(jnp.add, parts)
    for copy in copies:
        copy.wait()


def per_device(basis, zone, cond_table, heat_table):
    blocks = lax.axis_size("blk")
    slabs = lax.axis_size("dom")
    chips = blocks // CORES
    columns, planes, ny, nz = basis.shape
    rows = ny // chips
    half = ny // blocks
    total = columns * blocks
    weight = 1.0 / (slabs * planes * ny * nz)

    def swap(array, s):
        return lax.ppermute(array, "blk", [(i, i ^ s) for i in range(blocks)])

    def exchange(array, offset):
        partner = [((d + offset) ^ 1) - offset for d in range(slabs)]
        return lax.ppermute(array, "dom", [(d, to) for d, to in enumerate(partner) if 0 <= to < slabs])

    sent, center, others = prepare(basis, zone, cond_table, chips)
    others = [swap(other, CORES * (k + 1)) for k, other in enumerate(others)]
    count = chips - 1
    image = jax.ShapeDtypeStruct((half, columns, nz), BF16)
    partial = jax.ShapeDtypeStruct((rows, columns, nz), F32)
    flat = pltpu.VMEM((columns, rows * nz), BF16)
    params = pltpu.CompilerParams(vmem_limit_bytes=32 << 20)
    two = exchange(sent, 1)
    one = exchange(sent, 0)
    coef, near_partial = pl.pallas_call(
        functools.partial(plane_kernel, chips),
        out_shape=(jax.ShapeDtypeStruct((6, rows, nz), F32), partial),
        in_specs=[VMEM, SMEM, SMEM, VMEM],
        out_specs=[VMEM] * 2,
        scratch_shapes=[pltpu.VMEM((ny + 16, nz), F32)],
        compiler_params=params,
        cost_estimate=pl.CostEstimate(flops=COST, bytes_accessed=COST // 8, transcendentals=0),
    )(zone, cond_table, heat_table, center)
    far = []
    for other in others:
        far_two = exchange(lax.optimization_barrier((other, one))[0], 1)
        far.append((exchange(lax.optimization_barrier((other, two))[0], 0), far_two))
    near_mine, near_theirs, faces, near_flat = pl.pallas_call(
        near_kernel,
        out_shape=(
            image,
            image,
            jax.ShapeDtypeStruct((2, rows, nz), F32),
            jax.ShapeDtypeStruct((columns, rows * nz), BF16),
        ),
        in_specs=[VMEM] * 5,
        out_specs=[VMEM] * 4,
        compiler_params=params,
        cost_estimate=pl.CostEstimate(flops=1, bytes_accessed=1, transcendentals=0),
    )(coef, near_partial, center, one, two)
    whole = jax.ShapeDtypeStruct((total, 1, half, nz), BF16)

    def turning(n):
        return [
            pltpu.VMEM((n, columns * half, nz), F32),
            pltpu.VMEM((n, columns, 1, half, nz), BF16),
            pltpu.SemaphoreType.DMA((n,)),
        ]

    late = lax.optimization_barrier((center, others, faces))
    theirs = [swap(array[1:-1], 1) for array in (late[0], *late[1])]
    *far_partials, left, near_gram = pl.pallas_call(
        functools.partial(left_kernel, chips, weight),
        out_shape=[partial] * count + [
            jax.ShapeDtypeStruct((total, rows * nz), BF16),
            jax.ShapeDtypeStruct((total, columns), F32),
        ],
        in_specs=[VMEM] * (2 * chips + 2),
        out_specs=[VMEM] * (count + 2),
        compiler_params=params,
        cost_estimate=pl.CostEstimate(flops=1, bytes_accessed=1, transcendentals=0),
    )(coef, near_flat, center, *others, *theirs)

    applied = pl.pallas_call(
        first_kernel,
        out_shape=whole,
        in_specs=[VMEM] * 2,
        out_specs=pl.BlockSpec(memory_space=pl.ANY),
        scratch_shapes=turning(CORES),
        compiler_params=params,
        cost_estimate=pl.CostEstimate(flops=1, bytes_accessed=1, transcendentals=0),
    )(near_mine, swap(near_theirs, 1))
    faces, applied = lax.optimization_barrier((faces, applied))

    *images, gram = pl.pallas_call(
        functools.partial(far_kernel, chips, weight),
        out_shape=[image] * (2 * count) + [jax.ShapeDtypeStruct((total, chips * columns), F32)],
        in_specs=[VMEM] * (3 + 4 * count),
        out_specs=[VMEM] * (2 * count + 1),
        scratch_shapes=[flat],
        compiler_params=params,
    )(faces, left, near_gram, *far_partials, *others, *(two for _, two in far), *(one for one, _ in far))

    pieces = []
    for k in range(count):
        pieces += [images[k], swap(images[count + k], 1)]
    parts = slabs * blocks
    shares = gram.reshape(parts, total // parts, chips * columns)
    shares = lax.all_to_all(shares, ("dom", "blk"), split_axis=0, concat_axis=0, tiled=True)
    return tuple(pl.pallas_call(
        functools.partial(last_kernel, slabs, blocks),
        out_shape=(whole, jax.ShapeDtypeStruct((total // parts, total), F32)),
        in_specs=[VMEM, pl.BlockSpec(memory_space=pl.ANY)] + [VMEM] * len(pieces),
        out_specs=(pl.BlockSpec(memory_space=pl.ANY), VMEM),
        scratch_shapes=turning(len(pieces)),
        input_output_aliases={1: 0},
        compiler_params=params,
    )(shares, applied, *pieces))


def solution(mesh):
    placed = (P("blk", "dom", "roll", None), P("dom", "roll", None), P(), P())
    return jax.shard_map(
        per_device,
        mesh=mesh,
        in_specs=placed,
        out_specs=(P("roll", "dom", "blk", None), P(("dom", "blk"), "roll")),
        check_vma=False,
    )
```

```python
import functools

import jax
import jax.numpy as jnp
from jax import lax
from jax.experimental import pallas as pl
from jax.experimental.pallas import tpu as pltpu
from jax.sharding import PartitionSpec as P

ZONES = 16
CORES = 2
COST = 1 << 30
F32 = jnp.float32
BF16 = jnp.bfloat16
VMEM = pl.BlockSpec(memory_space=pltpu.VMEM)
SMEM = pl.BlockSpec(memory_space=pltpu.SMEM)
HBM = pl.BlockSpec(memory_space=pltpu.HBM)
ANY = pl.BlockSpec(memory_space=pl.ANY)


def lookup(zone, table_ref):
    result = jnp.zeros(zone.shape, F32)
    for which in range(ZONES):
        result = jnp.where(zone == which, table_ref[which], result)
    return result


def cond_of(zone, table_ref):
    return lookup(zone, table_ref).astype(BF16).astype(F32)


def halves():
    return lax.axis_index("dom") % 2


def prepare_kernel(chips, basis_hbm, zone_hbm, cond_hbm, *refs):
    near, center, plain, firsts, seconds = *refs[:3], refs[3:2 + chips], refs[2 + chips:2 * chips + 1]
    basis, zone, table, wide, turned, cond_pad, in_sems, out_sems = refs[2 * chips + 1:]
    columns, _, ny, nz = basis.shape
    rows = ny // chips
    part = rows // CORES // 2
    me = lax.axis_index("blk")
    chip, core, late = me // CORES, me % CORES, halves()
    step = 16
    chunks = columns // step
    loads = [
        pltpu.make_async_copy(basis_hbm.at[pl.ds(i * step, step)], basis.at[pl.ds(i * step, step)], in_sems.at[i])
        for i in range(chunks)
    ]
    loads.append(pltpu.make_async_copy(zone_hbm, zone, in_sems.at[chunks]))
    loads.append(pltpu.make_async_copy(cond_hbm, table, in_sems.at[chunks + 1]))
    for load in loads:
        load.start()
    turned[0] = jnp.zeros((columns, nz), BF16)
    turned[ny + 1] = jnp.zeros((columns, nz), BF16)
    stores = []

    def store(source, target):
        copy = pltpu.make_async_copy(source, target, out_sems.at[len(stores)])
        copy.start()
        stores.append(copy)

    loads[chunks].wait()
    loads[chunks + 1].wait()
    mine = zone[0, pl.ds(pl.multiple_of(chip * rows, rows), rows), :]
    own = cond_of(mine, table)
    cond_pad[...] = jnp.concatenate([own, jnp.zeros((columns - rows, nz), F32)], 0).astype(BF16)
    store(cond_pad, near.at[rows])
    for i in range(chunks):
        loads[i].wait()
        some = pl.ds(i * step, step)
        for c in range(i * step, (i + 1) * step):
            wide[c * ny:(c + 1) * ny, :] = basis[c, 0].astype(F32)
        for y in range(ny):
            turned[y + 1, some, :] = wide[pl.ds(i * step * ny + y, step, stride=ny), :].astype(BF16)
        store(turned.at[pl.ds(chip * rows + 1, rows), some], near.at[pl.ds(0, rows), some])
        for k in range(1, chips):
            base = (chip ^ k) * rows + 1
            for owner in range(CORES):
                start = base + (2 * owner + 1 - late) * part
                store(turned.at[pl.ds(start, part), some], firsts[k - 1].at[pl.ds(owner * part, part), some])
            for other in range(CORES):
                start = base + (2 * (core ^ other) + late) * part
                store(turned.at[pl.ds(start, part), some], seconds[k - 1].at[pl.ds(other * part, part), some])
        store(turned.at[pl.ds(chip * rows, rows + 2), some], center.at[:, some])
        store(turned.at[pl.ds(chip * rows + 1, rows), some], plain.at[:, some])
    for k in range(1, chips):
        base = (chip ^ k) * rows
        store(turned.at[pl.ds(base, 1)], firsts[k - 1].at[pl.ds(CORES * part, 1)])
        store(turned.at[pl.ds(base + rows + 1, 1)], firsts[k - 1].at[pl.ds(CORES * part + 1, 1)])
    for copy in stores:
        copy.wait()


def prepare(basis, zone, cond_table, chips):
    columns, _, ny, nz = basis.shape
    rows = ny // chips
    slabs = [rows + 1, rows + 2, rows] + [rows // 2 + 2] * (chips - 1) + [rows // 2] * (chips - 1)
    stores = 1 + (3 + 2 * CORES * (chips - 1)) * (columns // 16) + 2 * (chips - 1)
    results = pl.pallas_call(
        functools.partial(prepare_kernel, chips),
        out_shape=[jax.ShapeDtypeStruct((n, columns, nz), BF16) for n in slabs],
        in_specs=[HBM, HBM, HBM],
        out_specs=[ANY] * len(slabs),
        scratch_shapes=[
            pltpu.VMEM(basis.shape, BF16),
            pltpu.VMEM(zone.shape, jnp.int32),
            pltpu.SMEM((ZONES,), F32),
            pltpu.VMEM((columns * ny, nz), F32),
            pltpu.VMEM((ny + 2, columns, nz), BF16),
            pltpu.VMEM((columns, nz), BF16),
            pltpu.SemaphoreType.DMA((columns // 16 + 2,)),
            pltpu.SemaphoreType.DMA((stores,)),
        ],
        compiler_params=pltpu.CompilerParams(vmem_limit_bytes=16 << 20),
    )(*[pltpu.with_memory_space_constraint(x, pltpu.HBM) for x in (basis, zone, cond_table)])
    return (*results[:3], results[3:2 + chips], results[2 + chips:])


def plane_kernel(chips, zone_ref, cond_ref, heat_ref, center, coef, partial, cond_pad):
    rows = partial.shape[0]
    nz = center.shape[2]
    ny = zone_ref.shape[1]
    chip = lax.axis_index("blk") // CORES
    cond_pad[0:8, :] = jnp.zeros((8, nz), F32)
    cond_pad[8:8 + ny, :] = cond_of(zone_ref[0], cond_ref)
    cond_pad[8 + ny:16 + ny, :] = jnp.zeros((8, nz), F32)
    base = pl.multiple_of(chip * rows, 8)
    near = cond_pad[pl.ds(base, rows + 16), :]
    own = near[8:8 + rows]
    lane = lax.broadcasted_iota(jnp.int32, (rows, nz), 1)
    coef[0] = lookup(zone_ref[0, pl.ds(base, rows), :], heat_ref)
    beside = (
        near[7:7 + rows],
        near[9:9 + rows],
        jnp.where(lane == 0, 0.0, pltpu.roll(own, 1, 1)),
        jnp.where(lane == nz - 1, 0.0, pltpu.roll(own, nz - 1, 1)),
    )
    for which, other in enumerate(beside):
        coef[1 + which] = 0.5 * (own + other)
    coef[5] = own
    plane_rows(coef, center, partial)


def plane_rows(coef, center, partial, first=0):
    columns, nz = center.shape[1:]
    lane = lax.broadcasted_iota(jnp.int32, (columns, nz), 1)
    left_end, right_end = lane == 0, lane == nz - 1
    for i in range(partial.shape[0]):
        y = first + i
        face = [spread(coef, k, y, columns) for k in range(5)]
        v = center[y + 1].astype(F32)
        total = face[0] * v
        total += face[1] * (v - center[y].astype(F32))
        total += face[2] * (v - center[y + 2].astype(F32))
        total += face[3] * (v - jnp.where(left_end, 0.0, pltpu.roll(v, 1, 1)))
        total += face[4] * (v - jnp.where(right_end, 0.0, pltpu.roll(v, nz - 1, 1)))
        partial[i] = total


def spread(coef, k, y, columns):
    return jnp.broadcast_to(coef[k, pl.ds(y, 1), :], (columns, coef.shape[2]))


def with_dom(faces, y, v, partial, one, two):
    total = partial + spread(faces, 0, y, v.shape[0]) * (v - one)
    return total + spread(faces, 1, y, v.shape[0]) * (v - two)


def place(y, part, late):
    core, half = y // (2 * part), y // part % 2
    return ((half ^ late) * CORES + core) * part + y % part


def gram_of(left, right):
    return lax.dot_general(left, right, (((1,), (1,)), ((), ())), preferred_element_type=F32)


def near_kernel(coef, partial, center, one, two, mine, theirs, faces, flat):
    rows, columns, nz = partial.shape
    part = rows // CORES // 2
    core, late = lax.axis_index("blk") % CORES, halves()
    face = [0.5 * (coef[5] + ref[rows].astype(F32)[:rows]) for ref in (one, two)]
    which = lax.broadcasted_iota(jnp.int32, (rows, nz), 0) // part % 2
    for k in range(2):
        faces[k] = face[k]
        faces[3 + k] = jnp.where(which == late, face[k], 0.0)
    faces[2] = 0.5 * (face[0] + face[1])
    for y in range(rows):
        v, a, b, p = center[y + 1].astype(F32), one[y].astype(F32), two[y].astype(F32), partial[y]
        image = with_dom(faces, y, v, p, a, b).astype(BF16)
        share = 0.5 * p + spread(faces, 2, y, columns) * v
        share -= spread(faces, 3, y, columns) * a
        share -= spread(faces, 4, y, columns) * b
        flat[:, pl.ds(pl.multiple_of(place(y, part, late) * nz, nz), nz)] = share.astype(BF16)

        @pl.when(core == y // (2 * part))
        def _():
            mine[y % (2 * part)] = image

        @pl.when(core != y // (2 * part))
        def _():
            theirs[y % (2 * part)] = image


def gather(first, outer, second, core, center):
    part = second.shape[0] // CORES
    late = halves()
    for i in range(part):
        for c in range(CORES):
            center[1 + (2 * c + 1 - late) * part + i] = first[c * part + i]
            center[1 + (2 * (core ^ c) + late) * part + i] = second[c * part + i]
    center[0] = outer[0]
    center[2 * CORES * part + 1] = outer[1]


def gather_kernel(chips, coef, *refs):
    count = chips - 1
    firsts, seconds, other_firsts, outers, other_seconds = (refs[i * count:(i + 1) * count] for i in range(5))
    centers, partials, other_centers, other_partials = (refs[i * count:(i + 1) * count] for i in range(5, 9))
    core, late = lax.axis_index("blk") % CORES, halves()
    for k in range(count):
        halo = seconds[k].shape[0]
        gather(firsts[k], firsts[k].at[pl.ds(halo, 2)], seconds[k], core, centers[k])
        gather(other_firsts[k], outers[k], other_seconds[k], 1 - core, other_centers[k])
        plane_rows(coef, centers[k], partials[k])
        plane_rows(coef, other_centers[k], other_partials[k], (2 * core + 1 - late) * (halo // CORES))


def left_kernel(chips, faces, flat, *refs):
    count = chips - 1
    centers, others, partials = refs[:chips], refs[chips:2 * chips], refs[2 * chips:2 * chips + count]
    left, tall, flatter, right = refs[2 * chips + count:]
    rows, columns, nz = partials[0].shape
    part = rows // CORES // 2
    late = halves()
    for y in range(rows):
        where = pl.ds(pl.multiple_of(place(y, part, late) * nz, nz), nz)
        sides = [ref[y + 1] for ref in centers] + [others[0][y]] + [ref[y + 1] for ref in others[1:]]
        for i, side in enumerate(sides):
            left[i * columns:(i + 1) * columns, where] = side
    late_half = pl.ds(rows * nz // 2, rows * nz // 2)
    tall[:, 0:columns] = gram_of(left[...], flat[...])
    flatter[0:columns, :] = gram_of(flat[...], left[...])
    for k in range(count):
        for c in range(CORES):
            for i in range(part):
                y = (2 * c + 1 - late) * part + i
                share = 0.5 * partials[k][y] + spread(faces, 2, y, columns) * centers[k + 1][y + 1].astype(F32)
                right[:, (c * part + i) * nz:(c * part + i + 1) * nz] = share.astype(BF16)
        block = slice((k + 1) * columns, (k + 2) * columns)
        tall[:, block] = gram_of(left[:, late_half], right[...])
        flatter[block, :] = gram_of(right[...], left[:, late_half])


def gram_kernel(chips, weight, faces, left, tall, flatter, *refs):
    count = chips - 1
    partials, centers, ones, twos, mine, theirs = (refs[i * count:(i + 1) * count] for i in range(6))
    gram, right, rest = refs[6 * count:]
    rows, columns, nz = partials[0].shape
    part = rows // CORES // 2
    me = lax.axis_index("blk")
    core, late = me % CORES, halves()
    early_half = pl.ds(0, rows * nz // 2)
    rest[...] = jnp.zeros_like(rest)
    for k in range(count):
        for c in range(CORES):
            for i in range(part):
                y = (2 * c + late) * part + i
                v, p = centers[k][y + 1].astype(F32), partials[k][y]
                a, b = ones[k][c * part + i].astype(F32), twos[k][c * part + i].astype(F32)
                share = 0.5 * p + spread(faces, 2, y, columns) * v
                share -= spread(faces, 0, y, columns) * a
                share -= spread(faces, 1, y, columns) * b
                right[:, (c * part + i) * nz:(c * part + i + 1) * nz] = share.astype(BF16)
                image = with_dom(faces, y, v, p, a, b).astype(BF16)

                @pl.when(core == c)
                def _():
                    mine[k][i] = image

                @pl.when(core != c)
                def _():
                    theirs[k][i] = image
        block = slice((k + 1) * columns, (k + 2) * columns)
        rest[:, block] = gram_of(left[:, early_half], right[...])
        flatter[block, :] += gram_of(right[...], left[:, early_half])
    for i in range(chips * CORES):
        partner = CORES * (i % chips) + i // chips
        where = pl.ds(pl.multiple_of((me ^ partner) * columns, columns), columns)
        block = slice(i * columns, (i + 1) * columns)
        near = weight * (tall[block, :] + rest[block, :])
        far = jnp.zeros((columns, chips * columns), F32)
        share = jnp.concatenate([near, far], 1)
        if i < chips:
            share += weight * flatter[block, :]
        gram[where, :] = share


def turn_out(image, start, applied, wide, turned, sem):
    rows, columns, _ = image.shape
    for y in range(rows):
        wide[pl.ds(y, columns, stride=rows), :] = image[y].astype(F32)
    for c in range(columns):
        turned[c, 0] = wide[c * rows:(c + 1) * rows, :].astype(BF16)
    copy = pltpu.make_async_copy(turned, applied.at[pl.ds(start, columns)], sem)
    copy.start()
    return copy


def first_kernel(mine, theirs, applied, wide, turned, sems):
    me = lax.axis_index("blk")
    columns = mine.shape[1]
    copies = [
        turn_out(image, (me ^ s) * columns, applied, wide.at[s], turned.at[s], sems.at[s])
        for s, image in enumerate((mine, theirs))
    ]
    for copy in copies:
        copy.wait()


def last_kernel(slabs, blocks, shares, _, faces, *refs):
    chips = blocks // CORES
    count = chips - 1
    done, partials, centers = (refs[i * CORES * count:(i + 1) * CORES * count] for i in range(3))
    ones, twos = (refs[i * count:(i + 1) * count] for i in range(3 * CORES, 3 * CORES + 2))
    applied, reduced, wide, turned, sems = refs[(3 * CORES + 2) * count:]
    part, columns, _ = done[0].shape
    half = CORES * part
    me = lax.axis_index("blk")
    core, late = me % CORES, halves()
    first = (2 * core + 1 - late) * part
    copies = []
    for s in range(CORES * count):
        scratch = wide.at[s]
        for i in range(part):
            y = first + i
            p = partials[s][y] if s < count else partials[s][i]
            at = s // count * part + i
            v, a, b = (x.astype(F32) for x in (centers[s][y + 1], ones[s % count][at], twos[s % count][at]))
            image = with_dom(faces, y, v, p, a, b).astype(BF16).astype(F32)
            scratch[pl.ds((1 - late) * part + i, columns, stride=half), :] = image
            scratch[pl.ds(late * part + i, columns, stride=half), :] = done[s][i].astype(F32)
        for c in range(columns):
            turned[s, c, 0] = scratch[c * half:(c + 1) * half, :].astype(BF16)
        partner = CORES * (s % count + 1) + s // count
        copy = pltpu.make_async_copy(turned.at[s], applied.at[pl.ds((me ^ partner) * columns, columns)], sems.at[s])
        copy.start()
        copies.append(copy)
    sums = []
    for sender in range(blocks):
        total = shares[sender]
        for slab in range(1, slabs):
            total += shares[slab * blocks + sender]
        sums.append(total)
    for target in range(blocks):
        parts = []
        for sender in range(blocks):
            partner = sender ^ target
            i = partner % CORES * chips + partner // CORES
            parts.append(sums[sender][:, i * columns:(i + 1) * columns])
        reduced[:, target * columns:(target + 1) * columns] = functools.reduce(jnp.add, parts)
    for copy in copies:
        copy.wait()


def per_device(basis, zone, cond_table, heat_table):
    blocks = lax.axis_size("blk")
    slabs = lax.axis_size("dom")
    chips = blocks // CORES
    count = chips - 1
    columns, planes, ny, nz = basis.shape
    rows = ny // chips
    half = ny // blocks
    part = half // 2
    total = columns * blocks
    weight = 1.0 / (slabs * planes * ny * nz)
    image = jax.ShapeDtypeStruct((half, columns, nz), BF16)
    half_image = jax.ShapeDtypeStruct((part, columns, nz), BF16)
    center_shape = jax.ShapeDtypeStruct((rows + 2, columns, nz), BF16)
    partial = jax.ShapeDtypeStruct((rows, columns, nz), F32)
    whole = jax.ShapeDtypeStruct((total, 1, half, nz), BF16)
    params = pltpu.CompilerParams(vmem_limit_bytes=32 << 20)
    costly = pl.CostEstimate(flops=COST, bytes_accessed=COST // 8, transcendentals=0)
    cheap = pl.CostEstimate(flops=1, bytes_accessed=1, transcendentals=0)

    def call(kernel, out_shape, inputs, scratch=(), specs=None, out_specs=None, cost=cheap, aliases={}):
        return pl.pallas_call(
            kernel,
            out_shape=out_shape,
            in_specs=specs or [VMEM] * len(inputs),
            out_specs=out_specs or [VMEM] * len(out_shape),
            scratch_shapes=scratch,
            input_output_aliases=aliases,
            compiler_params=params,
            cost_estimate=cost,
        )(*inputs)

    def after(value, *others):
        return lax.optimization_barrier((value, *others))[0]

    def swap(array, s):
        return lax.ppermute(array, "blk", [(i, i ^ s) for i in range(blocks)])

    def exchange(array, offset, s=0):
        partner = [((d + offset) ^ 1) - offset for d in range(slabs)]
        pairs = [
            (d * blocks + b, to * blocks + (b ^ s))
            for d, to in enumerate(partner) if 0 <= to < slabs for b in range(blocks)
        ]
        return lax.ppermute(array, ("dom", "blk"), pairs)

    def turning(n):
        return [
            pltpu.VMEM((n, columns * half, nz), F32),
            pltpu.VMEM((n, columns, 1, half, nz), BF16),
            pltpu.SemaphoreType.DMA((n,)),
        ]

    sent, center, plain, firsts, seconds = prepare(basis, zone, cond_table, chips)
    two = exchange(sent, 1)
    one = exchange(sent, 0)
    firsts = [swap(array, CORES * (k + 1)) for k, array in enumerate(firsts)]
    seconds = [swap(array, CORES * (k + 1)) for k, array in enumerate(seconds)]
    plain = swap(plain, 1)
    coef, near_partial = call(
        functools.partial(plane_kernel, chips),
        (jax.ShapeDtypeStruct((6, rows, nz), F32), partial),
        (zone, cond_table, heat_table, after(center, plain)),
        [pltpu.VMEM((ny + 16, nz), F32)],
        [VMEM, SMEM, SMEM, VMEM],
        cost=costly,
    )
    early_two = [exchange(array, 1) for array in firsts]
    early_one = [exchange(array, 0) for array in firsts]
    other_firsts = [swap(array[:half], 1) for array in firsts]
    outers = [swap(array[half:], 1) for array in firsts]
    other_seconds = [swap(array, 1) for array in seconds]
    late = [jnp.concatenate([mine[:part], other[part:]]) for mine, other in zip(seconds, other_seconds)]
    late_two = [exchange(array, 1) for array in late]
    late_one = [exchange(array, 0) for array in late]

    near_mine, near_theirs, faces, near_flat = call(
        near_kernel,
        (
            image,
            image,
            jax.ShapeDtypeStruct((5, rows, nz), F32),
            jax.ShapeDtypeStruct((columns, rows * nz), BF16),
        ),
        (coef, near_partial, center, one, two),
    )
    results = call(
        functools.partial(gather_kernel, chips),
        [center_shape] * count + [partial] * count + [center_shape] * count
        + [jax.ShapeDtypeStruct((part, columns, nz), F32)] * count,
        (after(coef, faces), *firsts, *seconds, *other_firsts, *outers, *other_seconds),
    )
    centers, partials, other_centers, other_partials = (results[i * count:(i + 1) * count] for i in range(4))
    applied, = call(
        first_kernel, (whole,), (near_mine, swap(near_theirs, 1)), turning(CORES), out_specs=[ANY]
    )
    left, tall, flatter = call(
        functools.partial(left_kernel, chips),
        (
            jax.ShapeDtypeStruct((total, rows * nz), BF16),
            jax.ShapeDtypeStruct((total, chips * columns), F32),
            jax.ShapeDtypeStruct((chips * columns, total), F32),
        ),
        (faces, near_flat, center, *centers, plain, *other_centers, *partials),
        [pltpu.VMEM((columns, rows * nz // 2), BF16)],
    )
    *images, gram = call(
        functools.partial(gram_kernel, chips, weight),
        [half_image] * (2 * count) + [jax.ShapeDtypeStruct((total, total), F32)],
        (faces, left, tall, flatter, *partials, *centers, *early_one, *early_two),
        [pltpu.VMEM((columns, rows * nz // 2), BF16), pltpu.VMEM((total, chips * columns), F32)],
    )
    done = [*images[:count], *(swap(array, 1) for array in images[count:])]
    parts = slabs * blocks
    shares = gram.reshape(parts, total // parts, total)
    shares = lax.all_to_all(shares, ("dom", "blk"), split_axis=0, concat_axis=0, tiled=True)
    pieces = (*done, *partials, *other_partials, *centers, *other_centers, *late_one, *late_two)
    return tuple(call(
        functools.partial(last_kernel, slabs, blocks),
        (whole, jax.ShapeDtypeStruct((total // parts, total), F32)),
        (shares, applied, faces, *pieces),
        turning(CORES * count),
        [VMEM, ANY] + [VMEM] * (1 + len(pieces)),
        [ANY, VMEM],
        aliases={1: 0},
    ))


def solution(mesh):
    placed = (P("blk", "dom", "roll", None), P("dom", "roll", None), P(), P())
    return jax.shard_map(
        per_device,
        mesh=mesh,
        in_specs=placed,
        out_specs=(P("roll", "dom", "blk", None), P(("dom", "blk"), "roll")),
        check_vma=False,
    )
```

```python
import functools

import jax
import jax.numpy as jnp
from jax import lax
from jax.experimental import pallas as pl
from jax.experimental.pallas import tpu as pltpu
from jax.sharding import PartitionSpec as P

ZONES = 16
CORES = 2
COST = 1 << 30
F32 = jnp.float32
BF16 = jnp.bfloat16
VMEM = pl.BlockSpec(memory_space=pltpu.VMEM)
SMEM = pl.BlockSpec(memory_space=pltpu.SMEM)
HBM = pl.BlockSpec(memory_space=pltpu.HBM)
ANY = pl.BlockSpec(memory_space=pl.ANY)


def lookup(zone, table_ref):
    result = jnp.zeros(zone.shape, F32)
    for which in range(ZONES):
        result = jnp.where(zone == which, table_ref[which], result)
    return result


def cond_of(zone, table_ref):
    return lookup(zone, table_ref).astype(BF16).astype(F32)


def prepare_kernel(chips, basis_hbm, zone_hbm, cond_hbm, *refs):
    near, center, plain, firsts, seconds = *refs[:3], refs[3:2 + chips], refs[2 + chips:2 * chips + 1]
    basis, zone, table, wide, turned, cond_pad, in_sems, out_sems = refs[2 * chips + 1:]
    columns, _, ny, nz = basis.shape
    rows = ny // chips
    chip = lax.axis_index("blk") // CORES
    step = 16
    chunks = columns // step
    loads = [
        pltpu.make_async_copy(basis_hbm.at[pl.ds(i * step, step)], basis.at[pl.ds(i * step, step)], in_sems.at[i])
        for i in range(chunks)
    ]
    loads.append(pltpu.make_async_copy(zone_hbm, zone, in_sems.at[chunks]))
    loads.append(pltpu.make_async_copy(cond_hbm, table, in_sems.at[chunks + 1]))
    for load in loads:
        load.start()
    turned[0] = jnp.zeros((columns, nz), BF16)
    turned[ny + 1] = jnp.zeros((columns, nz), BF16)
    stores = []

    def store(source, target):
        copy = pltpu.make_async_copy(source, target, out_sems.at[len(stores)])
        copy.start()
        stores.append(copy)

    loads[chunks].wait()
    loads[chunks + 1].wait()
    mine = zone[0, pl.ds(pl.multiple_of(chip * rows, rows), rows), :]
    own = cond_of(mine, table)
    cond_pad[...] = jnp.concatenate([own, jnp.zeros((columns - rows, nz), F32)], 0).astype(BF16)
    store(cond_pad, near.at[rows])
    for i in range(chunks):
        loads[i].wait()
        some = pl.ds(i * step, step)
        for c in range(i * step, (i + 1) * step):
            wide[c * ny:(c + 1) * ny, :] = basis[c, 0].astype(F32)
        for y in range(ny):
            turned[y + 1, some, :] = wide[pl.ds(i * step * ny + y, step, stride=ny), :].astype(BF16)
        store(turned.at[pl.ds(chip * rows + 1, rows), some], near.at[pl.ds(0, rows), some])
        for k in range(1, chips):
            start = (chip ^ k) * rows
            store(turned.at[pl.ds(start, rows // 2 + 1), some], firsts[k - 1].at[:, some])
            store(turned.at[pl.ds(start + rows // 2 + 1, rows // 2 + 1), some], seconds[k - 1].at[:, some])
        store(turned.at[pl.ds(chip * rows, rows + 2), some], center.at[:, some])
        store(turned.at[pl.ds(chip * rows + 1, rows), some], plain.at[:, some])
    for copy in stores:
        copy.wait()


def prepare(basis, zone, cond_table, chips):
    columns, _, ny, nz = basis.shape
    rows = ny // chips
    slabs = [rows + 1, rows + 2, rows] + [rows // 2 + 1] * (2 * chips - 2)
    shapes = [jax.ShapeDtypeStruct((n, columns, nz), BF16) for n in slabs]
    results = pl.pallas_call(
        functools.partial(prepare_kernel, chips),
        out_shape=shapes,
        in_specs=[HBM, HBM, HBM],
        out_specs=[pl.BlockSpec(memory_space=pl.ANY)] * len(shapes),
        scratch_shapes=[
            pltpu.VMEM(basis.shape, BF16),
            pltpu.VMEM(zone.shape, jnp.int32),
            pltpu.SMEM((ZONES,), F32),
            pltpu.VMEM((columns * ny, nz), F32),
            pltpu.VMEM((ny + 2, columns, nz), BF16),
            pltpu.VMEM((columns, nz), BF16),
            pltpu.SemaphoreType.DMA((columns // 16 + 2,)),
            pltpu.SemaphoreType.DMA((1 + (2 * chips + 1) * (columns // 16),)),
        ],
        compiler_params=pltpu.CompilerParams(vmem_limit_bytes=16 << 20),
    )(*[pltpu.with_memory_space_constraint(x, pltpu.HBM) for x in (basis, zone, cond_table)])
    return (*results[:3], results[3:2 + chips], results[2 + chips:])


def plane_kernel(chips, zone_ref, cond_ref, heat_ref, center, coef, partial, cond_pad):
    rows = partial.shape[0]
    nz = center.shape[2]
    ny = zone_ref.shape[1]
    chip = lax.axis_index("blk") // CORES
    cond_pad[0:8, :] = jnp.zeros((8, nz), F32)
    cond_pad[8:8 + ny, :] = cond_of(zone_ref[0], cond_ref)
    cond_pad[8 + ny:16 + ny, :] = jnp.zeros((8, nz), F32)
    base = pl.multiple_of(chip * rows, 8)
    near = cond_pad[pl.ds(base, rows + 16), :]
    own = near[8:8 + rows]
    lane = lax.broadcasted_iota(jnp.int32, (rows, nz), 1)
    coef[0] = lookup(zone_ref[0, pl.ds(base, rows), :], heat_ref)
    beside = (
        near[7:7 + rows],
        near[9:9 + rows],
        jnp.where(lane == 0, 0.0, pltpu.roll(own, 1, 1)),
        jnp.where(lane == nz - 1, 0.0, pltpu.roll(own, nz - 1, 1)),
    )
    for which, other in enumerate(beside):
        coef[1 + which] = 0.5 * (own + other)
    coef[5] = own
    plane_rows(coef, center, partial)


def plane_rows(coef, center, partial):
    columns, nz = center.shape[1:]
    lane = lax.broadcasted_iota(jnp.int32, (columns, nz), 1)
    first, last = lane == 0, lane == nz - 1
    for y in range(partial.shape[0]):
        face = [jnp.broadcast_to(coef[k, y:y + 1, :], (columns, nz)) for k in range(5)]
        v = center[y + 1].astype(F32)
        total = face[0] * v
        total += face[1] * (v - center[y].astype(F32))
        total += face[2] * (v - center[y + 2].astype(F32))
        total += face[3] * (v - jnp.where(first, 0.0, pltpu.roll(v, 1, 1)))
        total += face[4] * (v - jnp.where(last, 0.0, pltpu.roll(v, nz - 1, 1)))
        partial[y] = total


def image_row(faces, y, partial, v, one, two):
    columns, nz = v.shape
    face = [jnp.broadcast_to(faces[k, y:y + 1, :], (columns, nz)) for k in range(2)]
    v = v.astype(F32)
    total = partial + face[0] * (v - one.astype(F32))
    return (total + face[1] * (v - two.astype(F32))).astype(BF16)


def gram_of(left, right):
    return lax.dot_general(left, right, (((1,), (1,)), ((), ())), preferred_element_type=F32)


def near_kernel(coef, partial, center, one, two, mine, theirs, faces, flat):
    rows, _, nz = partial.shape
    half = rows // CORES
    core = lax.axis_index("blk") % CORES
    for which, ref in enumerate((one, two)):
        faces[which] = 0.5 * (coef[5] + ref[rows].astype(F32)[:rows])
    for y in range(rows):
        image = image_row(faces, y, partial[y], center[y + 1], one[y], two[y])
        flat[:, y * nz:(y + 1) * nz] = image

        @pl.when(core == y // half)
        def _():
            mine[y % half] = image

        @pl.when(core != y // half)
        def _():
            theirs[y % half] = image


def gather_kernel(chips, coef, *refs):
    count = chips - 1
    firsts, seconds, centers, partials = (refs[i * count:(i + 1) * count] for i in range(4))
    for first, second, center, partial in zip(firsts, seconds, centers, partials):
        half = first.shape[0]
        center[0:half] = first[...]
        center[half:2 * half] = second[...]
        plane_rows(coef, center, partial)


def first_far_kernel(chips, faces, *refs):
    count = chips - 1
    partials, centers, ones, twos, images, flats = (refs[i * count:(i + 1) * count] for i in range(6))
    nz = partials[0].shape[2]
    for k in range(count):
        for y in range(partials[k].shape[0] // 2):
            image = image_row(faces, y, partials[k][y], centers[k][y + 1], ones[k][y + 1], twos[k][y + 1])
            flats[k][:, y * nz:(y + 1) * nz] = image
            images[k][y] = image


def left_kernel(chips, weight, flat, center, plain, *refs):
    count = chips - 1
    flats, centers, other_firsts, other_seconds = (refs[i * count:(i + 1) * count] for i in range(4))
    left, gram = refs[4 * count:]
    columns, nz = center.shape[1:]
    rows = center.shape[0] - 2
    half = rows // 2
    me = lax.axis_index("blk")
    for k, ref in enumerate((center, *centers)):
        for core in range(CORES):
            where = pl.ds(pl.multiple_of((me ^ (CORES * k + core)) * columns, columns), columns)
            for y in range(rows):
                if not core:
                    side = ref[y + 1]
                elif not k:
                    side = plain[y]
                else:
                    side = other_firsts[k - 1][y] if y < half else other_seconds[k - 1][y - half]
                left[where, y * nz:(y + 1) * nz] = side
    gram[:, 0:columns] = weight * gram_of(left[...], flat[...])
    for k in range(count):
        gram[:, (k + 1) * columns:(k + 2) * columns] = weight * gram_of(left[:, 0:half * nz], flats[k][...])


def second_far_kernel(chips, weight, faces, left, first_gram, *refs):
    count = chips - 1
    partials, centers, ones, twos, images, mine, theirs = (refs[i * count:(i + 1) * count] for i in range(7))
    gram, flat = refs[7 * count:]
    rows, columns, nz = partials[0].shape
    half = rows // 2
    core = lax.axis_index("blk") % CORES
    gram[:, 0:columns] = first_gram[:, 0:columns]
    for k in range(count):
        for i in range(half):
            y = half + i
            image = image_row(faces, y, partials[k][y], centers[k][y + 1], ones[k][i], twos[k][i])
            flat[:, i * nz:(i + 1) * nz] = image
            other = images[k][i]
            mine[k][i] = jnp.where(core == 0, other, image)
            theirs[k][i] = jnp.where(core == 0, image, other)
        block = slice((k + 1) * columns, (k + 2) * columns)
        gram[:, block] = first_gram[:, block] + weight * gram_of(left[:, half * nz:], flat[...])


def turn_out(image, start, applied, wide, turned, sem):
    rows, columns, _ = image.shape
    for y in range(rows):
        wide[pl.ds(y, columns, stride=rows), :] = image[y].astype(F32)
    for c in range(columns):
        turned[c, 0] = wide[c * rows:(c + 1) * rows, :].astype(BF16)
    copy = pltpu.make_async_copy(turned, applied.at[pl.ds(start, columns)], sem)
    copy.start()
    return copy


def first_kernel(mine, theirs, applied, wide, turned, sems):
    me = lax.axis_index("blk")
    columns = mine.shape[1]
    copies = [
        turn_out(image, (me ^ s) * columns, applied, wide.at[s], turned.at[s], sems.at[s])
        for s, image in enumerate((mine, theirs))
    ]
    for copy in copies:
        copy.wait()


def last_kernel(blocks, applied_in, *refs):
    del applied_in
    images, (applied, wide, turned, sems) = refs[:blocks - CORES], refs[blocks - CORES:]
    me = lax.axis_index("blk")
    columns = images[0].shape[1]
    copies = [
        turn_out(image, (me ^ (s + CORES)) * columns, applied, wide.at[s], turned.at[s], sems.at[s])
        for s, image in enumerate(images)
    ]
    for copy in copies:
        copy.wait()


def sum_kernel(slabs, blocks, shares, reduced):
    chips = blocks // CORES
    columns = shares.shape[2] // chips
    for core in range(CORES):
        sums = []
        for chip in range(chips):
            total = shares[CORES * chip + core]
            for slab in range(1, slabs):
                total += shares[slab * blocks + CORES * chip + core]
            sums.append(total)
        for target in range(chips):
            parts = [sums[chip][:, (chip ^ target) * columns:((chip ^ target) + 1) * columns] for chip in range(chips)]
            start = (CORES * target + core) * columns
            reduced[:, start:start + columns] = functools.reduce(jnp.add, parts)


def per_device(basis, zone, cond_table, heat_table):
    blocks = lax.axis_size("blk")
    slabs = lax.axis_size("dom")
    chips = blocks // CORES
    count = chips - 1
    columns, planes, ny, nz = basis.shape
    rows = ny // chips
    half = ny // blocks
    total = columns * blocks
    weight = 1.0 / (slabs * planes * ny * nz)
    image = jax.ShapeDtypeStruct((half, columns, nz), BF16)
    center_shape = jax.ShapeDtypeStruct((rows + 2, columns, nz), BF16)
    partial = jax.ShapeDtypeStruct((rows, columns, nz), F32)
    whole = jax.ShapeDtypeStruct((total, 1, half, nz), BF16)
    params = pltpu.CompilerParams(vmem_limit_bytes=32 << 20)
    costly = pl.CostEstimate(flops=COST, bytes_accessed=COST // 8, transcendentals=0)
    cheap = pl.CostEstimate(flops=1, bytes_accessed=1, transcendentals=0)

    def call(kernel, out_shape, inputs, scratch=(), specs=None, out_specs=None, cost=cheap, aliases={}):
        return pl.pallas_call(
            kernel,
            out_shape=out_shape,
            in_specs=specs or [VMEM] * len(inputs),
            out_specs=out_specs or [VMEM] * len(out_shape),
            scratch_shapes=scratch,
            input_output_aliases=aliases,
            compiler_params=params,
            cost_estimate=cost,
        )(*inputs)

    def after(value, *others):
        return lax.optimization_barrier((value, *others))[0]

    def swap(array, s):
        return lax.ppermute(array, "blk", [(i, i ^ s) for i in range(blocks)])

    def exchange(array, offset):
        partner = [((d + offset) ^ 1) - offset for d in range(slabs)]
        return lax.ppermute(array, "dom", [(d, to) for d, to in enumerate(partner) if 0 <= to < slabs])

    def turning(n):
        return [
            pltpu.VMEM((n, columns * half, nz), F32),
            pltpu.VMEM((n, columns, 1, half, nz), BF16),
            pltpu.SemaphoreType.DMA((n,)),
        ]

    sent, center, plain, firsts, seconds = prepare(basis, zone, cond_table, chips)
    two = exchange(sent, 1)
    one = exchange(sent, 0)
    plain = swap(plain, 1)
    firsts = [swap(array, CORES * (k + 1)) for k, array in enumerate(firsts)]
    seconds = [swap(array, CORES * (k + 1)) for k, array in enumerate(seconds)]
    coef, near_partial = call(
        functools.partial(plane_kernel, chips),
        (jax.ShapeDtypeStruct((6, rows, nz), F32), partial),
        (zone, cond_table, heat_table, after(center, plain)),
        [pltpu.VMEM((ny + 16, nz), F32)],
        [VMEM, SMEM, SMEM, VMEM],
        cost=costly,
    )
    firsts = [after(array, coef) for array in firsts]
    first_two = [exchange(array, 1) for array in firsts]
    first_one = [exchange(array, 0) for array in firsts]
    second_two = [exchange(array, 1) for array in seconds]
    second_one = [exchange(array, 0) for array in seconds]
    near_mine, near_theirs, faces, near_flat = call(
        near_kernel,
        (
            image,
            image,
            jax.ShapeDtypeStruct((2, rows, nz), F32),
            jax.ShapeDtypeStruct((columns, rows * nz), BF16),
        ),
        (coef, near_partial, center, one, two),
    )
    results = call(
        functools.partial(gather_kernel, chips), [center_shape] * count + [partial] * count, (coef, *firsts, *seconds)
    )
    centers, partials = results[:count], results[count:]
    other_firsts = [swap(after(array, two)[1:], 1) for array in firsts]
    other_seconds = [swap(after(array, two)[:-1], 1) for array in seconds]
    half_flat = jax.ShapeDtypeStruct((columns, rows * nz // 2), BF16)
    results = call(
        functools.partial(first_far_kernel, chips),
        [image] * count + [half_flat] * count,
        (faces, *partials, *centers, *first_one, *first_two),
    )
    images, flats = results[:count], results[count:]
    applied, = call(
        first_kernel, (whole,), (near_mine, swap(near_theirs, 1)), turning(CORES), out_specs=[ANY]
    )
    gram_shape = jax.ShapeDtypeStruct((total, chips * columns), F32)
    left, first_gram = call(
        functools.partial(left_kernel, chips, weight),
        (jax.ShapeDtypeStruct((total, rows * nz), BF16), gram_shape),
        (near_flat, center, plain, *flats, *centers, *other_firsts, *other_seconds),
    )
    *images, gram = call(
        functools.partial(second_far_kernel, chips, weight),
        [image] * (2 * count) + [gram_shape],
        (faces, left, first_gram, *partials, *centers, *second_one, *second_two, *images),
        [pltpu.VMEM((columns, rows * nz // 2), BF16)],
    )
    parts = slabs * blocks
    shares = gram.reshape(parts, total // parts, chips * columns)
    shares = lax.all_to_all(shares, ("dom", "blk"), split_axis=0, concat_axis=0, tiled=True)
    pieces = []
    for k in range(count):
        pieces += [images[k], swap(images[count + k], 1)]
    applied, = call(
        functools.partial(last_kernel, blocks),
        (whole,),
        (applied, *pieces),
        turning(len(pieces)),
        [ANY] + [VMEM] * len(pieces),
        [ANY],
        aliases={0: 0},
    )
    reduced, = call(
        functools.partial(sum_kernel, slabs, blocks), (jax.ShapeDtypeStruct((total // parts, total), F32),), (shares,)
    )
    return applied, reduced


def solution(mesh):
    placed = (P("blk", "dom", "roll", None), P("dom", "roll", None), P(), P())
    return jax.shard_map(
        per_device,
        mesh=mesh,
        in_specs=placed,
        out_specs=(P("roll", "dom", "blk", None), P(("dom", "blk"), "roll")),
        check_vma=False,
    )
```

```python
import functools

import jax
import jax.numpy as jnp
from jax import lax
from jax.experimental import pallas as pl
from jax.experimental.pallas import tpu as pltpu
from jax.sharding import PartitionSpec as P

ZONES = 16
CORES = 2
COST = 1 << 30
F32 = jnp.float32
BF16 = jnp.bfloat16
VMEM = pl.BlockSpec(memory_space=pltpu.VMEM)
SMEM = pl.BlockSpec(memory_space=pltpu.SMEM)
HBM = pl.BlockSpec(memory_space=pltpu.HBM)
ANY = pl.BlockSpec(memory_space=pl.ANY)


def lookup(zone, table_ref):
    result = jnp.zeros(zone.shape, F32)
    for which in range(ZONES):
        result = jnp.where(zone == which, table_ref[which], result)
    return result


def cond_of(zone, table_ref):
    return lookup(zone, table_ref).astype(BF16).astype(F32)


def prepare_kernel(chips, basis_hbm, zone_hbm, cond_hbm, *refs):
    near, center, plain, firsts, seconds = *refs[:3], refs[3:2 + chips], refs[2 + chips:2 * chips + 1]
    basis, zone, table, wide, turned, cond_pad, in_sems, out_sems = refs[2 * chips + 1:]
    columns, _, ny, nz = basis.shape
    rows = ny // chips
    chip = lax.axis_index("blk") // CORES
    step = 16
    chunks = columns // step
    loads = [
        pltpu.make_async_copy(basis_hbm.at[pl.ds(i * step, step)], basis.at[pl.ds(i * step, step)], in_sems.at[i])
        for i in range(chunks)
    ]
    loads.append(pltpu.make_async_copy(zone_hbm, zone, in_sems.at[chunks]))
    loads.append(pltpu.make_async_copy(cond_hbm, table, in_sems.at[chunks + 1]))
    for load in loads:
        load.start()
    turned[0] = jnp.zeros((columns, nz), BF16)
    turned[ny + 1] = jnp.zeros((columns, nz), BF16)
    stores = []

    def store(source, target):
        copy = pltpu.make_async_copy(source, target, out_sems.at[len(stores)])
        copy.start()
        stores.append(copy)

    loads[chunks].wait()
    loads[chunks + 1].wait()
    mine = zone[0, pl.ds(pl.multiple_of(chip * rows, rows), rows), :]
    own = cond_of(mine, table)
    cond_pad[...] = jnp.concatenate([own, jnp.zeros((columns - rows, nz), F32)], 0).astype(BF16)
    store(cond_pad, near.at[rows])
    for i in range(chunks):
        loads[i].wait()
        some = pl.ds(i * step, step)
        for c in range(i * step, (i + 1) * step):
            wide[c * ny:(c + 1) * ny, :] = basis[c, 0].astype(F32)
        for y in range(ny):
            turned[y + 1, some, :] = wide[pl.ds(i * step * ny + y, step, stride=ny), :].astype(BF16)
        store(turned.at[pl.ds(chip * rows + 1, rows), some], near.at[pl.ds(0, rows), some])
        for k in range(1, chips):
            start = (chip ^ k) * rows
            store(turned.at[pl.ds(start, rows // 2 + 1), some], firsts[k - 1].at[:, some])
            store(turned.at[pl.ds(start + rows // 2 + 1, rows // 2 + 1), some], seconds[k - 1].at[:, some])
        store(turned.at[pl.ds(chip * rows, rows + 2), some], center.at[:, some])
        store(turned.at[pl.ds(chip * rows + 1, rows), some], plain.at[:, some])
    for copy in stores:
        copy.wait()


def prepare(basis, zone, cond_table, chips):
    columns, _, ny, nz = basis.shape
    rows = ny // chips
    slabs = [rows + 1, rows + 2, rows] + [rows // 2 + 1] * (2 * chips - 2)
    shapes = [jax.ShapeDtypeStruct((n, columns, nz), BF16) for n in slabs]
    results = pl.pallas_call(
        functools.partial(prepare_kernel, chips),
        out_shape=shapes,
        in_specs=[HBM, HBM, HBM],
        out_specs=[pl.BlockSpec(memory_space=pl.ANY)] * len(shapes),
        scratch_shapes=[
            pltpu.VMEM(basis.shape, BF16),
            pltpu.VMEM(zone.shape, jnp.int32),
            pltpu.SMEM((ZONES,), F32),
            pltpu.VMEM((columns * ny, nz), F32),
            pltpu.VMEM((ny + 2, columns, nz), BF16),
            pltpu.VMEM((columns, nz), BF16),
            pltpu.SemaphoreType.DMA((columns // 16 + 2,)),
            pltpu.SemaphoreType.DMA((1 + (2 * chips + 1) * (columns // 16),)),
        ],
        compiler_params=pltpu.CompilerParams(vmem_limit_bytes=16 << 20),
    )(*[pltpu.with_memory_space_constraint(x, pltpu.HBM) for x in (basis, zone, cond_table)])
    return (*results[:3], results[3:2 + chips], results[2 + chips:])


def plane_kernel(chips, zone_ref, cond_ref, heat_ref, center, coef, partial, cond_pad):
    rows = partial.shape[0]
    nz = center.shape[2]
    ny = zone_ref.shape[1]
    chip = lax.axis_index("blk") // CORES
    cond_pad[0:8, :] = jnp.zeros((8, nz), F32)
    cond_pad[8:8 + ny, :] = cond_of(zone_ref[0], cond_ref)
    cond_pad[8 + ny:16 + ny, :] = jnp.zeros((8, nz), F32)
    base = pl.multiple_of(chip * rows, 8)
    near = cond_pad[pl.ds(base, rows + 16), :]
    own = near[8:8 + rows]
    lane = lax.broadcasted_iota(jnp.int32, (rows, nz), 1)
    coef[0] = lookup(zone_ref[0, pl.ds(base, rows), :], heat_ref)
    beside = (
        near[7:7 + rows],
        near[9:9 + rows],
        jnp.where(lane == 0, 0.0, pltpu.roll(own, 1, 1)),
        jnp.where(lane == nz - 1, 0.0, pltpu.roll(own, nz - 1, 1)),
    )
    for which, other in enumerate(beside):
        coef[1 + which] = 0.5 * (own + other)
    coef[5] = own
    plane_rows(coef, center, partial)


def plane_rows(coef, center, partial):
    columns, nz = center.shape[1:]
    lane = lax.broadcasted_iota(jnp.int32, (columns, nz), 1)
    first, last = lane == 0, lane == nz - 1
    for y in range(partial.shape[0]):
        face = [jnp.broadcast_to(coef[k, y:y + 1, :], (columns, nz)) for k in range(5)]
        v = center[y + 1].astype(F32)
        total = face[0] * v
        total += face[1] * (v - center[y].astype(F32))
        total += face[2] * (v - center[y + 2].astype(F32))
        total += face[3] * (v - jnp.where(first, 0.0, pltpu.roll(v, 1, 1)))
        total += face[4] * (v - jnp.where(last, 0.0, pltpu.roll(v, nz - 1, 1)))
        partial[y] = total


def image_row(faces, y, partial, v, one, two):
    columns, nz = v.shape
    face = [jnp.broadcast_to(faces[k, y:y + 1, :], (columns, nz)) for k in range(2)]
    v = v.astype(F32)
    total = partial + face[0] * (v - one.astype(F32))
    return (total + face[1] * (v - two.astype(F32))).astype(BF16)


def gram_of(left, right):
    return lax.dot_general(left, right, (((1,), (1,)), ((), ())), preferred_element_type=F32)


def near_kernel(coef, partial, center, one, two, mine, theirs, faces, flat):
    rows, _, nz = partial.shape
    half = rows // CORES
    core = lax.axis_index("blk") % CORES
    for which, ref in enumerate((one, two)):
        faces[which] = 0.5 * (coef[5] + ref[rows].astype(F32)[:rows])
    for y in range(rows):
        image = image_row(faces, y, partial[y], center[y + 1], one[y], two[y])
        flat[:, y * nz:(y + 1) * nz] = image

        @pl.when(core == y // half)
        def _():
            mine[y % half] = image

        @pl.when(core != y // half)
        def _():
            theirs[y % half] = image


def gather_kernel(chips, coef, *refs):
    count = chips - 1
    firsts, seconds, centers, partials = (refs[i * count:(i + 1) * count] for i in range(4))
    for first, second, center, partial in zip(firsts, seconds, centers, partials):
        half = first.shape[0]
        center[0:half] = first[...]
        center[half:2 * half] = second[...]
        plane_rows(coef, center, partial)


def first_far_kernel(chips, faces, *refs):
    count = chips - 1
    partials, centers, ones, twos, images, flats = (refs[i * count:(i + 1) * count] for i in range(6))
    nz = partials[0].shape[2]
    for k in range(count):
        for y in range(partials[k].shape[0] // 2):
            image = image_row(faces, y, partials[k][y], centers[k][y + 1], ones[k][y + 1], twos[k][y + 1])
            flats[k][:, y * nz:(y + 1) * nz] = image
            images[k][y] = image


def left_kernel(chips, weight, flat, center, plain, *refs):
    count = chips - 1
    flats, centers, other_firsts, other_seconds = (refs[i * count:(i + 1) * count] for i in range(4))
    left, gram = refs[4 * count:]
    columns, nz = center.shape[1:]
    rows = center.shape[0] - 2
    half = rows // 2
    me = lax.axis_index("blk")
    for k, ref in enumerate((center, *centers)):
        for core in range(CORES):
            where = pl.ds(pl.multiple_of((me ^ (CORES * k + core)) * columns, columns), columns)
            for y in range(rows):
                if not core:
                    side = ref[y + 1]
                elif not k:
                    side = plain[y]
                else:
                    side = other_firsts[k - 1][y] if y < half else other_seconds[k - 1][y - half]
                left[where, y * nz:(y + 1) * nz] = side
    gram[:, 0:columns] = weight * gram_of(left[...], flat[...])
    for k in range(count):
        gram[:, (k + 1) * columns:(k + 2) * columns] = weight * gram_of(left[:, 0:half * nz], flats[k][...])


def second_far_kernel(chips, weight, faces, left, first_gram, *refs):
    count = chips - 1
    partials, centers, ones, twos, images, mine, theirs = (refs[i * count:(i + 1) * count] for i in range(7))
    gram, flat = refs[7 * count:]
    rows, columns, nz = partials[0].shape
    half = rows // 2
    core = lax.axis_index("blk") % CORES
    gram[:, 0:columns] = first_gram[:, 0:columns]
    for k in range(count):
        for i in range(half):
            y = half + i
            image = image_row(faces, y, partials[k][y], centers[k][y + 1], ones[k][i], twos[k][i])
            flat[:, i * nz:(i + 1) * nz] = image
            other = images[k][i]
            mine[k][i] = jnp.where(core == 0, other, image)
            theirs[k][i] = jnp.where(core == 0, image, other)
        block = slice((k + 1) * columns, (k + 2) * columns)
        gram[:, block] = first_gram[:, block] + weight * gram_of(left[:, half * nz:], flat[...])


def turn_out(image, start, applied, wide, turned, sem):
    rows, columns, _ = image.shape
    for y in range(rows):
        wide[pl.ds(y, columns, stride=rows), :] = image[y].astype(F32)
    for c in range(columns):
        turned[c, 0] = wide[c * rows:(c + 1) * rows, :].astype(BF16)
    copy = pltpu.make_async_copy(turned, applied.at[pl.ds(start, columns)], sem)
    copy.start()
    return copy


def first_kernel(mine, theirs, applied, wide, turned, sems):
    me = lax.axis_index("blk")
    columns = mine.shape[1]
    copies = [
        turn_out(image, (me ^ s) * columns, applied, wide.at[s], turned.at[s], sems.at[s])
        for s, image in enumerate((mine, theirs))
    ]
    for copy in copies:
        copy.wait()


def last_kernel(blocks, applied_in, *refs):
    del applied_in
    images, (applied, wide, turned, sems) = refs[:blocks - CORES], refs[blocks - CORES:]
    me = lax.axis_index("blk")
    columns = images[0].shape[1]
    copies = [
        turn_out(image, (me ^ (s + CORES)) * columns, applied, wide.at[s], turned.at[s], sems.at[s])
        for s, image in enumerate(images)
    ]
    for copy in copies:
        copy.wait()


def sum_kernel(slabs, blocks, shares, reduced):
    chips = blocks // CORES
    columns = shares.shape[2] // chips
    for core in range(CORES):
        sums = []
        for chip in range(chips):
            total = shares[CORES * chip + core]
            for slab in range(1, slabs):
                total += shares[slab * blocks + CORES * chip + core]
            sums.append(total)
        for target in range(chips):
            parts = [sums[chip][:, (chip ^ target) * columns:((chip ^ target) + 1) * columns] for chip in range(chips)]
            start = (CORES * target + core) * columns
            reduced[:, start:start + columns] = functools.reduce(jnp.add, parts)


def per_device(basis, zone, cond_table, heat_table):
    blocks = lax.axis_size("blk")
    slabs = lax.axis_size("dom")
    chips = blocks // CORES
    count = chips - 1
    columns, planes, ny, nz = basis.shape
    rows = ny // chips
    half = ny // blocks
    total = columns * blocks
    weight = 1.0 / (slabs * planes * ny * nz)
    image = jax.ShapeDtypeStruct((half, columns, nz), BF16)
    center_shape = jax.ShapeDtypeStruct((rows + 2, columns, nz), BF16)
    partial = jax.ShapeDtypeStruct((rows, columns, nz), F32)
    whole = jax.ShapeDtypeStruct((total, 1, half, nz), BF16)
    params = pltpu.CompilerParams(vmem_limit_bytes=32 << 20)
    costly = pl.CostEstimate(flops=COST, bytes_accessed=COST // 8, transcendentals=0)
    cheap = pl.CostEstimate(flops=1, bytes_accessed=1, transcendentals=0)

    def call(kernel, out_shape, inputs, scratch=(), specs=None, out_specs=None, cost=cheap, aliases={}):
        return pl.pallas_call(
            kernel,
            out_shape=out_shape,
            in_specs=specs or [VMEM] * len(inputs),
            out_specs=out_specs or [VMEM] * len(out_shape),
            scratch_shapes=scratch,
            input_output_aliases=aliases,
            compiler_params=params,
            cost_estimate=cost,
        )(*inputs)

    def after(value, *others):
        return lax.optimization_barrier((value, *others))[0]

    def swap(array, s):
        return lax.ppermute(array, "blk", [(i, i ^ s) for i in range(blocks)])

    def exchange(array, offset):
        partner = [((d + offset) ^ 1) - offset for d in range(slabs)]
        return lax.ppermute(array, "dom", [(d, to) for d, to in enumerate(partner) if 0 <= to < slabs])

    def turning(n):
        return [
            pltpu.VMEM((n, columns * half, nz), F32),
            pltpu.VMEM((n, columns, 1, half, nz), BF16),
            pltpu.SemaphoreType.DMA((n,)),
        ]

    sent, center, plain, firsts, seconds = prepare(basis, zone, cond_table, chips)
    two = exchange(sent, 1)
    one = exchange(sent, 0)
    firsts = [swap(array, CORES * (k + 1)) for k, array in enumerate(firsts)]
    seconds = [swap(array, CORES * (k + 1)) for k, array in enumerate(seconds)]
    coef, near_partial = call(
        functools.partial(plane_kernel, chips),
        (jax.ShapeDtypeStruct((6, rows, nz), F32), partial),
        (zone, cond_table, heat_table, center),
        [pltpu.VMEM((ny + 16, nz), F32)],
        [VMEM, SMEM, SMEM, VMEM],
        cost=costly,
    )
    firsts = [after(array, coef) for array in firsts]
    first_two = [exchange(array, 1) for array in firsts]
    first_one = [exchange(array, 0) for array in firsts]
    second_two = [exchange(array, 1) for array in seconds]
    second_one = [exchange(array, 0) for array in seconds]
    near_mine, near_theirs, faces, near_flat = call(
        near_kernel,
        (
            image,
            image,
            jax.ShapeDtypeStruct((2, rows, nz), F32),
            jax.ShapeDtypeStruct((columns, rows * nz), BF16),
        ),
        (coef, near_partial, center, one, two),
    )
    results = call(
        functools.partial(gather_kernel, chips), [center_shape] * count + [partial] * count, (coef, *firsts, *seconds)
    )
    centers, partials = results[:count], results[count:]
    plain = swap(after(plain, one, two), 1)
    other_firsts = [swap(after(array, two)[1:], 1) for array in firsts]
    other_seconds = [swap(after(array, two)[:-1], 1) for array in seconds]
    half_flat = jax.ShapeDtypeStruct((columns, rows * nz // 2), BF16)
    results = call(
        functools.partial(first_far_kernel, chips),
        [image] * count + [half_flat] * count,
        (faces, *partials, *centers, *first_one, *first_two),
    )
    images, flats = results[:count], results[count:]
    applied, = call(
        first_kernel, (whole,), (near_mine, swap(near_theirs, 1)), turning(CORES), out_specs=[ANY]
    )
    gram_shape = jax.ShapeDtypeStruct((total, chips * columns), F32)
    left, first_gram = call(
        functools.partial(left_kernel, chips, weight),
        (jax.ShapeDtypeStruct((total, rows * nz), BF16), gram_shape),
        (near_flat, center, plain, *flats, *centers, *other_firsts, *other_seconds),
    )
    *images, gram = call(
        functools.partial(second_far_kernel, chips, weight),
        [image] * (2 * count) + [gram_shape],
        (faces, left, first_gram, *partials, *centers, *second_one, *second_two, *images),
        [pltpu.VMEM((columns, rows * nz // 2), BF16)],
    )
    parts = slabs * blocks
    shares = gram.reshape(parts, total // parts, chips * columns)
    shares = lax.all_to_all(shares, ("dom", "blk"), split_axis=0, concat_axis=0, tiled=True)
    pieces = []
    for k in range(count):
        pieces += [images[k], swap(images[count + k], 1)]
    applied, = call(
        functools.partial(last_kernel, blocks),
        (whole,),
        (applied, *pieces),
        turning(len(pieces)),
        [ANY] + [VMEM] * len(pieces),
        [ANY],
        aliases={0: 0},
    )
    reduced, = call(
        functools.partial(sum_kernel, slabs, blocks), (jax.ShapeDtypeStruct((total // parts, total), F32),), (after(shares, applied),)
    )
    return applied, reduced


def solution(mesh):
    placed = (P("blk", "dom", "roll", None), P("dom", "roll", None), P(), P())
    return jax.shard_map(
        per_device,
        mesh=mesh,
        in_specs=placed,
        out_specs=(P("roll", "dom", "blk", None), P(("dom", "blk"), "roll")),
        check_vma=False,
    )
```

```python
import functools

import jax
import jax.numpy as jnp
from jax import lax
from jax.experimental import pallas as pl
from jax.experimental.pallas import tpu as pltpu
from jax.sharding import PartitionSpec as P

ZONES = 16
CORES = 2
COST = 1 << 30
F32 = jnp.float32
BF16 = jnp.bfloat16
VMEM = pl.BlockSpec(memory_space=pltpu.VMEM)
SMEM = pl.BlockSpec(memory_space=pltpu.SMEM)
HBM = pl.BlockSpec(memory_space=pltpu.HBM)
ANY = pl.BlockSpec(memory_space=pl.ANY)


def lookup(zone, table_ref):
    result = jnp.zeros(zone.shape, F32)
    for which in range(ZONES):
        result = jnp.where(zone == which, table_ref[which], result)
    return result


def cond_of(zone, table_ref):
    return lookup(zone, table_ref).astype(BF16).astype(F32)


def prepare_kernel(chips, basis_hbm, zone_hbm, cond_hbm, *refs):
    near, center, plain, firsts, seconds = *refs[:3], refs[3:2 + chips], refs[2 + chips:2 * chips + 1]
    basis, zone, table, wide, turned, cond_pad, in_sems, out_sems = refs[2 * chips + 1:]
    columns, _, ny, nz = basis.shape
    rows = ny // chips
    chip = lax.axis_index("blk") // CORES
    step = 16
    chunks = columns // step
    loads = [
        pltpu.make_async_copy(basis_hbm.at[pl.ds(i * step, step)], basis.at[pl.ds(i * step, step)], in_sems.at[i])
        for i in range(chunks)
    ]
    loads.append(pltpu.make_async_copy(zone_hbm, zone, in_sems.at[chunks]))
    loads.append(pltpu.make_async_copy(cond_hbm, table, in_sems.at[chunks + 1]))
    for load in loads:
        load.start()
    turned[0] = jnp.zeros((columns, nz), BF16)
    turned[ny + 1] = jnp.zeros((columns, nz), BF16)
    stores = []

    def store(source, target):
        copy = pltpu.make_async_copy(source, target, out_sems.at[len(stores)])
        copy.start()
        stores.append(copy)

    loads[chunks].wait()
    loads[chunks + 1].wait()
    mine = zone[0, pl.ds(pl.multiple_of(chip * rows, rows), rows), :]
    own = cond_of(mine, table)
    cond_pad[...] = jnp.concatenate([own, jnp.zeros((columns - rows, nz), F32)], 0).astype(BF16)
    store(cond_pad, near.at[rows])
    for i in range(chunks):
        loads[i].wait()
        some = pl.ds(i * step, step)
        for c in range(i * step, (i + 1) * step):
            wide[c * ny:(c + 1) * ny, :] = basis[c, 0].astype(F32)
        for y in range(ny):
            turned[y + 1, some, :] = wide[pl.ds(i * step * ny + y, step, stride=ny), :].astype(BF16)
        store(turned.at[pl.ds(chip * rows + 1, rows), some], near.at[pl.ds(0, rows), some])
        for k in range(1, chips):
            start = (chip ^ k) * rows
            store(turned.at[pl.ds(start, rows // 2 + 1), some], firsts[k - 1].at[:, some])
            store(turned.at[pl.ds(start + rows // 2 + 1, rows // 2 + 1), some], seconds[k - 1].at[:, some])
        store(turned.at[pl.ds(chip * rows, rows + 2), some], center.at[:, some])
        store(turned.at[pl.ds(chip * rows + 1, rows), some], plain.at[:, some])
    for copy in stores:
        copy.wait()


def prepare(basis, zone, cond_table, chips):
    columns, _, ny, nz = basis.shape
    rows = ny // chips
    slabs = [rows + 1, rows + 2, rows] + [rows // 2 + 1] * (2 * chips - 2)
    shapes = [jax.ShapeDtypeStruct((n, columns, nz), BF16) for n in slabs]
    results = pl.pallas_call(
        functools.partial(prepare_kernel, chips),
        out_shape=shapes,
        in_specs=[HBM, HBM, HBM],
        out_specs=[pl.BlockSpec(memory_space=pl.ANY)] * len(shapes),
        scratch_shapes=[
            pltpu.VMEM(basis.shape, BF16),
            pltpu.VMEM(zone.shape, jnp.int32),
            pltpu.SMEM((ZONES,), F32),
            pltpu.VMEM((columns * ny, nz), F32),
            pltpu.VMEM((ny + 2, columns, nz), BF16),
            pltpu.VMEM((columns, nz), BF16),
            pltpu.SemaphoreType.DMA((columns // 16 + 2,)),
            pltpu.SemaphoreType.DMA((1 + (2 * chips + 1) * (columns // 16),)),
        ],
        compiler_params=pltpu.CompilerParams(vmem_limit_bytes=16 << 20),
    )(*[pltpu.with_memory_space_constraint(x, pltpu.HBM) for x in (basis, zone, cond_table)])
    return (*results[:3], results[3:2 + chips], results[2 + chips:])


def plane_kernel(chips, zone_ref, cond_ref, heat_ref, center, coef, partial, cond_pad):
    rows = partial.shape[0]
    nz = center.shape[2]
    ny = zone_ref.shape[1]
    chip = lax.axis_index("blk") // CORES
    cond_pad[0:8, :] = jnp.zeros((8, nz), F32)
    cond_pad[8:8 + ny, :] = cond_of(zone_ref[0], cond_ref)
    cond_pad[8 + ny:16 + ny, :] = jnp.zeros((8, nz), F32)
    base = pl.multiple_of(chip * rows, 8)
    near = cond_pad[pl.ds(base, rows + 16), :]
    own = near[8:8 + rows]
    lane = lax.broadcasted_iota(jnp.int32, (rows, nz), 1)
    coef[0] = lookup(zone_ref[0, pl.ds(base, rows), :], heat_ref)
    beside = (
        near[7:7 + rows],
        near[9:9 + rows],
        jnp.where(lane == 0, 0.0, pltpu.roll(own, 1, 1)),
        jnp.where(lane == nz - 1, 0.0, pltpu.roll(own, nz - 1, 1)),
    )
    for which, other in enumerate(beside):
        coef[1 + which] = 0.5 * (own + other)
    coef[5] = own
    plane_rows(coef, center, partial)


def plane_rows(coef, center, partial):
    columns, nz = center.shape[1:]
    lane = lax.broadcasted_iota(jnp.int32, (columns, nz), 1)
    first, last = lane == 0, lane == nz - 1
    for y in range(partial.shape[0]):
        face = [jnp.broadcast_to(coef[k, y:y + 1, :], (columns, nz)) for k in range(5)]
        v = center[y + 1].astype(F32)
        total = face[0] * v
        total += face[1] * (v - center[y].astype(F32))
        total += face[2] * (v - center[y + 2].astype(F32))
        total += face[3] * (v - jnp.where(first, 0.0, pltpu.roll(v, 1, 1)))
        total += face[4] * (v - jnp.where(last, 0.0, pltpu.roll(v, nz - 1, 1)))
        partial[y] = total


def image_row(faces, y, partial, v, one, two):
    columns, nz = v.shape
    face = [jnp.broadcast_to(faces[k, y:y + 1, :], (columns, nz)) for k in range(2)]
    v = v.astype(F32)
    total = partial + face[0] * (v - one.astype(F32))
    return (total + face[1] * (v - two.astype(F32))).astype(BF16)


def gram_of(left, right):
    return lax.dot_general(left, right, (((1,), (1,)), ((), ())), preferred_element_type=F32)


def near_kernel(coef, partial, center, one, two, mine, theirs, faces, flat):
    rows, _, nz = partial.shape
    half = rows // CORES
    core = lax.axis_index("blk") % CORES
    for which, ref in enumerate((one, two)):
        faces[which] = 0.5 * (coef[5] + ref[rows].astype(F32)[:rows])
    for y in range(rows):
        image = image_row(faces, y, partial[y], center[y + 1], one[y], two[y])
        flat[:, y * nz:(y + 1) * nz] = image

        @pl.when(core == y // half)
        def _():
            mine[y % half] = image

        @pl.when(core != y // half)
        def _():
            theirs[y % half] = image


def gather_kernel(chips, coef, *refs):
    count = chips - 1
    firsts, seconds, centers, partials = (refs[i * count:(i + 1) * count] for i in range(4))
    for first, second, center, partial in zip(firsts, seconds, centers, partials):
        half = first.shape[0]
        center[0:half] = first[...]
        center[half:2 * half] = second[...]
        plane_rows(coef, center, partial)


def first_far_kernel(chips, faces, *refs):
    count = chips - 1
    partials, centers, twos, ones, images, flats = (refs[i * count:(i + 1) * count] for i in range(6))
    nz = partials[0].shape[2]
    for k in range(count):
        for y in range(partials[k].shape[0] // 2):
            image = image_row(faces, y, partials[k][y], centers[k][y + 1], ones[k][y + 1], twos[k][y + 1])
            flats[k][:, y * nz:(y + 1) * nz] = image
            images[k][y] = image


def left_kernel(chips, weight, flat, center, plain, *refs):
    count = chips - 1
    flats, centers, other_firsts, other_seconds = (refs[i * count:(i + 1) * count] for i in range(4))
    left, gram = refs[4 * count:]
    columns, nz = center.shape[1:]
    rows = center.shape[0] - 2
    half = rows // 2
    me = lax.axis_index("blk")
    for k, ref in enumerate((center, *centers)):
        for core in range(CORES):
            where = pl.ds(pl.multiple_of((me ^ (CORES * k + core)) * columns, columns), columns)
            for y in range(rows):
                if not core:
                    side = ref[y + 1]
                elif not k:
                    side = plain[y]
                else:
                    side = other_firsts[k - 1][y] if y < half else other_seconds[k - 1][y - half]
                left[where, y * nz:(y + 1) * nz] = side
    gram[:, 0:columns] = weight * gram_of(left[...], flat[...])
    for k in range(count):
        gram[:, (k + 1) * columns:(k + 2) * columns] = weight * gram_of(left[:, 0:half * nz], flats[k][...])


def second_far_kernel(chips, weight, faces, left, first_gram, *refs):
    count = chips - 1
    partials, centers, twos, ones, images, mine, theirs = (refs[i * count:(i + 1) * count] for i in range(7))
    gram, flat = refs[7 * count:]
    rows, columns, nz = partials[0].shape
    half = rows // 2
    core = lax.axis_index("blk") % CORES
    gram[:, 0:columns] = first_gram[:, 0:columns]
    for k in range(count):
        for i in range(half):
            y = half + i
            image = image_row(faces, y, partials[k][y], centers[k][y + 1], ones[k][i], twos[k][i])
            flat[:, i * nz:(i + 1) * nz] = image
            other = images[k][i]
            mine[k][i] = jnp.where(core == 0, other, image)
            theirs[k][i] = jnp.where(core == 0, image, other)
        block = slice((k + 1) * columns, (k + 2) * columns)
        gram[:, block] = first_gram[:, block] + weight * gram_of(left[:, half * nz:], flat[...])


def turn_out(image, start, applied, wide, turned, sem):
    rows, columns, _ = image.shape
    for y in range(rows):
        wide[pl.ds(y, columns, stride=rows), :] = image[y].astype(F32)
    for c in range(columns):
        turned[c, 0] = wide[c * rows:(c + 1) * rows, :].astype(BF16)
    copy = pltpu.make_async_copy(turned, applied.at[pl.ds(start, columns)], sem)
    copy.start()
    return copy


def first_kernel(mine, theirs, applied, wide, turned, sems):
    me = lax.axis_index("blk")
    columns = mine.shape[1]
    copies = [
        turn_out(image, (me ^ s) * columns, applied, wide.at[s], turned.at[s], sems.at[s])
        for s, image in enumerate((mine, theirs))
    ]
    for copy in copies:
        copy.wait()


def last_kernel(blocks, applied_in, *refs):
    del applied_in
    images, (applied, wide, turned, sems) = refs[:blocks - CORES], refs[blocks - CORES:]
    me = lax.axis_index("blk")
    columns = images[0].shape[1]
    copies = [
        turn_out(image, (me ^ (s + CORES)) * columns, applied, wide.at[s], turned.at[s], sems.at[s])
        for s, image in enumerate(images)
    ]
    for copy in copies:
        copy.wait()


def sum_kernel(slabs, blocks, shares, reduced):
    chips = blocks // CORES
    columns = shares.shape[2] // chips
    for core in range(CORES):
        sums = []
        for chip in range(chips):
            total = shares[CORES * chip + core]
            for slab in range(1, slabs):
                total += shares[slab * blocks + CORES * chip + core]
            sums.append(total)
        for target in range(chips):
            parts = [sums[chip][:, (chip ^ target) * columns:((chip ^ target) + 1) * columns] for chip in range(chips)]
            start = (CORES * target + core) * columns
            reduced[:, start:start + columns] = functools.reduce(jnp.add, parts)


def per_device(basis, zone, cond_table, heat_table):
    blocks = lax.axis_size("blk")
    slabs = lax.axis_size("dom")
    chips = blocks // CORES
    count = chips - 1
    columns, planes, ny, nz = basis.shape
    rows = ny // chips
    half = ny // blocks
    total = columns * blocks
    weight = 1.0 / (slabs * planes * ny * nz)
    image = jax.ShapeDtypeStruct((half, columns, nz), BF16)
    center_shape = jax.ShapeDtypeStruct((rows + 2, columns, nz), BF16)
    partial = jax.ShapeDtypeStruct((rows, columns, nz), F32)
    whole = jax.ShapeDtypeStruct((total, 1, half, nz), BF16)
    params = pltpu.CompilerParams(vmem_limit_bytes=32 << 20)
    costly = pl.CostEstimate(flops=COST, bytes_accessed=COST // 8, transcendentals=0)
    cheap = pl.CostEstimate(flops=1, bytes_accessed=1, transcendentals=0)

    def call(kernel, out_shape, inputs, scratch=(), specs=None, out_specs=None, cost=cheap, aliases={}):
        return pl.pallas_call(
            kernel,
            out_shape=out_shape,
            in_specs=specs or [VMEM] * len(inputs),
            out_specs=out_specs or [VMEM] * len(out_shape),
            scratch_shapes=scratch,
            input_output_aliases=aliases,
            compiler_params=params,
            cost_estimate=cost,
        )(*inputs)

    def after(value, *others):
        return lax.optimization_barrier((value, *others))[0]

    def swap(array, s):
        return lax.ppermute(array, "blk", [(i, i ^ s) for i in range(blocks)])

    def exchange(array, offset):
        partner = [((d + offset) ^ 1) - offset for d in range(slabs)]
        return lax.ppermute(array, "dom", [(d, to) for d, to in enumerate(partner) if 0 <= to < slabs])

    def turning(n):
        return [
            pltpu.VMEM((n, columns * half, nz), F32),
            pltpu.VMEM((n, columns, 1, half, nz), BF16),
            pltpu.SemaphoreType.DMA((n,)),
        ]

    sent, center, plain, firsts, seconds = prepare(basis, zone, cond_table, chips)
    two = exchange(sent, 1)
    one = exchange(sent, 0)
    firsts = [swap(array, CORES * (k + 1)) for k, array in enumerate(firsts)]
    coef, near_partial = call(
        functools.partial(plane_kernel, chips),
        (jax.ShapeDtypeStruct((6, rows, nz), F32), partial),
        (zone, cond_table, heat_table, center),
        [pltpu.VMEM((ny + 16, nz), F32)],
        [VMEM, SMEM, SMEM, VMEM],
        cost=costly,
    )
    seconds = [swap(after(array, coef), CORES * (k + 1)) for k, array in enumerate(seconds)]
    firsts = [after(array, coef) for array in firsts]
    first_two = [exchange(array, 1) for array in firsts]
    first_one = [exchange(array, 0) for array in firsts]
    second_two = [exchange(array, 1) for array in seconds]
    second_one = [exchange(array, 0) for array in seconds]
    near_mine, near_theirs, faces, near_flat = call(
        near_kernel,
        (
            image,
            image,
            jax.ShapeDtypeStruct((2, rows, nz), F32),
            jax.ShapeDtypeStruct((columns, rows * nz), BF16),
        ),
        (coef, near_partial, center, one, two),
    )
    results = call(
        functools.partial(gather_kernel, chips), [center_shape] * count + [partial] * count, (coef, *firsts, *seconds)
    )
    centers, partials = results[:count], results[count:]
    plain = swap(after(plain, *seconds), 1)
    other_firsts = [swap(after(array, two)[1:], 1) for array in firsts]
    other_seconds = [swap(after(array, two)[:-1], 1) for array in seconds]
    half_flat = jax.ShapeDtypeStruct((columns, rows * nz // 2), BF16)
    results = call(
        functools.partial(first_far_kernel, chips),
        [image] * count + [half_flat] * count,
        (faces, *partials, *centers, *first_two, *first_one),
    )
    images, flats = results[:count], results[count:]
    applied, = call(
        first_kernel, (whole,), (near_mine, swap(near_theirs, 1)), turning(CORES), out_specs=[ANY]
    )
    gram_shape = jax.ShapeDtypeStruct((total, chips * columns), F32)
    left, first_gram = call(
        functools.partial(left_kernel, chips, weight),
        (jax.ShapeDtypeStruct((total, rows * nz), BF16), gram_shape),
        (near_flat, center, plain, *flats, *centers, *other_firsts, *other_seconds),
    )
    *images, gram = call(
        functools.partial(second_far_kernel, chips, weight),
        [image] * (2 * count) + [gram_shape],
        (faces, left, first_gram, *partials, *centers, *second_two, *second_one, *images),
        [pltpu.VMEM((columns, rows * nz // 2), BF16)],
    )
    parts = slabs * blocks
    shares = gram.reshape(parts, total // parts, chips * columns)
    shares = lax.all_to_all(shares, ("dom", "blk"), split_axis=0, concat_axis=0, tiled=True)
    pieces = []
    for k in range(count):
        pieces += [images[k], swap(images[count + k], 1)]
    applied, = call(
        functools.partial(last_kernel, blocks),
        (whole,),
        (applied, *pieces),
        turning(len(pieces)),
        [ANY] + [VMEM] * len(pieces),
        [ANY],
        aliases={0: 0},
    )
    reduced, = call(
        functools.partial(sum_kernel, slabs, blocks), (jax.ShapeDtypeStruct((total // parts, total), F32),), (after(shares, applied),)
    )
    return applied, reduced


def solution(mesh):
    placed = (P("blk", "dom", "roll", None), P("dom", "roll", None), P(), P())
    return jax.shard_map(
        per_device,
        mesh=mesh,
        in_specs=placed,
        out_specs=(P("roll", "dom", "blk", None), P(("dom", "blk"), "roll")),
        check_vma=False,
    )
```

```python
import functools

import jax
import jax.numpy as jnp
from jax import lax
from jax.experimental import pallas as pl
from jax.experimental.pallas import tpu as pltpu
from jax.sharding import PartitionSpec as P

ZONES = 16
CORES = 2
COST = 1 << 30
F32 = jnp.float32
BF16 = jnp.bfloat16
VMEM = pl.BlockSpec(memory_space=pltpu.VMEM)
SMEM = pl.BlockSpec(memory_space=pltpu.SMEM)
HBM = pl.BlockSpec(memory_space=pltpu.HBM)
ANY = pl.BlockSpec(memory_space=pl.ANY)


def lookup(zone, table_ref):
    result = jnp.zeros(zone.shape, F32)
    for which in range(ZONES):
        result = jnp.where(zone == which, table_ref[which], result)
    return result


def cond_of(zone, table_ref):
    return lookup(zone, table_ref).astype(BF16).astype(F32)


def prepare_kernel(chips, basis_hbm, zone_hbm, cond_hbm, *refs):
    near, outer, firsts, seconds = *refs[:2], refs[2:1 + chips], refs[1 + chips:2 * chips]
    basis, zone, table, wide, turned, cond_pad, in_sems, out_sems = refs[2 * chips:]
    columns, _, ny, nz = basis.shape
    rows = ny // chips
    chip = lax.axis_index("blk") // CORES
    step = 16
    chunks = columns // step
    loads = [
        pltpu.make_async_copy(basis_hbm.at[pl.ds(i * step, step)], basis.at[pl.ds(i * step, step)], in_sems.at[i])
        for i in range(chunks)
    ]
    loads.append(pltpu.make_async_copy(zone_hbm, zone, in_sems.at[chunks]))
    loads.append(pltpu.make_async_copy(cond_hbm, table, in_sems.at[chunks + 1]))
    for load in loads:
        load.start()
    turned[0] = jnp.zeros((columns, nz), BF16)
    turned[ny + 1] = jnp.zeros((columns, nz), BF16)
    stores = []

    def store(source, target):
        copy = pltpu.make_async_copy(source, target, out_sems.at[len(stores)])
        copy.start()
        stores.append(copy)

    loads[chunks].wait()
    loads[chunks + 1].wait()
    mine = zone[0, pl.ds(pl.multiple_of(chip * rows, rows), rows), :]
    own = cond_of(mine, table)
    cond_pad[...] = jnp.concatenate([own, jnp.zeros((columns - rows, nz), F32)], 0).astype(BF16)
    store(cond_pad, near.at[rows])
    for i in range(chunks):
        loads[i].wait()
        some = pl.ds(i * step, step)
        for c in range(i * step, (i + 1) * step):
            wide[c * ny:(c + 1) * ny, :] = basis[c, 0].astype(F32)
        for y in range(ny):
            turned[y + 1, some, :] = wide[pl.ds(i * step * ny + y, step, stride=ny), :].astype(BF16)
        store(turned.at[pl.ds(chip * rows + 1, rows), some], near.at[pl.ds(0, rows), some])
        for k in range(1, chips):
            start = (chip ^ k) * rows
            store(turned.at[pl.ds(start, rows // 2 + 1), some], firsts[k - 1].at[:, some])
            store(turned.at[pl.ds(start + rows // 2 + 1, rows // 2 + 1), some], seconds[k - 1].at[:, some])
    store(turned.at[pl.ds(chip * rows, 1)], outer.at[pl.ds(0, 1)])
    store(turned.at[pl.ds((chip + 1) * rows + 1, 1)], outer.at[pl.ds(1, 1)])
    for copy in stores:
        copy.wait()


def prepare(basis, zone, cond_table, chips):
    columns, _, ny, nz = basis.shape
    rows = ny // chips
    slabs = [rows + 1, 2] + [rows // 2 + 1] * (2 * chips - 2)
    shapes = [jax.ShapeDtypeStruct((n, columns, nz), BF16) for n in slabs]
    results = pl.pallas_call(
        functools.partial(prepare_kernel, chips),
        out_shape=shapes,
        in_specs=[HBM, HBM, HBM],
        out_specs=[pl.BlockSpec(memory_space=pl.ANY)] * len(shapes),
        scratch_shapes=[
            pltpu.VMEM(basis.shape, BF16),
            pltpu.VMEM(zone.shape, jnp.int32),
            pltpu.SMEM((ZONES,), F32),
            pltpu.VMEM((columns * ny, nz), F32),
            pltpu.VMEM((ny + 2, columns, nz), BF16),
            pltpu.VMEM((columns, nz), BF16),
            pltpu.SemaphoreType.DMA((columns // 16 + 2,)),
            pltpu.SemaphoreType.DMA((3 + (2 * chips - 1) * (columns // 16),)),
        ],
        compiler_params=pltpu.CompilerParams(vmem_limit_bytes=16 << 20),
    )(*[pltpu.with_memory_space_constraint(x, pltpu.HBM) for x in (basis, zone, cond_table)])
    return (*results[:2], results[2:1 + chips], results[1 + chips:])


def plane_kernel(chips, zone_ref, cond_ref, heat_ref, near_rows, outer, coef, partial, cond_pad, center):
    rows, _, nz = partial.shape
    center[0] = outer[0]
    center[1:rows + 1] = near_rows[0:rows]
    center[rows + 1] = outer[1]
    ny = zone_ref.shape[1]
    chip = lax.axis_index("blk") // CORES
    cond_pad[0:8, :] = jnp.zeros((8, nz), F32)
    cond_pad[8:8 + ny, :] = cond_of(zone_ref[0], cond_ref)
    cond_pad[8 + ny:16 + ny, :] = jnp.zeros((8, nz), F32)
    base = pl.multiple_of(chip * rows, 8)
    near = cond_pad[pl.ds(base, rows + 16), :]
    own = near[8:8 + rows]
    lane = lax.broadcasted_iota(jnp.int32, (rows, nz), 1)
    coef[0] = lookup(zone_ref[0, pl.ds(base, rows), :], heat_ref)
    beside = (
        near[7:7 + rows],
        near[9:9 + rows],
        jnp.where(lane == 0, 0.0, pltpu.roll(own, 1, 1)),
        jnp.where(lane == nz - 1, 0.0, pltpu.roll(own, nz - 1, 1)),
    )
    for which, other in enumerate(beside):
        coef[1 + which] = 0.5 * (own + other)
    coef[5] = own
    plane_rows(coef, center, partial)


def plane_rows(coef, center, partial):
    columns, nz = center.shape[1:]
    lane = lax.broadcasted_iota(jnp.int32, (columns, nz), 1)
    first, last = lane == 0, lane == nz - 1
    for y in range(partial.shape[0]):
        face = [jnp.broadcast_to(coef[k, y:y + 1, :], (columns, nz)) for k in range(5)]
        v = center[y + 1].astype(F32)
        total = face[0] * v
        total += face[1] * (v - center[y].astype(F32))
        total += face[2] * (v - center[y + 2].astype(F32))
        total += face[3] * (v - jnp.where(first, 0.0, pltpu.roll(v, 1, 1)))
        total += face[4] * (v - jnp.where(last, 0.0, pltpu.roll(v, nz - 1, 1)))
        partial[y] = total


def image_row(faces, y, partial, v, one, two):
    columns, nz = v.shape
    face = [jnp.broadcast_to(faces[k, y:y + 1, :], (columns, nz)) for k in range(2)]
    v = v.astype(F32)
    total = partial + face[0] * (v - one.astype(F32))
    return (total + face[1] * (v - two.astype(F32))).astype(BF16)


def gram_of(left, right):
    return lax.dot_general(left, right, (((1,), (1,)), ((), ())), preferred_element_type=F32)


def near_kernel(coef, partial, center, one, two, mine, theirs, faces, flat):
    rows, _, nz = partial.shape
    half = rows // CORES
    core = lax.axis_index("blk") % CORES
    for which, ref in enumerate((one, two)):
        faces[which] = 0.5 * (coef[5] + ref[rows].astype(F32)[:rows])
    for y in range(rows):
        image = image_row(faces, y, partial[y], center[y], one[y], two[y])
        flat[:, y * nz:(y + 1) * nz] = image

        @pl.when(core == y // half)
        def _():
            mine[y % half] = image

        @pl.when(core != y // half)
        def _():
            theirs[y % half] = image


def gather_kernel(chips, coef, *refs):
    count = chips - 1
    firsts, seconds, centers, partials = (refs[i * count:(i + 1) * count] for i in range(4))
    for first, second, center, partial in zip(firsts, seconds, centers, partials):
        half = first.shape[0]
        center[0:half] = first[...]
        center[half:2 * half] = second[...]
        plane_rows(coef, center, partial)


def first_far_kernel(chips, faces, *refs):
    count = chips - 1
    partials, centers, twos, ones, images, flats = (refs[i * count:(i + 1) * count] for i in range(6))
    nz = partials[0].shape[2]
    for k in range(count):
        for y in range(partials[k].shape[0] // 2):
            image = image_row(faces, y, partials[k][y], centers[k][y + 1], ones[k][y + 1], twos[k][y + 1])
            flats[k][:, y * nz:(y + 1) * nz] = image
            images[k][y] = image


def left_kernel(chips, weight, flat, center, plain, *refs):
    count = chips - 1
    flats, centers, other_firsts, other_seconds = (refs[i * count:(i + 1) * count] for i in range(4))
    left, gram = refs[4 * count:]
    columns, nz = center.shape[1:]
    half = other_firsts[0].shape[0]
    rows = 2 * half
    me = lax.axis_index("blk")
    for k, ref in enumerate((center, *centers)):
        for core in range(CORES):
            where = pl.ds(pl.multiple_of((me ^ (CORES * k + core)) * columns, columns), columns)
            for y in range(rows):
                if not k:
                    side = (plain if core else center)[y]
                elif not core:
                    side = ref[y + 1]
                else:
                    side = other_firsts[k - 1][y] if y < half else other_seconds[k - 1][y - half]
                left[where, y * nz:(y + 1) * nz] = side
    gram[:, 0:columns] = weight * gram_of(left[...], flat[...])
    for k in range(count):
        gram[:, (k + 1) * columns:(k + 2) * columns] = weight * gram_of(left[:, 0:half * nz], flats[k][...])


def second_far_kernel(chips, weight, faces, left, first_gram, *refs):
    count = chips - 1
    partials, centers, twos, ones, images, mine, theirs = (refs[i * count:(i + 1) * count] for i in range(7))
    gram, flat = refs[7 * count:]
    rows, columns, nz = partials[0].shape
    half = rows // 2
    core = lax.axis_index("blk") % CORES
    gram[:, 0:columns] = first_gram[:, 0:columns]
    for k in range(count):
        for i in range(half):
            y = half + i
            image = image_row(faces, y, partials[k][y], centers[k][y + 1], ones[k][i], twos[k][i])
            flat[:, i * nz:(i + 1) * nz] = image
            other = images[k][i]
            mine[k][i] = jnp.where(core == 0, other, image)
            theirs[k][i] = jnp.where(core == 0, image, other)
        block = slice((k + 1) * columns, (k + 2) * columns)
        gram[:, block] = first_gram[:, block] + weight * gram_of(left[:, half * nz:], flat[...])


def turn_out(image, start, applied, wide, turned, sem):
    rows, columns, _ = image.shape
    for y in range(rows):
        wide[pl.ds(y, columns, stride=rows), :] = image[y].astype(F32)
    for c in range(columns):
        turned[c, 0] = wide[c * rows:(c + 1) * rows, :].astype(BF16)
    copy = pltpu.make_async_copy(turned, applied.at[pl.ds(start, columns)], sem)
    copy.start()
    return copy


def first_kernel(mine, theirs, applied, wide, turned, sems):
    me = lax.axis_index("blk")
    columns = mine.shape[1]
    copies = [
        turn_out(image, (me ^ s) * columns, applied, wide.at[s], turned.at[s], sems.at[s])
        for s, image in enumerate((mine, theirs))
    ]
    for copy in copies:
        copy.wait()


def last_kernel(blocks, applied_in, *refs):
    del applied_in
    images, (applied, wide, turned, sems) = refs[:blocks - CORES], refs[blocks - CORES:]
    me = lax.axis_index("blk")
    columns = images[0].shape[1]
    copies = [
        turn_out(image, (me ^ (s + CORES)) * columns, applied, wide.at[s], turned.at[s], sems.at[s])
        for s, image in enumerate(images)
    ]
    for copy in copies:
        copy.wait()


def sum_kernel(slabs, blocks, shares, reduced):
    chips = blocks // CORES
    columns = shares.shape[2] // chips
    for core in range(CORES):
        sums = []
        for chip in range(chips):
            total = shares[CORES * chip + core]
            for slab in range(1, slabs):
                total += shares[slab * blocks + CORES * chip + core]
            sums.append(total)
        for target in range(chips):
            parts = [sums[chip][:, (chip ^ target) * columns:((chip ^ target) + 1) * columns] for chip in range(chips)]
            start = (CORES * target + core) * columns
            reduced[:, start:start + columns] = functools.reduce(jnp.add, parts)


def per_device(basis, zone, cond_table, heat_table):
    blocks = lax.axis_size("blk")
    slabs = lax.axis_size("dom")
    chips = blocks // CORES
    count = chips - 1
    columns, planes, ny, nz = basis.shape
    rows = ny // chips
    half = ny // blocks
    total = columns * blocks
    weight = 1.0 / (slabs * planes * ny * nz)
    image = jax.ShapeDtypeStruct((half, columns, nz), BF16)
    center_shape = jax.ShapeDtypeStruct((rows + 2, columns, nz), BF16)
    partial = jax.ShapeDtypeStruct((rows, columns, nz), F32)
    whole = jax.ShapeDtypeStruct((total, 1, half, nz), BF16)
    params = pltpu.CompilerParams(vmem_limit_bytes=32 << 20)
    costly = pl.CostEstimate(flops=COST, bytes_accessed=COST // 8, transcendentals=0)
    cheap = pl.CostEstimate(flops=1, bytes_accessed=1, transcendentals=0)

    def call(kernel, out_shape, inputs, scratch=(), specs=None, out_specs=None, cost=cheap, aliases={}):
        return pl.pallas_call(
            kernel,
            out_shape=out_shape,
            in_specs=specs or [VMEM] * len(inputs),
            out_specs=out_specs or [VMEM] * len(out_shape),
            scratch_shapes=scratch,
            input_output_aliases=aliases,
            compiler_params=params,
            cost_estimate=cost,
        )(*inputs)

    def after(value, *others):
        return lax.optimization_barrier((value, *others))[0]

    def swap(array, s):
        return lax.ppermute(array, "blk", [(i, i ^ s) for i in range(blocks)])

    def exchange(array, offset):
        partner = [((d + offset) ^ 1) - offset for d in range(slabs)]
        return lax.ppermute(array, "dom", [(d, to) for d, to in enumerate(partner) if 0 <= to < slabs])

    def turning(n):
        return [
            pltpu.VMEM((n, columns * half, nz), F32),
            pltpu.VMEM((n, columns, 1, half, nz), BF16),
            pltpu.SemaphoreType.DMA((n,)),
        ]

    sent, outer, firsts, seconds = prepare(basis, zone, cond_table, chips)
    two = exchange(sent, 1)
    one = exchange(sent, 0)
    firsts = [swap(array, CORES * (k + 1)) for k, array in enumerate(firsts)]
    coef, near_partial = call(
        functools.partial(plane_kernel, chips),
        (jax.ShapeDtypeStruct((6, rows, nz), F32), partial),
        (zone, cond_table, heat_table, sent, outer),
        [pltpu.VMEM((ny + 16, nz), F32), pltpu.VMEM((rows + 2, columns, nz), BF16)],
        [VMEM, SMEM, SMEM, VMEM, VMEM],
        cost=costly,
    )
    seconds = [swap(after(array, coef), CORES * (k + 1)) for k, array in enumerate(seconds)]
    firsts = [after(array, coef) for array in firsts]
    first_two = [exchange(array, 1) for array in firsts]
    first_one = [exchange(array, 0) for array in firsts]
    second_two = [exchange(array, 1) for array in seconds]
    second_one = [exchange(array, 0) for array in seconds]
    near_mine, near_theirs, faces, near_flat = call(
        near_kernel,
        (
            image,
            image,
            jax.ShapeDtypeStruct((2, rows, nz), F32),
            jax.ShapeDtypeStruct((columns, rows * nz), BF16),
        ),
        (coef, near_partial, sent, one, two),
    )
    results = call(
        functools.partial(gather_kernel, chips), [center_shape] * count + [partial] * count, (coef, *firsts, *seconds)
    )
    centers, partials = results[:count], results[count:]
    plain = swap(after(sent, one, two), 1)
    other_firsts = [swap(after(array, one, two)[1:], 1) for array in firsts]
    other_seconds = [swap(after(array, one, two)[:-1], 1) for array in seconds]
    half_flat = jax.ShapeDtypeStruct((columns, rows * nz // 2), BF16)
    results = call(
        functools.partial(first_far_kernel, chips),
        [image] * count + [half_flat] * count,
        (faces, *partials, *centers, *first_two, *first_one),
    )
    images, flats = results[:count], results[count:]
    applied, = call(
        first_kernel, (whole,), (near_mine, swap(near_theirs, 1)), turning(CORES), out_specs=[ANY]
    )
    gram_shape = jax.ShapeDtypeStruct((total, chips * columns), F32)
    left, first_gram = call(
        functools.partial(left_kernel, chips, weight),
        (jax.ShapeDtypeStruct((total, rows * nz), BF16), gram_shape),
        (near_flat, sent, plain, *flats, *centers, *other_firsts, *other_seconds),
    )
    *images, gram = call(
        functools.partial(second_far_kernel, chips, weight),
        [image] * (2 * count) + [gram_shape],
        (faces, left, first_gram, *partials, *centers, *second_two, *second_one, *images),
        [pltpu.VMEM((columns, rows * nz // 2), BF16)],
    )
    parts = slabs * blocks
    shares = gram.reshape(parts, total // parts, chips * columns)
    shares = lax.all_to_all(shares, ("dom", "blk"), split_axis=0, concat_axis=0, tiled=True)
    pieces = []
    for k in range(count):
        pieces += [images[k], swap(images[count + k], 1)]
    applied, = call(
        functools.partial(last_kernel, blocks),
        (whole,),
        (applied, *pieces),
        turning(len(pieces)),
        [ANY] + [VMEM] * len(pieces),
        [ANY],
        aliases={0: 0},
    )
    reduced, = call(
        functools.partial(sum_kernel, slabs, blocks), (jax.ShapeDtypeStruct((total // parts, total), F32),), (after(shares, applied),)
    )
    return applied, reduced


def solution(mesh):
    placed = (P("blk", "dom", "roll", None), P("dom", "roll", None), P(), P())
    return jax.shard_map(
        per_device,
        mesh=mesh,
        in_specs=placed,
        out_specs=(P("roll", "dom", "blk", None), P(("dom", "blk"), "roll")),
        check_vma=False,
    )
```

```python
import functools

import jax
import jax.numpy as jnp
from jax import lax
from jax.experimental import pallas as pl
from jax.experimental.pallas import tpu as pltpu
from jax.sharding import PartitionSpec as P

ZONES = 16
CORES = 2
COST = 1 << 30
F32 = jnp.float32
BF16 = jnp.bfloat16
VMEM = pl.BlockSpec(memory_space=pltpu.VMEM)
SMEM = pl.BlockSpec(memory_space=pltpu.SMEM)
HBM = pl.BlockSpec(memory_space=pltpu.HBM)
ANY = pl.BlockSpec(memory_space=pl.ANY)


def lookup(zone, table_ref):
    result = jnp.zeros(zone.shape, F32)
    for which in range(ZONES):
        result = jnp.where(zone == which, table_ref[which], result)
    return result


def cond_of(zone, table_ref):
    return lookup(zone, table_ref).astype(BF16).astype(F32)


def halves():
    return lax.axis_index("dom") % 2


def prepare_kernel(chips, basis_hbm, zone_hbm, cond_hbm, *refs):
    near, center, firsts, seconds = refs[0], refs[1], refs[2:1 + chips], refs[1 + chips:2 * chips]
    basis, zone, table, wide, turned, cond_pad, in_sems, out_sems = refs[2 * chips:]
    columns, _, ny, nz = basis.shape
    rows = ny // chips
    part = rows // CORES // 2
    me = lax.axis_index("blk")
    chip, core, late = me // CORES, me % CORES, halves()
    step = 16
    chunks = columns // step
    loads = [
        pltpu.make_async_copy(basis_hbm.at[pl.ds(i * step, step)], basis.at[pl.ds(i * step, step)], in_sems.at[i])
        for i in range(chunks)
    ]
    loads.append(pltpu.make_async_copy(zone_hbm, zone, in_sems.at[chunks]))
    loads.append(pltpu.make_async_copy(cond_hbm, table, in_sems.at[chunks + 1]))
    for load in loads:
        load.start()
    turned[0] = jnp.zeros((columns, nz), BF16)
    turned[ny + 1] = jnp.zeros((columns, nz), BF16)
    stores = []

    def store(source, target):
        copy = pltpu.make_async_copy(source, target, out_sems.at[len(stores)])
        copy.start()
        stores.append(copy)

    loads[chunks].wait()
    loads[chunks + 1].wait()
    mine = zone[0, pl.ds(pl.multiple_of(chip * rows, rows), rows), :]
    own = cond_of(mine, table)
    cond_pad[...] = jnp.concatenate([own, jnp.zeros((columns - rows, nz), F32)], 0).astype(BF16)
    store(cond_pad, near.at[CORES * part])
    for i in range(chunks):
        loads[i].wait()
        some = pl.ds(i * step, step)
        for c in range(i * step, (i + 1) * step):
            wide[c * ny:(c + 1) * ny, :] = basis[c, 0].astype(F32)
        for y in range(ny):
            turned[y + 1, some, :] = wide[pl.ds(i * step * ny + y, step, stride=ny), :].astype(BF16)
        for k in reversed(range(chips)):
            base = (chip ^ k) * rows + 1
            for owner in range(CORES):
                start = base + (2 * owner + 1 - late) * part
                target = firsts[k - 1] if k else near
                store(turned.at[pl.ds(start, part), some], target.at[pl.ds(owner * part, part), some])
            for other in range(CORES if k else 0):
                start = base + (2 * (core ^ other) + late) * part
                store(turned.at[pl.ds(start, part), some], seconds[k - 1].at[pl.ds(other * part, part), some])
        store(turned.at[pl.ds(chip * rows, rows + 2), some], center.at[:, some])
    for k in range(1, chips):
        base = (chip ^ k) * rows
        store(turned.at[pl.ds(base, 1)], firsts[k - 1].at[pl.ds(CORES * part, 1)])
        store(turned.at[pl.ds(base + rows + 1, 1)], firsts[k - 1].at[pl.ds(CORES * part + 1, 1)])
    for copy in stores:
        copy.wait()


def prepare(basis, zone, cond_table, chips):
    columns, _, ny, nz = basis.shape
    rows = ny // chips
    slabs = [rows // 2 + 1, rows + 2] + [rows // 2 + 2] * (chips - 1) + [rows // 2] * (chips - 1)
    stores = 1 + (1 + CORES * (2 * chips - 1)) * (columns // 16) + 2 * (chips - 1)
    results = pl.pallas_call(
        functools.partial(prepare_kernel, chips),
        out_shape=[jax.ShapeDtypeStruct((n, columns, nz), BF16) for n in slabs],
        in_specs=[HBM, HBM, HBM],
        out_specs=[ANY] * len(slabs),
        scratch_shapes=[
            pltpu.VMEM(basis.shape, BF16),
            pltpu.VMEM(zone.shape, jnp.int32),
            pltpu.SMEM((ZONES,), F32),
            pltpu.VMEM((columns * ny, nz), F32),
            pltpu.VMEM((ny + 2, columns, nz), BF16),
            pltpu.VMEM((columns, nz), BF16),
            pltpu.SemaphoreType.DMA((columns // 16 + 2,)),
            pltpu.SemaphoreType.DMA((stores,)),
        ],
        compiler_params=pltpu.CompilerParams(vmem_limit_bytes=16 << 20),
    )(*[pltpu.with_memory_space_constraint(x, pltpu.HBM) for x in (basis, zone, cond_table)])
    return (*results[:2], results[2:1 + chips], results[1 + chips:])


def plane_kernel(chips, zone_ref, cond_ref, heat_ref, center, other, coef, partial, other_partial, late_rows, cond_pad):
    rows = partial.shape[0]
    nz = center.shape[2]
    ny = zone_ref.shape[1]
    chip = lax.axis_index("blk") // CORES
    cond_pad[0:8, :] = jnp.zeros((8, nz), F32)
    cond_pad[8:8 + ny, :] = cond_of(zone_ref[0], cond_ref)
    cond_pad[8 + ny:16 + ny, :] = jnp.zeros((8, nz), F32)
    base = pl.multiple_of(chip * rows, 8)
    near = cond_pad[pl.ds(base, rows + 16), :]
    own = near[8:8 + rows]
    lane = lax.broadcasted_iota(jnp.int32, (rows, nz), 1)
    coef[0] = lookup(zone_ref[0, pl.ds(base, rows), :], heat_ref)
    beside = (
        near[7:7 + rows],
        near[9:9 + rows],
        jnp.where(lane == 0, 0.0, pltpu.roll(own, 1, 1)),
        jnp.where(lane == nz - 1, 0.0, pltpu.roll(own, nz - 1, 1)),
    )
    for which, node in enumerate(beside):
        coef[1 + which] = 0.5 * (own + node)
    coef[5] = own
    plane_rows(coef, center, partial)
    core, late = lax.axis_index("blk") % CORES, halves()
    part = rows // CORES // 2
    plane_rows(coef, other, other_partial, (2 * core + 1 - late) * part)
    for which, ref in enumerate((center, other)):
        for i in range(part):
            late_rows[which * part + i] = ref[(2 * core + late) * part + i + 1]


def plane_rows(coef, center, partial, first=0):
    columns, nz = center.shape[1:]
    lane = lax.broadcasted_iota(jnp.int32, (columns, nz), 1)
    left_end, right_end = lane == 0, lane == nz - 1
    for i in range(partial.shape[0]):
        y = first + i
        face = [spread(coef, k, y, columns) for k in range(5)]
        v = center[y + 1].astype(F32)
        total = face[0] * v
        total += face[1] * (v - center[y].astype(F32))
        total += face[2] * (v - center[y + 2].astype(F32))
        total += face[3] * (v - jnp.where(left_end, 0.0, pltpu.roll(v, 1, 1)))
        total += face[4] * (v - jnp.where(right_end, 0.0, pltpu.roll(v, nz - 1, 1)))
        partial[i] = total


def spread(coef, k, y, columns):
    return jnp.broadcast_to(coef[k, pl.ds(y, 1), :], (columns, coef.shape[2]))


def with_dom(faces, y, v, partial, one, two):
    total = partial + spread(faces, 0, y, v.shape[0]) * (v - one)
    return total + spread(faces, 1, y, v.shape[0]) * (v - two)


def place(y, part, late):
    core, half = y // (2 * part), y // part % 2
    return ((half ^ late) * CORES + core) * part + y % part


def gram_of(left, right):
    return lax.dot_general(left, right, (((1,), (1,)), ((), ())), preferred_element_type=F32)


def early_rows(faces, partial, center, one, two, mine, theirs, store):
    columns = center.shape[1]
    part = partial.shape[0] // CORES // 2
    core, late = lax.axis_index("blk") % CORES, halves()
    for c in range(CORES):
        for i in range(part):
            y, at = (2 * c + late) * part + i, c * part + i
            v, p = center[y + 1].astype(F32), partial[y]
            a, b = one[at].astype(F32), two[at].astype(F32)
            share = 0.5 * p + spread(faces, 2, y, columns) * v
            share -= spread(faces, 0, y, columns) * a
            share -= spread(faces, 1, y, columns) * b
            store(at, share.astype(BF16))
            image = with_dom(faces, y, v, p, a, b).astype(BF16)

            @pl.when(core == c)
            def _():
                mine[i] = image

            @pl.when(core != c)
            def _():
                theirs[i] = image


def late_rows_of(faces, partial, center, store):
    columns = center.shape[1]
    part = partial.shape[0] // CORES // 2
    late = halves()
    for c in range(CORES):
        for i in range(part):
            y = (2 * c + 1 - late) * part + i
            share = 0.5 * partial[y] + spread(faces, 2, y, columns) * center[y + 1].astype(F32)
            store(c * part + i, share.astype(BF16))


def near_kernel(coef, partial, center, one, two, mine, theirs, faces, flat):
    rows, _, nz = partial.shape
    for k, ref in enumerate((one, two)):
        faces[k] = 0.5 * (coef[5] + ref[rows // 2].astype(F32)[:rows])
    faces[2] = 0.5 * (faces[0] + faces[1])

    def store(first):
        def put(at, share):
            flat[:, (first + at) * nz:(first + at + 1) * nz] = share
        return put

    early_rows(faces, partial, center, one, two, mine, theirs, store(0))
    late_rows_of(faces, partial, center, store(rows // 2))


def gather(first, outer, second, core, center):
    part = second.shape[0] // CORES
    late = halves()
    for i in range(part):
        for c in range(CORES):
            center[1 + (2 * c + 1 - late) * part + i] = first[c * part + i]
            center[1 + (2 * (core ^ c) + late) * part + i] = second[c * part + i]
    center[0] = outer[0]
    center[2 * CORES * part + 1] = outer[1]


def gather_kernel(chips, coef, *refs):
    count = chips - 1
    firsts, seconds, other_firsts, outers, other_seconds = (refs[i * count:(i + 1) * count] for i in range(5))
    centers, partials, other_centers, other_partials = (refs[i * count:(i + 1) * count] for i in range(5, 9))
    core, late = lax.axis_index("blk") % CORES, halves()
    for k in range(count):
        halo = seconds[k].shape[0]
        gather(firsts[k], firsts[k].at[pl.ds(halo, 2)], seconds[k], core, centers[k])
        gather(other_firsts[k], outers[k], other_seconds[k], 1 - core, other_centers[k])
        plane_rows(coef, centers[k], partials[k])
        plane_rows(coef, other_centers[k], other_partials[k], (2 * core + 1 - late) * (halo // CORES))


def left_kernel(chips, faces, flat, *refs):
    count = chips - 1
    centers, others, partials = refs[:chips], refs[chips:2 * chips], refs[2 * chips:2 * chips + count]
    left, tall, flatter, right = refs[2 * chips + count:]
    rows, columns, nz = partials[0].shape
    part = rows // CORES // 2
    late = halves()
    for y in range(rows):
        where = pl.ds(pl.multiple_of(place(y, part, late) * nz, nz), nz)
        for i, ref in enumerate((*centers, *others)):
            left[i * columns:(i + 1) * columns, where] = ref[y + 1]
    late_half = pl.ds(rows * nz // 2, rows * nz // 2)
    tall[:, 0:columns] = gram_of(left[...], flat[...])
    flatter[0:columns, :] = gram_of(flat[...], left[...])
    for k in range(count):
        def put(at, share):
            right[:, at * nz:(at + 1) * nz] = share

        late_rows_of(faces, partials[k], centers[k + 1], put)
        block = slice((k + 1) * columns, (k + 2) * columns)
        tall[:, block] = gram_of(left[:, late_half], right[...])
        flatter[block, :] = gram_of(right[...], left[:, late_half])


def gram_kernel(chips, weight, faces, left, tall, flatter, *refs):
    count = chips - 1
    partials, centers, twos, ones, mine, theirs = (refs[i * count:(i + 1) * count] for i in range(6))
    gram, right, rest = refs[6 * count:]
    rows, columns, nz = partials[0].shape
    me = lax.axis_index("blk")
    early_half = pl.ds(0, rows * nz // 2)
    rest[...] = jnp.zeros_like(rest)
    for k in range(count):
        def put(at, share):
            right[:, at * nz:(at + 1) * nz] = share

        early_rows(faces, partials[k], centers[k], ones[k], twos[k], mine[k], theirs[k], put)
        block = slice((k + 1) * columns, (k + 2) * columns)
        rest[:, block] = gram_of(left[:, early_half], right[...])
        flatter[block, :] += gram_of(right[...], left[:, early_half])
    for i in range(chips * CORES):
        partner = CORES * (i % chips) + i // chips
        where = pl.ds(pl.multiple_of((me ^ partner) * columns, columns), columns)
        block = slice(i * columns, (i + 1) * columns)
        near = weight * (tall[block, :] + rest[block, :])
        far = jnp.zeros((columns, chips * columns), F32)
        share = jnp.concatenate([near, far], 1)
        if i < chips:
            share += weight * flatter[block, :]
        gram[where, :] = share


def late_kernel(chips, faces, two, one, *refs):
    blocks = chips * CORES
    done, partials, centers = (refs[i * blocks:(i + 1) * blocks] for i in range(3))
    applied, wide, turned, sems = refs[3 * blocks:]
    part, columns, _ = done[0].shape
    half = CORES * part
    me = lax.axis_index("blk")
    core, late = me % CORES, halves()
    first = (2 * core + 1 - late) * part
    copies = []
    for s in range(blocks):
        scratch = wide.at[s]
        for i in range(part):
            y = first + i
            at = (CORES * (s % chips) + s // chips) * part + i
            p = partials[s][y] if s < chips else partials[s][i]
            v, a, b = (x.astype(F32) for x in (centers[s][y + 1], one[at], two[at]))
            image = with_dom(faces, y, v, p, a, b).astype(BF16).astype(F32)
            scratch[pl.ds((1 - late) * part + i, columns, stride=half), :] = image
            scratch[pl.ds(late * part + i, columns, stride=half), :] = done[s][i].astype(F32)
        for c in range(columns):
            turned[s, c, 0] = scratch[c * half:(c + 1) * half, :].astype(BF16)
        partner = CORES * (s % chips) + s // chips
        copy = pltpu.make_async_copy(turned.at[s], applied.at[pl.ds((me ^ partner) * columns, columns)], sems.at[s])
        copy.start()
        copies.append(copy)
    for copy in copies:
        copy.wait()


def sum_kernel(slabs, blocks, shares, reduced):
    chips = blocks // CORES
    columns = shares.shape[2] // blocks
    sums = []
    for sender in range(blocks):
        total = shares[sender]
        for slab in range(1, slabs):
            total += shares[slab * blocks + sender]
        sums.append(total)
    for target in range(blocks):
        parts = []
        for sender in range(blocks):
            partner = sender ^ target
            i = partner % CORES * chips + partner // CORES
            parts.append(sums[sender][:, i * columns:(i + 1) * columns])
        reduced[:, target * columns:(target + 1) * columns] = functools.reduce(jnp.add, parts)


def per_device(basis, zone, cond_table, heat_table):
    blocks = lax.axis_size("blk")
    slabs = lax.axis_size("dom")
    chips = blocks // CORES
    count = chips - 1
    columns, planes, ny, nz = basis.shape
    rows = ny // chips
    half = ny // blocks
    part = half // 2
    total = columns * blocks
    weight = 1.0 / (slabs * planes * ny * nz)
    image = jax.ShapeDtypeStruct((half, columns, nz), BF16)
    half_image = jax.ShapeDtypeStruct((part, columns, nz), BF16)
    center_shape = jax.ShapeDtypeStruct((rows + 2, columns, nz), BF16)
    partial = jax.ShapeDtypeStruct((rows, columns, nz), F32)
    whole = jax.ShapeDtypeStruct((total, 1, half, nz), BF16)
    params = pltpu.CompilerParams(vmem_limit_bytes=32 << 20)
    costly = pl.CostEstimate(flops=COST, bytes_accessed=COST // 8, transcendentals=0)
    cheap = pl.CostEstimate(flops=1, bytes_accessed=1, transcendentals=0)

    def call(kernel, out_shape, inputs, scratch=(), specs=None, out_specs=None, cost=cheap, aliases={}):
        return pl.pallas_call(
            kernel,
            out_shape=out_shape,
            in_specs=specs or [VMEM] * len(inputs),
            out_specs=out_specs or [VMEM] * len(out_shape),
            scratch_shapes=scratch,
            input_output_aliases=aliases,
            compiler_params=params,
            cost_estimate=cost,
        )(*inputs)

    def after(value, *others):
        return lax.optimization_barrier((value, *others))[0]

    def swap(array, s):
        return lax.ppermute(array, "blk", [(i, i ^ s) for i in range(blocks)])

    def exchange(array, offset, s=0):
        partner = [((d + offset) ^ 1) - offset for d in range(slabs)]
        pairs = [
            (d * blocks + b, to * blocks + (b ^ s))
            for d, to in enumerate(partner) if 0 <= to < slabs for b in range(blocks)
        ]
        return lax.ppermute(array, ("dom", "blk"), pairs)

    near, center, firsts, seconds = prepare(basis, zone, cond_table, chips)
    other = swap(center, 1)
    firsts = [swap(array, CORES * (k + 1)) for k, array in enumerate(firsts)]
    two = exchange(near, 1)
    one = exchange(near, 0)
    coef, near_partial, other_partial, late_near = call(
        functools.partial(plane_kernel, chips),
        (
            jax.ShapeDtypeStruct((6, rows, nz), F32),
            partial,
            jax.ShapeDtypeStruct((part, columns, nz), F32),
            image,
        ),
        (zone, cond_table, heat_table, center, other),
        [pltpu.VMEM((ny + 16, nz), F32)],
        [VMEM, SMEM, SMEM, VMEM, VMEM],
        cost=costly,
    )
    seconds = [swap(array, CORES * (k + 1)) for k, array in enumerate(seconds)]
    firsts = [after(array, coef, one) for array in firsts]
    early_two = [exchange(array, 1) for array in firsts]
    early_one = [exchange(array, 0) for array in firsts]
    other_firsts = [swap(after(array, two)[:half], 1) for array in firsts]
    outers = [swap(after(array, two)[half:], 1) for array in firsts]
    other_seconds = [swap(after(array, coef), 1) for array in seconds]
    late = [late_near]
    for mine, theirs in zip(seconds, other_seconds):
        late += [mine[:part], theirs[part:]]
    late = jnp.concatenate(late)
    late_two, late_one = exchange(late, 1), exchange(late, 0)

    near_mine, near_theirs, faces, near_flat = call(
        near_kernel,
        (
            half_image,
            half_image,
            jax.ShapeDtypeStruct((3, rows, nz), F32),
            jax.ShapeDtypeStruct((columns, rows * nz), BF16),
        ),
        (coef, near_partial, center, one, two),
    )
    results = call(
        functools.partial(gather_kernel, chips),
        [center_shape] * count + [partial] * count + [center_shape] * count
        + [jax.ShapeDtypeStruct((part, columns, nz), F32)] * count,
        (after(coef, faces), *firsts, *seconds, *other_firsts, *outers, *other_seconds),
    )
    centers, partials, other_centers, other_partials = (results[i * count:(i + 1) * count] for i in range(4))
    left, tall, flatter = call(
        functools.partial(left_kernel, chips),
        (
            jax.ShapeDtypeStruct((total, rows * nz), BF16),
            jax.ShapeDtypeStruct((total, chips * columns), F32),
            jax.ShapeDtypeStruct((chips * columns, total), F32),
        ),
        (faces, near_flat, center, *centers, other, *other_centers, *partials),
        [pltpu.VMEM((columns, rows * nz // 2), BF16)],
    )
    *images, gram = call(
        functools.partial(gram_kernel, chips, weight),
        [half_image] * (2 * count) + [jax.ShapeDtypeStruct((total, total), F32)],
        (faces, left, tall, flatter, *partials, *centers, *early_two, *early_one),
        [pltpu.VMEM((columns, rows * nz // 2), BF16), pltpu.VMEM((total, chips * columns), F32)],
    )
    parts = slabs * blocks
    shares = gram.reshape(parts, total // parts, total)
    shares = lax.all_to_all(shares, ("dom", "blk"), split_axis=0, concat_axis=0, tiled=True)
    done = [near_mine, *images[:count], *(swap(array, 1) for array in (near_theirs, *images[count:]))]
    pieces = (
        late_two, late_one, *done, near_partial, *partials, other_partial, *other_partials,
        center, *centers, other, *other_centers,
    )
    applied, = call(
        functools.partial(late_kernel, chips),
        (whole,),
        (faces, *pieces),
        [
            pltpu.VMEM((blocks, columns * half, nz), F32),
            pltpu.VMEM((blocks, columns, 1, half, nz), BF16),
            pltpu.SemaphoreType.DMA((blocks,)),
        ],
        out_specs=[ANY],
    )
    reduced, = call(
        functools.partial(sum_kernel, slabs, blocks), (jax.ShapeDtypeStruct((total // parts, total), F32),),
        (after(shares, applied),)
    )
    return applied, reduced


def solution(mesh):
    placed = (P("blk", "dom", "roll", None), P("dom", "roll", None), P(), P())
    return jax.shard_map(
        per_device,
        mesh=mesh,
        in_specs=placed,
        out_specs=(P("roll", "dom", "blk", None), P(("dom", "blk"), "roll")),
        check_vma=False,
    )
```

```python
import functools

import jax
import jax.numpy as jnp
from jax import lax
from jax.experimental import pallas as pl
from jax.experimental.pallas import tpu as pltpu
from jax.sharding import PartitionSpec as P

ZONES = 16
CORES = 2
COST = 1 << 30
F32 = jnp.float32
BF16 = jnp.bfloat16
VMEM = pl.BlockSpec(memory_space=pltpu.VMEM)
SMEM = pl.BlockSpec(memory_space=pltpu.SMEM)
HBM = pl.BlockSpec(memory_space=pltpu.HBM)
ANY = pl.BlockSpec(memory_space=pl.ANY)


def lookup(zone, table_ref):
    result = jnp.zeros(zone.shape, F32)
    for which in range(ZONES):
        result = jnp.where(zone == which, table_ref[which], result)
    return result


def cond_of(zone, table_ref):
    return lookup(zone, table_ref).astype(BF16).astype(F32)


def halves():
    return lax.axis_index("dom") % 2


def prepare_kernel(chips, basis_hbm, zone_hbm, cond_hbm, *refs):
    near, center, firsts, seconds = refs[0], refs[1], refs[2:1 + chips], refs[1 + chips:2 * chips]
    basis, zone, table, wide, turned, cond_pad, in_sems, out_sems = refs[2 * chips:]
    columns, _, ny, nz = basis.shape
    rows = ny // chips
    part = rows // CORES // 2
    me = lax.axis_index("blk")
    chip, core, late = me // CORES, me % CORES, halves()
    step = 16
    chunks = columns // step
    loads = [
        pltpu.make_async_copy(basis_hbm.at[pl.ds(i * step, step)], basis.at[pl.ds(i * step, step)], in_sems.at[i])
        for i in range(chunks)
    ]
    loads.append(pltpu.make_async_copy(zone_hbm, zone, in_sems.at[chunks]))
    loads.append(pltpu.make_async_copy(cond_hbm, table, in_sems.at[chunks + 1]))
    for load in loads:
        load.start()
    turned[0] = jnp.zeros((columns, nz), BF16)
    turned[ny + 1] = jnp.zeros((columns, nz), BF16)
    stores = []

    def store(source, target):
        copy = pltpu.make_async_copy(source, target, out_sems.at[len(stores)])
        copy.start()
        stores.append(copy)

    loads[chunks].wait()
    loads[chunks + 1].wait()
    mine = zone[0, pl.ds(pl.multiple_of(chip * rows, rows), rows), :]
    own = cond_of(mine, table)
    cond_pad[...] = jnp.concatenate([own, jnp.zeros((columns - rows, nz), F32)], 0).astype(BF16)
    store(cond_pad, near.at[CORES * part])
    for i in range(chunks):
        loads[i].wait()
        some = pl.ds(i * step, step)
        for c in range(i * step, (i + 1) * step):
            wide[c * ny:(c + 1) * ny, :] = basis[c, 0].astype(F32)
        for y in range(ny):
            turned[y + 1, some, :] = wide[pl.ds(i * step * ny + y, step, stride=ny), :].astype(BF16)
        for k in reversed(range(chips)):
            base = (chip ^ k) * rows + 1
            for owner in range(CORES):
                start = base + (2 * owner + 1 - late) * part
                target = firsts[k - 1] if k else near
                store(turned.at[pl.ds(start, part), some], target.at[pl.ds(owner * part, part), some])
            for other in range(CORES if k else 0):
                start = base + (2 * (core ^ other) + late) * part
                store(turned.at[pl.ds(start, part), some], seconds[k - 1].at[pl.ds(other * part, part), some])
        store(turned.at[pl.ds(chip * rows, rows + 2), some], center.at[:, some])
    for k in range(1, chips):
        base = (chip ^ k) * rows
        store(turned.at[pl.ds(base, 1)], firsts[k - 1].at[pl.ds(CORES * part, 1)])
        store(turned.at[pl.ds(base + rows + 1, 1)], firsts[k - 1].at[pl.ds(CORES * part + 1, 1)])
    for copy in stores:
        copy.wait()


def prepare(basis, zone, cond_table, chips):
    columns, _, ny, nz = basis.shape
    rows = ny // chips
    slabs = [rows // 2 + 1, rows + 2] + [rows // 2 + 2] * (chips - 1) + [rows // 2] * (chips - 1)
    stores = 1 + (1 + CORES * (2 * chips - 1)) * (columns // 16) + 2 * (chips - 1)
    results = pl.pallas_call(
        functools.partial(prepare_kernel, chips),
        out_shape=[jax.ShapeDtypeStruct((n, columns, nz), BF16) for n in slabs],
        in_specs=[HBM, HBM, HBM],
        out_specs=[ANY] * len(slabs),
        scratch_shapes=[
            pltpu.VMEM(basis.shape, BF16),
            pltpu.VMEM(zone.shape, jnp.int32),
            pltpu.SMEM((ZONES,), F32),
            pltpu.VMEM((columns * ny, nz), F32),
            pltpu.VMEM((ny + 2, columns, nz), BF16),
            pltpu.VMEM((columns, nz), BF16),
            pltpu.SemaphoreType.DMA((columns // 16 + 2,)),
            pltpu.SemaphoreType.DMA((stores,)),
        ],
        compiler_params=pltpu.CompilerParams(vmem_limit_bytes=16 << 20),
    )(*[pltpu.with_memory_space_constraint(x, pltpu.HBM) for x in (basis, zone, cond_table)])
    return (*results[:2], results[2:1 + chips], results[1 + chips:])


def plane_kernel(chips, zone_ref, cond_ref, heat_ref, center, coef, partial, late_rows, late_terms, cond_pad):
    rows = partial.shape[0]
    nz = center.shape[2]
    ny = zone_ref.shape[1]
    chip = lax.axis_index("blk") // CORES
    cond_pad[0:8, :] = jnp.zeros((8, nz), F32)
    cond_pad[8:8 + ny, :] = cond_of(zone_ref[0], cond_ref)
    cond_pad[8 + ny:16 + ny, :] = jnp.zeros((8, nz), F32)
    base = pl.multiple_of(chip * rows, 8)
    near = cond_pad[pl.ds(base, rows + 16), :]
    own = near[8:8 + rows]
    lane = lax.broadcasted_iota(jnp.int32, (rows, nz), 1)
    coef[0] = lookup(zone_ref[0, pl.ds(base, rows), :], heat_ref)
    beside = (
        near[7:7 + rows],
        near[9:9 + rows],
        jnp.where(lane == 0, 0.0, pltpu.roll(own, 1, 1)),
        jnp.where(lane == nz - 1, 0.0, pltpu.roll(own, nz - 1, 1)),
    )
    for which, node in enumerate(beside):
        coef[1 + which] = 0.5 * (own + node)
    coef[5] = own
    plane_rows(coef, center, partial)
    keep_late(center, partial, late_rows, late_terms)


def keep_late(center, partial, late_rows, late_terms):
    part = late_rows.shape[0]
    first = (2 * (lax.axis_index("blk") % CORES) + 1 - halves()) * part
    for i in range(part):
        late_rows[i] = center[first + i + 1]
        late_terms[i] = partial[first + i]


def plane_rows(coef, center, partial, first=0):
    columns, nz = center.shape[1:]
    lane = lax.broadcasted_iota(jnp.int32, (columns, nz), 1)
    left_end, right_end = lane == 0, lane == nz - 1
    for i in range(partial.shape[0]):
        y = first + i
        face = [spread(coef, k, y, columns) for k in range(5)]
        v = center[y + 1].astype(F32)
        total = face[0] * v
        total += face[1] * (v - center[y].astype(F32))
        total += face[2] * (v - center[y + 2].astype(F32))
        total += face[3] * (v - jnp.where(left_end, 0.0, pltpu.roll(v, 1, 1)))
        total += face[4] * (v - jnp.where(right_end, 0.0, pltpu.roll(v, nz - 1, 1)))
        partial[i] = total


def spread(coef, k, y, columns):
    return jnp.broadcast_to(coef[k, pl.ds(y, 1), :], (columns, coef.shape[2]))


def with_dom(faces, y, v, partial, one, two):
    total = partial + spread(faces, 0, y, v.shape[0]) * (v - one)
    return total + spread(faces, 1, y, v.shape[0]) * (v - two)


def place(y, part, late):
    core, half = y // (2 * part), y // part % 2
    return ((half ^ late) * CORES + core) * part + y % part


def gram_of(left, right):
    return lax.dot_general(left, right, (((1,), (1,)), ((), ())), preferred_element_type=F32)


def early_rows(faces, partial, center, one, two, mine, theirs, store):
    columns = center.shape[1]
    part = partial.shape[0] // CORES // 2
    core, late = lax.axis_index("blk") % CORES, halves()
    for c in range(CORES):
        for i in range(part):
            y, at = (2 * c + late) * part + i, c * part + i
            v, p = center[y + 1].astype(F32), partial[y]
            a, b = one[at].astype(F32), two[at].astype(F32)
            share = 0.5 * p + spread(faces, 2, y, columns) * v
            share -= spread(faces, 0, y, columns) * a
            share -= spread(faces, 1, y, columns) * b
            store(at, share.astype(BF16))
            image = with_dom(faces, y, v, p, a, b).astype(BF16)

            @pl.when(core == c)
            def _():
                mine[i] = image

            @pl.when(core != c)
            def _():
                theirs[i] = image


def late_rows_of(faces, partial, center, store):
    columns = center.shape[1]
    part = partial.shape[0] // CORES // 2
    late = halves()
    for c in range(CORES):
        for i in range(part):
            y = (2 * c + 1 - late) * part + i
            share = 0.5 * partial[y] + spread(faces, 2, y, columns) * center[y + 1].astype(F32)
            store(c * part + i, share.astype(BF16))


def near_kernel(coef, partial, center, one, two, mine, theirs, faces, flat):
    rows, _, nz = partial.shape
    for k, ref in enumerate((one, two)):
        faces[k] = 0.5 * (coef[5] + ref[rows // 2].astype(F32)[:rows])
    faces[2] = 0.5 * (faces[0] + faces[1])

    def store(first):
        def put(at, share):
            flat[:, (first + at) * nz:(first + at + 1) * nz] = share
        return put

    early_rows(faces, partial, center, one, two, mine, theirs, store(0))
    late_rows_of(faces, partial, center, store(rows // 2))


def gather(first, outer, second, core, center):
    part = second.shape[0] // CORES
    late = halves()
    for i in range(part):
        for c in range(CORES):
            center[1 + (2 * c + 1 - late) * part + i] = first[c * part + i]
            center[1 + (2 * (core ^ c) + late) * part + i] = second[c * part + i]
    center[0] = outer[0]
    center[2 * CORES * part + 1] = outer[1]


def gather_kernel(chips, coef, other, *refs):
    count = chips - 1
    firsts, seconds, other_firsts, outers, other_seconds = (refs[i * count:(i + 1) * count] for i in range(5))
    centers, partials, other_centers = (refs[i * count:(i + 1) * count] for i in range(5, 8))
    refs = refs[8 * count:]
    late_rows, late_terms = refs[:count + chips], refs[count + chips:]
    part = late_rows[0].shape[0]
    core, late = lax.axis_index("blk") % CORES, halves()
    first = (2 * core + 1 - late) * part
    for k in range(count):
        halo = seconds[k].shape[0]
        gather(firsts[k], firsts[k].at[pl.ds(halo, 2)], seconds[k], core, centers[k])
        gather(other_firsts[k], outers[k], other_seconds[k], 1 - core, other_centers[k])
        plane_rows(coef, centers[k], partials[k])
        keep_late(centers[k], partials[k], late_rows[k], late_terms[k])
    for k, center in enumerate((other, *other_centers)):
        plane_rows(coef, center, late_terms[count + k], first)
        for i in range(part):
            late_rows[count + k][i] = center[first + i + 1]


def pack_kernel(chips, center, other, *refs):
    count = chips - 1
    seconds, other_seconds, packed = refs[:count], refs[count:2 * count], refs[2 * count]
    part = packed.shape[0] // (CORES * chips)
    first = (2 * (lax.axis_index("blk") % CORES) + halves()) * part
    for i in range(part):
        packed[i] = center[first + i + 1]
        packed[part + i] = other[first + i + 1]
    for k in range(count):
        start = (k + 1) * CORES * part
        packed[start:start + part] = seconds[k][0:part]
        packed[start + part:start + 2 * part] = other_seconds[k][part:2 * part]


def left_kernel(chips, faces, flat, *refs):
    count = chips - 1
    centers, others, partials = refs[:chips], refs[chips:2 * chips], refs[2 * chips:2 * chips + count]
    left, tall, flatter, right = refs[2 * chips + count:]
    rows, columns, nz = partials[0].shape
    part = rows // CORES // 2
    late = halves()
    for y in range(rows):
        where = pl.ds(pl.multiple_of(place(y, part, late) * nz, nz), nz)
        for i, ref in enumerate((*centers, *others)):
            left[i * columns:(i + 1) * columns, where] = ref[y + 1]
    late_half = pl.ds(rows * nz // 2, rows * nz // 2)
    tall[:, 0:columns] = gram_of(left[...], flat[...])
    flatter[0:columns, :] = gram_of(flat[...], left[...])
    for k in range(count):
        def put(at, share):
            right[:, at * nz:(at + 1) * nz] = share

        late_rows_of(faces, partials[k], centers[k + 1], put)
        block = slice((k + 1) * columns, (k + 2) * columns)
        tall[:, block] = gram_of(left[:, late_half], right[...])
        flatter[block, :] = gram_of(right[...], left[:, late_half])


def gram_kernel(chips, weight, faces, left, tall, flatter, *refs):
    count = chips - 1
    partials, centers, twos, ones, mine, theirs = (refs[i * count:(i + 1) * count] for i in range(6))
    gram, right, rest = refs[6 * count:]
    rows, columns, nz = partials[0].shape
    me = lax.axis_index("blk")
    early_half = pl.ds(0, rows * nz // 2)
    rest[...] = jnp.zeros_like(rest)
    for k in range(count):
        def put(at, share):
            right[:, at * nz:(at + 1) * nz] = share

        early_rows(faces, partials[k], centers[k], ones[k], twos[k], mine[k], theirs[k], put)
        block = slice((k + 1) * columns, (k + 2) * columns)
        rest[:, block] = gram_of(left[:, early_half], right[...])
        flatter[block, :] += gram_of(right[...], left[:, early_half])
    for i in range(chips * CORES):
        partner = CORES * (i % chips) + i // chips
        where = pl.ds(pl.multiple_of((me ^ partner) * columns, columns), columns)
        block = slice(i * columns, (i + 1) * columns)
        near = weight * (tall[block, :] + rest[block, :])
        far = jnp.zeros((columns, chips * columns), F32)
        share = jnp.concatenate([near, far], 1)
        if i < chips:
            share += weight * flatter[block, :]
        gram[where, :] = share


def late_kernel(chips, faces, two, one, *refs):
    blocks = chips * CORES
    done, partials, centers = (refs[i * blocks:(i + 1) * blocks] for i in range(3))
    applied, wide, turned, sems = refs[3 * blocks:]
    part, columns, _ = done[0].shape
    half = CORES * part
    me = lax.axis_index("blk")
    core, late = me % CORES, halves()
    first = (2 * core + 1 - late) * part
    copies = []
    for s in range(blocks):
        scratch = wide.at[s]
        for i in range(part):
            y = first + i
            at = (CORES * (s % chips) + s // chips) * part + i
            p = partials[s][i]
            v, a, b = (x.astype(F32) for x in (centers[s][i], one[at], two[at]))
            image = with_dom(faces, y, v, p, a, b).astype(BF16).astype(F32)
            scratch[pl.ds((1 - late) * part + i, columns, stride=half), :] = image
            scratch[pl.ds(late * part + i, columns, stride=half), :] = done[s][i].astype(F32)
        for c in range(columns):
            turned[s, c, 0] = scratch[c * half:(c + 1) * half, :].astype(BF16)
        partner = CORES * (s % chips) + s // chips
        copy = pltpu.make_async_copy(turned.at[s], applied.at[pl.ds((me ^ partner) * columns, columns)], sems.at[s])
        copy.start()
        copies.append(copy)
    for copy in copies:
        copy.wait()


def sum_kernel(slabs, blocks, shares, reduced):
    chips = blocks // CORES
    columns = shares.shape[2] // blocks
    sums = []
    for sender in range(blocks):
        total = shares[sender]
        for slab in range(1, slabs):
            total += shares[slab * blocks + sender]
        sums.append(total)
    for target in range(blocks):
        parts = []
        for sender in range(blocks):
            partner = sender ^ target
            i = partner % CORES * chips + partner // CORES
            parts.append(sums[sender][:, i * columns:(i + 1) * columns])
        reduced[:, target * columns:(target + 1) * columns] = functools.reduce(jnp.add, parts)


def per_device(basis, zone, cond_table, heat_table):
    blocks = lax.axis_size("blk")
    slabs = lax.axis_size("dom")
    chips = blocks // CORES
    count = chips - 1
    columns, planes, ny, nz = basis.shape
    rows = ny // chips
    half = ny // blocks
    part = half // 2
    total = columns * blocks
    weight = 1.0 / (slabs * planes * ny * nz)
    image = jax.ShapeDtypeStruct((half, columns, nz), BF16)
    half_image = jax.ShapeDtypeStruct((part, columns, nz), BF16)
    center_shape = jax.ShapeDtypeStruct((rows + 2, columns, nz), BF16)
    partial = jax.ShapeDtypeStruct((rows, columns, nz), F32)
    whole = jax.ShapeDtypeStruct((total, 1, half, nz), BF16)
    params = pltpu.CompilerParams(vmem_limit_bytes=32 << 20)
    costly = pl.CostEstimate(flops=COST, bytes_accessed=COST // 8, transcendentals=0)
    cheap = pl.CostEstimate(flops=1, bytes_accessed=1, transcendentals=0)

    def call(kernel, out_shape, inputs, scratch=(), specs=None, out_specs=None, cost=cheap, aliases={}):
        return pl.pallas_call(
            kernel,
            out_shape=out_shape,
            in_specs=specs or [VMEM] * len(inputs),
            out_specs=out_specs or [VMEM] * len(out_shape),
            scratch_shapes=scratch,
            input_output_aliases=aliases,
            compiler_params=params,
            cost_estimate=cost,
        )(*inputs)

    def hbm(array):
        return pltpu.with_memory_space_constraint(array, pltpu.HBM)

    def after(value, *others):
        return lax.optimization_barrier((value, *others))[0]

    def swap(array, s):
        return lax.ppermute(array, "blk", [(i, i ^ s) for i in range(blocks)])

    def exchange(array, offset, s=0):
        partner = [((d + offset) ^ 1) - offset for d in range(slabs)]
        pairs = [
            (d * blocks + b, to * blocks + (b ^ s))
            for d, to in enumerate(partner) if 0 <= to < slabs for b in range(blocks)
        ]
        return lax.ppermute(array, ("dom", "blk"), pairs)

    late_shape = pltpu.HBM((part, columns, nz), BF16)
    terms_shape = pltpu.HBM((part, columns, nz), F32)

    near, center, firsts, seconds = prepare(basis, zone, cond_table, chips)
    two = exchange(near, 1)
    one = exchange(near, 0)
    firsts = [swap(array, CORES * (k + 1)) for k, array in enumerate(firsts)]
    other = swap(center, 1)
    coef, near_partial, late_rows, late_terms = call(
        functools.partial(plane_kernel, chips),
        (jax.ShapeDtypeStruct((6, rows, nz), F32), partial, late_shape, terms_shape),
        (hbm(zone), hbm(cond_table), hbm(heat_table), after(center, other)),
        [pltpu.VMEM((ny + 16, nz), F32)],
        [VMEM, SMEM, SMEM, VMEM],
        cost=costly,
    )
    seconds = [swap(array, CORES * (k + 1)) for k, array in enumerate(seconds)]
    firsts = [after(array, coef, one) for array in firsts]
    early_two = [exchange(array, 1) for array in firsts]
    early_one = [exchange(array, 0) for array in firsts]
    other_firsts = [swap(after(array, two)[:half], 1) for array in firsts]
    outers = [swap(after(array, two)[half:], 1) for array in firsts]
    other_seconds = [swap(after(array, coef), 1) for array in seconds]
    late, = call(
        functools.partial(pack_kernel, chips),
        (jax.ShapeDtypeStruct((CORES * chips * part, columns, nz), BF16),),
        (center, other, *seconds, *other_seconds),
    )
    late_two, late_one = exchange(late, 1), exchange(late, 0)

    near_mine, near_theirs, faces, near_flat = call(
        near_kernel,
        (
            late_shape,
            half_image,
            jax.ShapeDtypeStruct((3, rows, nz), F32),
            jax.ShapeDtypeStruct((columns, rows * nz), BF16),
        ),
        (coef, near_partial, center, one, two),
    )
    results = call(
        functools.partial(gather_kernel, chips),
        [center_shape] * count + [partial] * count + [center_shape] * count
        + [late_shape] * (count + chips) + [terms_shape] * (count + chips),
        (after(coef, faces), other, *firsts, *seconds, *other_firsts, *outers, *other_seconds),
    )
    centers, partials, other_centers = (results[i * count:(i + 1) * count] for i in range(3))
    results = results[3 * count:]
    late_rows = [late_rows, *results[:count + chips]]
    late_terms = [late_terms, *results[count + chips:]]
    left, tall, flatter = call(
        functools.partial(left_kernel, chips),
        (
            jax.ShapeDtypeStruct((total, rows * nz), BF16),
            jax.ShapeDtypeStruct((total, chips * columns), F32),
            jax.ShapeDtypeStruct((chips * columns, total), F32),
        ),
        (faces, near_flat, center, *centers, other, *other_centers, *partials),
        [pltpu.VMEM((columns, rows * nz // 2), BF16)],
    )
    *images, gram = call(
        functools.partial(gram_kernel, chips, weight),
        [late_shape] * (2 * count) + [pltpu.HBM((total, total), F32)],
        (faces, left, tall, flatter, *partials, *centers, *early_two, *early_one),
        [pltpu.VMEM((columns, rows * nz // 2), BF16), pltpu.VMEM((total, chips * columns), F32)],
    )
    parts = slabs * blocks
    shares = gram.reshape(parts, total // parts, total)
    shares = lax.all_to_all(shares, ("dom", "blk"), split_axis=0, concat_axis=0, tiled=True)
    done = [near_mine, *images[:count], *(swap(array, 1) for array in (near_theirs, *images[count:]))]
    pieces = [hbm(x) for x in (faces, late_two, late_one, *done, *late_terms, *late_rows)]
    applied, = call(
        functools.partial(late_kernel, chips),
        (whole,),
        pieces,
        [
            pltpu.VMEM((blocks, columns * half, nz), F32),
            pltpu.VMEM((blocks, columns, 1, half, nz), BF16),
            pltpu.SemaphoreType.DMA((blocks,)),
        ],
        out_specs=[ANY],
    )
    reduced, = call(
        functools.partial(sum_kernel, slabs, blocks), (jax.ShapeDtypeStruct((total // parts, total), F32),),
        (after(shares, applied),)
    )
    return applied, reduced


def solution(mesh):
    placed = (P("blk", "dom", "roll", None), P("dom", "roll", None), P(), P())
    return jax.shard_map(
        per_device,
        mesh=mesh,
        in_specs=placed,
        out_specs=(P("roll", "dom", "blk", None), P(("dom", "blk"), "roll")),
        check_vma=False,
    )
```

```python
import functools

import jax
import jax.numpy as jnp
from jax import lax
from jax.experimental import pallas as pl
from jax.experimental.pallas import tpu as pltpu
from jax.sharding import PartitionSpec as P

ZONES = 16
CORES = 2
COST = 1 << 30
F32 = jnp.float32
BF16 = jnp.bfloat16
VMEM = pl.BlockSpec(memory_space=pltpu.VMEM)
SMEM = pl.BlockSpec(memory_space=pltpu.SMEM)
HBM = pl.BlockSpec(memory_space=pltpu.HBM)
ANY = pl.BlockSpec(memory_space=pl.ANY)


def lookup(zone, table_ref):
    result = jnp.zeros(zone.shape, F32)
    for which in range(ZONES):
        result = jnp.where(zone == which, table_ref[which], result)
    return result


def cond_of(zone, table_ref):
    return lookup(zone, table_ref).astype(BF16).astype(F32)


def prepare_kernel(chips, basis_hbm, zone_hbm, cond_hbm, *refs):
    near, center, plain, firsts, seconds = *refs[:3], refs[3:2 + chips], refs[2 + chips:2 * chips + 1]
    basis, zone, table, wide, turned, cond_pad, in_sems, out_sems = refs[2 * chips + 1:]
    columns, _, ny, nz = basis.shape
    rows = ny // chips
    chip = lax.axis_index("blk") // CORES
    step = 16
    chunks = columns // step
    pitch = wide.shape[0] // columns
    loads = [
        pltpu.make_async_copy(basis_hbm.at[pl.ds(i * step, step)], basis.at[pl.ds(i * step, step)], in_sems.at[i])
        for i in range(chunks)
    ]
    loads.append(pltpu.make_async_copy(zone_hbm, zone, in_sems.at[chunks]))
    loads.append(pltpu.make_async_copy(cond_hbm, table, in_sems.at[chunks + 1]))
    for load in loads:
        load.start()
    turned[0] = jnp.zeros((columns, nz), BF16)
    turned[ny + 1] = jnp.zeros((columns, nz), BF16)
    stores = []

    def store(source, target):
        copy = pltpu.make_async_copy(source, target, out_sems.at[len(stores)])
        copy.start()
        stores.append(copy)

    for i in range(chunks):
        if i == chunks - 1:
            loads[chunks].wait()
            loads[chunks + 1].wait()
            mine = zone[0, pl.ds(pl.multiple_of(chip * rows, rows), rows), :]
            own = cond_of(mine, table)
            cond_pad[...] = jnp.concatenate([own, jnp.zeros((columns - rows, nz), F32)], 0).astype(BF16)
            store(cond_pad, near.at[rows])
        loads[i].wait()
        some = pl.ds(i * step, step)
        for c in range(i * step, (i + 1) * step):
            wide[c * pitch:c * pitch + ny, :] = basis[c, 0].astype(F32)
        for y in range(ny):
            turned[y + 1, some, :] = wide[pl.ds(i * step * pitch + y, step, stride=pitch), :].astype(BF16)
        store(turned.at[pl.ds(chip * rows + 1, rows), some], near.at[pl.ds(0, rows), some])
        for k in range(1, chips):
            start = (chip ^ k) * rows
            store(turned.at[pl.ds(start, rows // 2 + 1), some], firsts[k - 1].at[:, some])
            store(turned.at[pl.ds(start + rows // 2 + 1, rows // 2 + 1), some], seconds[k - 1].at[:, some])
        store(turned.at[pl.ds(chip * rows, rows + 2), some], center.at[:, some])
        store(turned.at[pl.ds(chip * rows + 1, rows), some], plain.at[:, some])
    for copy in stores:
        copy.wait()


def prepare(basis, zone, cond_table, chips):
    columns, _, ny, nz = basis.shape
    rows = ny // chips
    slabs = [rows + 1, rows + 2, rows] + [rows // 2 + 1] * (2 * chips - 2)
    shapes = [jax.ShapeDtypeStruct((n, columns, nz), BF16) for n in slabs]
    results = pl.pallas_call(
        functools.partial(prepare_kernel, chips),
        out_shape=shapes,
        in_specs=[HBM, HBM, HBM],
        out_specs=[pl.BlockSpec(memory_space=pl.ANY)] * len(shapes),
        scratch_shapes=[
            pltpu.VMEM(basis.shape, BF16),
            pltpu.VMEM(zone.shape, jnp.int32),
            pltpu.SMEM((ZONES,), F32),
            pltpu.VMEM((columns * (ny + 8), nz), F32),
            pltpu.VMEM((ny + 2, columns, nz), BF16),
            pltpu.VMEM((columns, nz), BF16),
            pltpu.SemaphoreType.DMA((columns // 16 + 2,)),
            pltpu.SemaphoreType.DMA((1 + (2 * chips + 1) * (columns // 16),)),
        ],
        compiler_params=pltpu.CompilerParams(vmem_limit_bytes=16 << 20),
    )(*[pltpu.with_memory_space_constraint(x, pltpu.HBM) for x in (basis, zone, cond_table)])
    return (*results[:3], results[3:2 + chips], results[2 + chips:])


def plane_kernel(chips, zone_ref, cond_ref, heat_ref, center, coef, partial, cond_pad):
    rows = partial.shape[0]
    nz = center.shape[2]
    ny = zone_ref.shape[1]
    chip = lax.axis_index("blk") // CORES
    cond_pad[0:8, :] = jnp.zeros((8, nz), F32)
    cond_pad[8:8 + ny, :] = cond_of(zone_ref[0], cond_ref)
    cond_pad[8 + ny:16 + ny, :] = jnp.zeros((8, nz), F32)
    base = pl.multiple_of(chip * rows, 8)
    near = cond_pad[pl.ds(base, rows + 16), :]
    own = near[8:8 + rows]
    lane = lax.broadcasted_iota(jnp.int32, (rows, nz), 1)
    coef[0] = lookup(zone_ref[0, pl.ds(base, rows), :], heat_ref)
    beside = (
        near[7:7 + rows],
        near[9:9 + rows],
        jnp.where(lane == 0, 0.0, pltpu.roll(own, 1, 1)),
        jnp.where(lane == nz - 1, 0.0, pltpu.roll(own, nz - 1, 1)),
    )
    for which, other in enumerate(beside):
        coef[1 + which] = 0.5 * (own + other)
    coef[5] = own
    plane_rows(coef, center, partial)


def plane_rows(coef, center, partial):
    columns, nz = center.shape[1:]
    lane = lax.broadcasted_iota(jnp.int32, (columns, nz), 1)
    first, last = lane == 0, lane == nz - 1
    for y in range(partial.shape[0]):
        face = [jnp.broadcast_to(coef[k, y:y + 1, :], (columns, nz)) for k in range(5)]
        v = center[y + 1].astype(F32)
        total = face[0] * v
        total += face[1] * (v - center[y].astype(F32))
        total += face[2] * (v - center[y + 2].astype(F32))
        total += face[3] * (v - jnp.where(first, 0.0, pltpu.roll(v, 1, 1)))
        total += face[4] * (v - jnp.where(last, 0.0, pltpu.roll(v, nz - 1, 1)))
        partial[y] = total


def image_row(faces, y, partial, v, one, two):
    columns, nz = v.shape
    face = [jnp.broadcast_to(faces[k, y:y + 1, :], (columns, nz)) for k in range(2)]
    v = v.astype(F32)
    total = partial + face[0] * (v - one.astype(F32))
    return (total + face[1] * (v - two.astype(F32))).astype(BF16)


def gram_of(left, right):
    return lax.dot_general(left, right, (((1,), (1,)), ((), ())), preferred_element_type=F32)


def near_kernel(coef, partial, center, one, two, mine, theirs, faces, flat):
    rows, _, nz = partial.shape
    half = rows // CORES
    core = lax.axis_index("blk") % CORES
    for which, ref in enumerate((one, two)):
        faces[which] = 0.5 * (coef[5] + ref[rows].astype(F32)[:rows])
    for y in range(rows):
        image = image_row(faces, y, partial[y], center[y + 1], one[y], two[y])
        flat[:, y * nz:(y + 1) * nz] = image

        @pl.when(core == y // half)
        def _():
            mine[y % half] = image

        @pl.when(core != y // half)
        def _():
            theirs[y % half] = image


def gather_kernel(chips, coef, *refs):
    count = chips - 1
    firsts, seconds, centers, partials = (refs[i * count:(i + 1) * count] for i in range(4))
    for first, second, center, partial in zip(firsts, seconds, centers, partials):
        half = first.shape[0]
        center[0:half] = first[...]
        center[half:2 * half] = second[...]
        plane_rows(coef, center, partial)


def first_far_kernel(chips, faces, *refs):
    count = chips - 1
    partials, centers, twos, ones, images, flats = (refs[i * count:(i + 1) * count] for i in range(6))
    nz = partials[0].shape[2]
    for k in range(count):
        for y in range(partials[k].shape[0] // 2):
            image = image_row(faces, y, partials[k][y], centers[k][y + 1], ones[k][y + 1], twos[k][y + 1])
            flats[k][:, y * nz:(y + 1) * nz] = image
            images[k][y] = image


def left_kernel(chips, weight, flat, center, plain, *refs):
    count = chips - 1
    flats, centers, other_firsts, other_seconds = (refs[i * count:(i + 1) * count] for i in range(4))
    left, gram = refs[4 * count:]
    columns, nz = center.shape[1:]
    rows = center.shape[0] - 2
    half = rows // 2
    me = lax.axis_index("blk")
    for k, ref in enumerate((center, *centers)):
        for core in range(CORES):
            where = pl.ds(pl.multiple_of((me ^ (CORES * k + core)) * columns, columns), columns)
            for y in range(rows):
                if not core:
                    side = ref[y + 1]
                elif not k:
                    side = plain[y]
                else:
                    side = other_firsts[k - 1][y] if y < half else other_seconds[k - 1][y - half]
                left[where, y * nz:(y + 1) * nz] = side
    gram[:, 0:columns] = weight * gram_of(left[...], flat[...])
    for k in range(count):
        gram[:, (k + 1) * columns:(k + 2) * columns] = weight * gram_of(left[:, 0:half * nz], flats[k][...])


def second_far_kernel(chips, weight, faces, left, first_gram, *refs):
    count = chips - 1
    partials, centers, twos, ones, images, mine, theirs = (refs[i * count:(i + 1) * count] for i in range(7))
    gram = refs[7 * count]
    rows, columns, nz = partials[0].shape
    half = rows // 2
    core = lax.axis_index("blk") % CORES
    gram[:, 0:columns] = first_gram[:, 0:columns]
    for k in range(count):
        total = first_gram[:, (k + 1) * columns:(k + 2) * columns]
        for i in range(0, half, 2):
            pair = []
            for at in (i, i + 1):
                y = half + at
                image = image_row(faces, y, partials[k][y], centers[k][y + 1], ones[k][at], twos[k][at])
                other = images[k][at]
                mine[k][at] = jnp.where(core == 0, other, image)
                theirs[k][at] = jnp.where(core == 0, image, other)
                pair.append(image)
            y = half + i
            total += weight * gram_of(left[:, y * nz:(y + 2) * nz], jnp.concatenate(pair, 1))
        gram[:, (k + 1) * columns:(k + 2) * columns] = total


def turn_out(image, start, applied, wide, turned, sem):
    rows, columns, _ = image.shape
    for y in range(rows):
        wide[pl.ds(y, columns, stride=rows), :] = image[y].astype(F32)
    for c in range(columns):
        turned[c, 0] = wide[c * rows:(c + 1) * rows, :].astype(BF16)
    copy = pltpu.make_async_copy(turned, applied.at[pl.ds(start, columns)], sem)
    copy.start()
    return copy


def first_kernel(mine, theirs, applied, wide, turned, sems):
    me = lax.axis_index("blk")
    columns = mine.shape[1]
    copies = [
        turn_out(image, (me ^ s) * columns, applied, wide.at[s], turned.at[s], sems.at[s])
        for s, image in enumerate((mine, theirs))
    ]
    for copy in copies:
        copy.wait()


def last_kernel(blocks, applied_in, *refs):
    del applied_in
    images, (applied, wide, turned, sems) = refs[:blocks - CORES], refs[blocks - CORES:]
    me = lax.axis_index("blk")
    columns = images[0].shape[1]
    copies = [
        turn_out(image, (me ^ (s + CORES)) * columns, applied, wide.at[s], turned.at[s], sems.at[s])
        for s, image in enumerate(images)
    ]
    for copy in copies:
        copy.wait()


def sum_kernel(slabs, blocks, shares, reduced):
    chips = blocks // CORES
    columns = shares.shape[2] // chips
    for core in range(CORES):
        sums = []
        for chip in range(chips):
            total = shares[CORES * chip + core]
            for slab in range(1, slabs):
                total += shares[slab * blocks + CORES * chip + core]
            sums.append(total)
        for target in range(chips):
            parts = [sums[chip][:, (chip ^ target) * columns:((chip ^ target) + 1) * columns] for chip in range(chips)]
            start = (CORES * target + core) * columns
            reduced[:, start:start + columns] = functools.reduce(jnp.add, parts)


def per_device(basis, zone, cond_table, heat_table):
    blocks = lax.axis_size("blk")
    slabs = lax.axis_size("dom")
    chips = blocks // CORES
    count = chips - 1
    columns, planes, ny, nz = basis.shape
    rows = ny // chips
    half = ny // blocks
    total = columns * blocks
    weight = 1.0 / (slabs * planes * ny * nz)
    image = jax.ShapeDtypeStruct((half, columns, nz), BF16)
    center_shape = jax.ShapeDtypeStruct((rows + 2, columns, nz), BF16)
    partial = jax.ShapeDtypeStruct((rows, columns, nz), F32)
    whole = jax.ShapeDtypeStruct((total, 1, half, nz), BF16)
    params = pltpu.CompilerParams(vmem_limit_bytes=32 << 20)
    costly = pl.CostEstimate(flops=COST, bytes_accessed=COST // 8, transcendentals=0)
    cheap = pl.CostEstimate(flops=1, bytes_accessed=1, transcendentals=0)

    def call(kernel, out_shape, inputs, scratch=(), specs=None, out_specs=None, cost=cheap, aliases={}):
        return pl.pallas_call(
            kernel,
            out_shape=out_shape,
            in_specs=specs or [VMEM] * len(inputs),
            out_specs=out_specs or [VMEM] * len(out_shape),
            scratch_shapes=scratch,
            input_output_aliases=aliases,
            compiler_params=params,
            cost_estimate=cost,
        )(*inputs)

    def after(value, *others):
        return lax.optimization_barrier((value, *others))[0]

    def swap(array, s):
        return lax.ppermute(array, "blk", [(i, i ^ s) for i in range(blocks)])

    def exchange(array, offset):
        partner = [((d + offset) ^ 1) - offset for d in range(slabs)]
        return lax.ppermute(array, "dom", [(d, to) for d, to in enumerate(partner) if 0 <= to < slabs])

    def turning(n):
        return [
            pltpu.VMEM((n, columns * half, nz), F32),
            pltpu.VMEM((n, columns, 1, half, nz), BF16),
            pltpu.SemaphoreType.DMA((n,)),
        ]

    sent, center, plain, firsts, seconds = prepare(basis, zone, cond_table, chips)
    two = exchange(sent, 1)
    one = exchange(sent, 0)
    firsts = [swap(array, CORES * (k + 1)) for k, array in enumerate(firsts)]
    coef, near_partial = call(
        functools.partial(plane_kernel, chips),
        (jax.ShapeDtypeStruct((6, rows, nz), F32), partial),
        (zone, cond_table, heat_table, center),
        [pltpu.VMEM((ny + 16, nz), F32)],
        [VMEM, SMEM, SMEM, VMEM],
        cost=costly,
    )
    seconds = [swap(after(array, coef), CORES * (k + 1)) for k, array in enumerate(seconds)]
    firsts = [after(array, coef) for array in firsts]
    first_two = [exchange(array, 1) for array in firsts]
    first_one = [exchange(array, 0) for array in firsts]
    second_two = [exchange(array, 1) for array in seconds]
    second_one = [exchange(array, 0) for array in seconds]
    near_mine, near_theirs, faces, near_flat = call(
        near_kernel,
        (
            image,
            image,
            jax.ShapeDtypeStruct((2, rows, nz), F32),
            jax.ShapeDtypeStruct((columns, rows * nz), BF16),
        ),
        (coef, near_partial, center, one, two),
    )
    results = call(
        functools.partial(gather_kernel, chips), [center_shape] * count + [partial] * count, (coef, *firsts, *seconds)
    )
    centers, partials = results[:count], results[count:]
    plain = swap(after(plain, *seconds), 1)
    other_firsts = [swap(after(array, two)[1:], 1) for array in firsts]
    other_seconds = [swap(after(array, two)[:-1], 1) for array in seconds]
    half_flat = jax.ShapeDtypeStruct((columns, rows * nz // 2), BF16)
    results = call(
        functools.partial(first_far_kernel, chips),
        [image] * count + [half_flat] * count,
        (faces, *partials, *centers, *first_two, *first_one),
    )
    images, flats = results[:count], results[count:]
    applied, = call(
        first_kernel, (whole,), (near_mine, swap(near_theirs, 1)), turning(CORES), out_specs=[ANY]
    )
    gram_shape = jax.ShapeDtypeStruct((total, chips * columns), F32)
    left, first_gram = call(
        functools.partial(left_kernel, chips, weight),
        (jax.ShapeDtypeStruct((total, rows * nz), BF16), gram_shape),
        (near_flat, center, plain, *flats, *centers, *other_firsts, *other_seconds),
    )
    *images, gram = call(
        functools.partial(second_far_kernel, chips, weight),
        [image] * (2 * count) + [gram_shape],
        (faces, left, first_gram, *partials, *centers, *second_two, *second_one, *images),
    )
    parts = slabs * blocks
    shares = gram.reshape(parts, total // parts, chips * columns)
    shares = lax.all_to_all(shares, ("dom", "blk"), split_axis=0, concat_axis=0, tiled=True)
    pieces = []
    for k in range(count):
        pieces += [images[k], swap(images[count + k], 1)]
    applied, = call(
        functools.partial(last_kernel, blocks),
        (whole,),
        (applied, *pieces),
        turning(len(pieces)),
        [ANY] + [VMEM] * len(pieces),
        [ANY],
        aliases={0: 0},
    )
    reduced, = call(
        functools.partial(sum_kernel, slabs, blocks), (jax.ShapeDtypeStruct((total // parts, total), F32),), (after(shares, applied),)
    )
    return applied, reduced


def solution(mesh):
    placed = (P("blk", "dom", "roll", None), P("dom", "roll", None), P(), P())
    return jax.shard_map(
        per_device,
        mesh=mesh,
        in_specs=placed,
        out_specs=(P("roll", "dom", "blk", None), P(("dom", "blk"), "roll")),
        check_vma=False,
    )
```

```python
import functools

import jax
import jax.numpy as jnp
from jax import lax
from jax.experimental import pallas as pl
from jax.experimental.pallas import tpu as pltpu
from jax.sharding import PartitionSpec as P

ZONES = 16
CORES = 2
COST = 1 << 30
F32 = jnp.float32
BF16 = jnp.bfloat16
VMEM = pl.BlockSpec(memory_space=pltpu.VMEM)
SMEM = pl.BlockSpec(memory_space=pltpu.SMEM)
HBM = pl.BlockSpec(memory_space=pltpu.HBM)
ANY = pl.BlockSpec(memory_space=pl.ANY)


def lookup(zone, table_ref):
    result = jnp.zeros(zone.shape, F32)
    for which in range(ZONES):
        result = jnp.where(zone == which, table_ref[which], result)
    return result


def cond_of(zone, table_ref):
    return lookup(zone, table_ref).astype(BF16).astype(F32)


def prepare_kernel(chips, basis_hbm, zone_hbm, cond_hbm, *refs):
    near, center, plain, firsts, seconds = *refs[:3], refs[3:2 + chips], refs[2 + chips:2 * chips + 1]
    basis, zone, table, wide, turned, cond_pad, in_sems, out_sems = refs[2 * chips + 1:]
    columns, _, ny, nz = basis.shape
    rows = ny // chips
    chip = lax.axis_index("blk") // CORES
    step = 16
    chunks = columns // step
    pitch = wide.shape[0] // columns
    loads = [
        pltpu.make_async_copy(basis_hbm.at[pl.ds(i * step, step)], basis.at[pl.ds(i * step, step)], in_sems.at[i])
        for i in range(chunks)
    ]
    loads.append(pltpu.make_async_copy(zone_hbm, zone, in_sems.at[chunks]))
    loads.append(pltpu.make_async_copy(cond_hbm, table, in_sems.at[chunks + 1]))
    for load in loads:
        load.start()
    turned[0] = jnp.zeros((columns, nz), BF16)
    turned[ny + 1] = jnp.zeros((columns, nz), BF16)
    stores = []

    def store(source, target):
        copy = pltpu.make_async_copy(source, target, out_sems.at[len(stores)])
        copy.start()
        stores.append(copy)

    for i in range(chunks):
        if i == chunks - 1:
            loads[chunks].wait()
            loads[chunks + 1].wait()
            mine = zone[0, pl.ds(pl.multiple_of(chip * rows, rows), rows), :]
            own = cond_of(mine, table)
            cond_pad[...] = jnp.concatenate([own, jnp.zeros((columns - rows, nz), F32)], 0).astype(BF16)
            store(cond_pad, near.at[rows])
        loads[i].wait()
        some = pl.ds(i * step, step)
        for c in range(i * step, (i + 1) * step):
            wide[c * pitch:c * pitch + ny, :] = basis[c, 0].astype(F32)
        for y in range(ny):
            turned[y + 1, some, :] = wide[pl.ds(i * step * pitch + y, step, stride=pitch), :].astype(BF16)
        store(turned.at[pl.ds(chip * rows + 1, rows), some], near.at[pl.ds(0, rows), some])
        for k in range(1, chips):
            start = (chip ^ k) * rows
            store(turned.at[pl.ds(start, rows // 2 + 1), some], firsts[k - 1].at[:, some])
            store(turned.at[pl.ds(start + rows // 2 + 1, rows // 2 + 1), some], seconds[k - 1].at[:, some])
        store(turned.at[pl.ds(chip * rows, rows + 2), some], center.at[:, some])
        store(turned.at[pl.ds(chip * rows + 1, rows), some], plain.at[:, some])
    for copy in stores:
        copy.wait()


def prepare(basis, zone, cond_table, chips):
    columns, _, ny, nz = basis.shape
    rows = ny // chips
    slabs = [rows + 1, rows + 2, rows] + [rows // 2 + 1] * (2 * chips - 2)
    shapes = [jax.ShapeDtypeStruct((n, columns, nz), BF16) for n in slabs]
    results = pl.pallas_call(
        functools.partial(prepare_kernel, chips),
        out_shape=shapes,
        in_specs=[HBM, HBM, HBM],
        out_specs=[pl.BlockSpec(memory_space=pl.ANY)] * len(shapes),
        scratch_shapes=[
            pltpu.VMEM(basis.shape, BF16),
            pltpu.VMEM(zone.shape, jnp.int32),
            pltpu.SMEM((ZONES,), F32),
            pltpu.VMEM((columns * (ny + 8), nz), F32),
            pltpu.VMEM((ny + 2, columns, nz), BF16),
            pltpu.VMEM((columns, nz), BF16),
            pltpu.SemaphoreType.DMA((columns // 16 + 2,)),
            pltpu.SemaphoreType.DMA((1 + (2 * chips + 1) * (columns // 16),)),
        ],
        compiler_params=pltpu.CompilerParams(vmem_limit_bytes=16 << 20),
    )(*[pltpu.with_memory_space_constraint(x, pltpu.HBM) for x in (basis, zone, cond_table)])
    return (*results[:3], results[3:2 + chips], results[2 + chips:])


def plane_kernel(chips, zone_ref, cond_ref, heat_ref, center, coef, partial, cond_pad):
    rows = partial.shape[0]
    nz = center.shape[2]
    ny = zone_ref.shape[1]
    chip = lax.axis_index("blk") // CORES
    cond_pad[0:8, :] = jnp.zeros((8, nz), F32)
    cond_pad[8:8 + ny, :] = cond_of(zone_ref[0], cond_ref)
    cond_pad[8 + ny:16 + ny, :] = jnp.zeros((8, nz), F32)
    base = pl.multiple_of(chip * rows, 8)
    near = cond_pad[pl.ds(base, rows + 16), :]
    own = near[8:8 + rows]
    lane = lax.broadcasted_iota(jnp.int32, (rows, nz), 1)
    coef[0] = lookup(zone_ref[0, pl.ds(base, rows), :], heat_ref)
    beside = (
        near[7:7 + rows],
        near[9:9 + rows],
        jnp.where(lane == 0, 0.0, pltpu.roll(own, 1, 1)),
        jnp.where(lane == nz - 1, 0.0, pltpu.roll(own, nz - 1, 1)),
    )
    for which, other in enumerate(beside):
        coef[1 + which] = 0.5 * (own + other)
    coef[5] = own
    plane_rows(coef, center, partial)


def plane_rows(coef, center, partial):
    columns, nz = center.shape[1:]
    lane = lax.broadcasted_iota(jnp.int32, (columns, nz), 1)
    first, last = lane == 0, lane == nz - 1
    for y in range(partial.shape[0]):
        face = [jnp.broadcast_to(coef[k, y:y + 1, :], (columns, nz)) for k in range(5)]
        v = center[y + 1].astype(F32)
        total = face[0] * v
        total += face[1] * (v - center[y].astype(F32))
        total += face[2] * (v - center[y + 2].astype(F32))
        total += face[3] * (v - jnp.where(first, 0.0, pltpu.roll(v, 1, 1)))
        total += face[4] * (v - jnp.where(last, 0.0, pltpu.roll(v, nz - 1, 1)))
        partial[y] = total


def image_row(faces, y, partial, v, one, two):
    columns, nz = v.shape
    face = [jnp.broadcast_to(faces[k, y:y + 1, :], (columns, nz)) for k in range(2)]
    v = v.astype(F32)
    total = partial + face[0] * (v - one.astype(F32))
    return (total + face[1] * (v - two.astype(F32))).astype(BF16)


def gram_of(left, right):
    return lax.dot_general(left, right, (((1,), (1,)), ((), ())), preferred_element_type=F32)


def near_kernel(coef, partial, center, one, two, mine, theirs, faces, flat):
    rows, _, nz = partial.shape
    half = rows // CORES
    core = lax.axis_index("blk") % CORES
    for which, ref in enumerate((one, two)):
        faces[which] = 0.5 * (coef[5] + ref[rows].astype(F32)[:rows])
    for y in range(rows):
        image = image_row(faces, y, partial[y], center[y + 1], one[y], two[y])
        flat[:, y * nz:(y + 1) * nz] = image

        @pl.when(core == y // half)
        def _():
            mine[y % half] = image

        @pl.when(core != y // half)
        def _():
            theirs[y % half] = image


def gather_kernel(chips, coef, *refs):
    count = chips - 1
    firsts, seconds, centers, partials = (refs[i * count:(i + 1) * count] for i in range(4))
    for first, second, center, partial in zip(firsts, seconds, centers, partials):
        half = first.shape[0]
        center[0:half] = first[...]
        center[half:2 * half] = second[...]
        plane_rows(coef, center, partial)


def first_far_kernel(chips, faces, *refs):
    count = chips - 1
    partials, centers, twos, ones, images, flats = (refs[i * count:(i + 1) * count] for i in range(6))
    nz = partials[0].shape[2]
    for k in range(count):
        for y in range(partials[k].shape[0] // 2):
            image = image_row(faces, y, partials[k][y], centers[k][y + 1], ones[k][y + 1], twos[k][y + 1])
            flats[k][:, y * nz:(y + 1) * nz] = image
            images[k][y] = image


def left_kernel(chips, weight, flat, center, plain, *refs):
    count = chips - 1
    flats, centers, other_firsts, other_seconds = (refs[i * count:(i + 1) * count] for i in range(4))
    left, gram = refs[4 * count:]
    columns, nz = center.shape[1:]
    rows = center.shape[0] - 2
    half = rows // 2
    me = lax.axis_index("blk")
    for k, ref in enumerate((center, *centers)):
        for core in range(CORES):
            where = pl.ds(pl.multiple_of((me ^ (CORES * k + core)) * columns, columns), columns)
            for y in range(rows):
                if not core:
                    side = ref[y + 1]
                elif not k:
                    side = plain[y]
                else:
                    side = other_firsts[k - 1][y] if y < half else other_seconds[k - 1][y - half]
                left[where, y * nz:(y + 1) * nz] = side
    gram[:, 0:columns] = weight * gram_of(left[...], flat[...])
    for k in range(count):
        gram[:, (k + 1) * columns:(k + 2) * columns] = weight * gram_of(left[:, 0:half * nz], flats[k][...])


def second_far_kernel(chips, weight, faces, left, first_gram, *refs):
    count = chips - 1
    partials, centers, twos, ones, images, mine, low, high = (refs[i * count:(i + 1) * count] for i in range(8))
    gram = refs[8 * count]
    rows, columns, nz = partials[0].shape
    half = rows // 2
    core = lax.axis_index("blk") % CORES
    gram[:, 0:columns] = first_gram[:, 0:columns]
    for k in range(count):
        block = slice((k + 1) * columns, (k + 2) * columns)
        total = jnp.zeros((left.shape[0], columns), F32)
        for i in range(0, half, 2):
            pair = []
            for at in (i, i + 1):
                y = half + at
                image = image_row(faces, y, partials[k][y], centers[k][y + 1], ones[k][at], twos[k][at])
                other = images[k][at]
                mine[k][at] = jnp.where(core == 0, other, image)
                theirs = low[k] if at < half // 2 else high[k]
                theirs[at % (half // 2)] = jnp.where(core == 0, image, other)
                pair.append(image)
            y = half + i
            total += gram_of(left[:, y * nz:(y + 2) * nz], jnp.concatenate(pair, 1))
        gram[:, block] = first_gram[:, block] + weight * total


def turn_out(image, start, applied, wide, turned, sem):
    rows = sum(part.shape[0] for part in image)
    columns = image[0].shape[1]
    for y, row in enumerate(part.at[y] for part in image for y in range(part.shape[0])):
        wide[pl.ds(y, columns, stride=rows), :] = row[...].astype(F32)
    for c in range(columns):
        turned[c, 0] = wide[c * rows:(c + 1) * rows, :].astype(BF16)
    copy = pltpu.make_async_copy(turned, applied.at[pl.ds(start, columns)], sem)
    copy.start()
    return copy


def first_kernel(mine, theirs, applied, wide, turned, sems):
    me = lax.axis_index("blk")
    columns = mine.shape[1]
    copies = [
        turn_out(image, (me ^ s) * columns, applied, wide.at[s], turned.at[s], sems.at[s])
        for s, image in enumerate(((mine,), (theirs,)))
    ]
    for copy in copies:
        copy.wait()


def last_kernel(blocks, applied_in, *refs):
    del applied_in
    *pieces, applied, wide, turned, sems = refs
    images = []
    for mine, low, high in zip(pieces[0::3], pieces[1::3], pieces[2::3]):
        images += [(mine,), (low, high)]
    me = lax.axis_index("blk")
    columns = pieces[0].shape[1]
    copies = [
        turn_out(image, (me ^ (s + CORES)) * columns, applied, wide.at[s], turned.at[s], sems.at[s])
        for s, image in enumerate(images)
    ]
    for copy in copies:
        copy.wait()


def sum_kernel(slabs, blocks, shares, reduced):
    chips = blocks // CORES
    columns = shares.shape[2] // chips
    for core in range(CORES):
        sums = []
        for chip in range(chips):
            total = shares[CORES * chip + core]
            for slab in range(1, slabs):
                total += shares[slab * blocks + CORES * chip + core]
            sums.append(total)
        for target in range(chips):
            parts = [sums[chip][:, (chip ^ target) * columns:((chip ^ target) + 1) * columns] for chip in range(chips)]
            start = (CORES * target + core) * columns
            reduced[:, start:start + columns] = functools.reduce(jnp.add, parts)


def per_device(basis, zone, cond_table, heat_table):
    blocks = lax.axis_size("blk")
    slabs = lax.axis_size("dom")
    chips = blocks // CORES
    count = chips - 1
    columns, planes, ny, nz = basis.shape
    rows = ny // chips
    half = ny // blocks
    total = columns * blocks
    weight = 1.0 / (slabs * planes * ny * nz)
    image = jax.ShapeDtypeStruct((half, columns, nz), BF16)
    center_shape = jax.ShapeDtypeStruct((rows + 2, columns, nz), BF16)
    partial = jax.ShapeDtypeStruct((rows, columns, nz), F32)
    whole = jax.ShapeDtypeStruct((total, 1, half, nz), BF16)
    params = pltpu.CompilerParams(vmem_limit_bytes=32 << 20)
    costly = pl.CostEstimate(flops=COST, bytes_accessed=COST // 8, transcendentals=0)
    cheap = pl.CostEstimate(flops=1, bytes_accessed=1, transcendentals=0)

    def call(kernel, out_shape, inputs, scratch=(), specs=None, out_specs=None, cost=cheap, aliases={}):
        return pl.pallas_call(
            kernel,
            out_shape=out_shape,
            in_specs=specs or [VMEM] * len(inputs),
            out_specs=out_specs or [VMEM] * len(out_shape),
            scratch_shapes=scratch,
            input_output_aliases=aliases,
            compiler_params=params,
            cost_estimate=cost,
        )(*inputs)

    def after(value, *others):
        return lax.optimization_barrier((value, *others))[0]

    def swap(array, s):
        return lax.ppermute(array, "blk", [(i, i ^ s) for i in range(blocks)])

    def exchange(array, offset):
        partner = [((d + offset) ^ 1) - offset for d in range(slabs)]
        return lax.ppermute(array, "dom", [(d, to) for d, to in enumerate(partner) if 0 <= to < slabs])

    def turning(n):
        return [
            pltpu.VMEM((n, columns * half, nz), F32),
            pltpu.VMEM((n, columns, 1, half, nz), BF16),
            pltpu.SemaphoreType.DMA((n,)),
        ]

    sent, center, plain, firsts, seconds = prepare(basis, zone, cond_table, chips)
    two = exchange(sent, 1)
    one = exchange(sent, 0)
    firsts = [swap(array, CORES * (k + 1)) for k, array in enumerate(firsts)]
    coef, near_partial = call(
        functools.partial(plane_kernel, chips),
        (jax.ShapeDtypeStruct((6, rows, nz), F32), partial),
        (zone, cond_table, heat_table, center),
        [pltpu.VMEM((ny + 16, nz), F32)],
        [VMEM, SMEM, SMEM, VMEM],
        cost=costly,
    )
    seconds = [swap(after(array, coef), CORES * (k + 1)) for k, array in enumerate(seconds)]
    firsts = [after(array, coef) for array in firsts]
    first_two = [exchange(array, 1) for array in firsts]
    first_one = [exchange(array, 0) for array in firsts]
    second_two = [exchange(array, 1) for array in seconds]
    second_one = [exchange(array, 0) for array in seconds]
    near_mine, near_theirs, faces, near_flat = call(
        near_kernel,
        (
            image,
            image,
            jax.ShapeDtypeStruct((2, rows, nz), F32),
            jax.ShapeDtypeStruct((columns, rows * nz), BF16),
        ),
        (coef, near_partial, center, one, two),
    )
    results = call(
        functools.partial(gather_kernel, chips), [center_shape] * count + [partial] * count, (coef, *firsts, *seconds)
    )
    centers, partials = results[:count], results[count:]
    plain = swap(after(plain, *seconds), 1)
    other_firsts = [swap(after(array, two)[1:], 1) for array in firsts]
    other_seconds = [swap(after(array, two)[:-1], 1) for array in seconds]
    half_flat = jax.ShapeDtypeStruct((columns, rows * nz // 2), BF16)
    results = call(
        functools.partial(first_far_kernel, chips),
        [image] * count + [half_flat] * count,
        (faces, *partials, *centers, *first_two, *first_one),
    )
    images, flats = results[:count], results[count:]
    applied, = call(
        first_kernel, (whole,), (near_mine, swap(near_theirs, 1)), turning(CORES), out_specs=[ANY]
    )
    gram_shape = jax.ShapeDtypeStruct((total, chips * columns), F32)
    left, first_gram = call(
        functools.partial(left_kernel, chips, weight),
        (jax.ShapeDtypeStruct((total, rows * nz), BF16), gram_shape),
        (near_flat, center, plain, *flats, *centers, *other_firsts, *other_seconds),
    )
    *images, gram = call(
        functools.partial(second_far_kernel, chips, weight),
        [image] * count + [jax.ShapeDtypeStruct((half // 2, columns, nz), BF16)] * (2 * count) + [gram_shape],
        (faces, left, first_gram, *partials, *centers, *second_two, *second_one, *images),
    )
    parts = slabs * blocks
    shares = gram.reshape(parts, total // parts, chips * columns)
    shares = lax.all_to_all(shares, ("dom", "blk"), split_axis=0, concat_axis=0, tiled=True)
    pieces = []
    for k in range(count):
        pieces += [images[k], *(swap(images[i * count + k], 1) for i in (1, 2))]
    applied, = call(
        functools.partial(last_kernel, blocks),
        (whole,),
        (applied, *pieces),
        turning(CORES * count),
        [ANY] + [VMEM] * len(pieces),
        [ANY],
        aliases={0: 0},
    )
    reduced, = call(
        functools.partial(sum_kernel, slabs, blocks), (jax.ShapeDtypeStruct((total // parts, total), F32),), (after(shares, applied),)
    )
    return applied, reduced


def solution(mesh):
    placed = (P("blk", "dom", "roll", None), P("dom", "roll", None), P(), P())
    return jax.shard_map(
        per_device,
        mesh=mesh,
        in_specs=placed,
        out_specs=(P("roll", "dom", "blk", None), P(("dom", "blk"), "roll")),
        check_vma=False,
    )
```

```python
import functools

import jax
import jax.numpy as jnp
from jax import lax
from jax.experimental import pallas as pl
from jax.experimental.pallas import tpu as pltpu
from jax.sharding import PartitionSpec as P

ZONES = 16
CORES = 2
COST = 1 << 30
F32 = jnp.float32
BF16 = jnp.bfloat16
VMEM = pl.BlockSpec(memory_space=pltpu.VMEM)
SMEM = pl.BlockSpec(memory_space=pltpu.SMEM)
HBM = pl.BlockSpec(memory_space=pltpu.HBM)
ANY = pl.BlockSpec(memory_space=pl.ANY)


def lookup(zone, table_ref):
    result = jnp.zeros(zone.shape, F32)
    for which in range(ZONES):
        result = jnp.where(zone == which, table_ref[which], result)
    return result


def cond_of(zone, table_ref):
    return lookup(zone, table_ref).astype(BF16).astype(F32)


def prepare_kernel(chips, basis_hbm, zone_hbm, cond_hbm, *refs):
    near, center, plain, firsts, seconds = *refs[:3], refs[3:2 + chips], refs[2 + chips:2 * chips + 1]
    basis, zone, table, wide, turned, cond_pad, in_sems, out_sems = refs[2 * chips + 1:]
    columns, _, ny, nz = basis.shape
    rows = ny // chips
    chip = lax.axis_index("blk") // CORES
    step = 16
    chunks = columns // step
    pitch = wide.shape[0] // columns
    loads = [
        pltpu.make_async_copy(basis_hbm.at[pl.ds(i * step, step)], basis.at[pl.ds(i * step, step)], in_sems.at[i])
        for i in range(chunks)
    ]
    loads.append(pltpu.make_async_copy(zone_hbm, zone, in_sems.at[chunks]))
    loads.append(pltpu.make_async_copy(cond_hbm, table, in_sems.at[chunks + 1]))
    for load in loads:
        load.start()
    turned[0] = jnp.zeros((columns, nz), BF16)
    turned[ny + 1] = jnp.zeros((columns, nz), BF16)
    stores = []

    def store(source, target):
        copy = pltpu.make_async_copy(source, target, out_sems.at[len(stores)])
        copy.start()
        stores.append(copy)

    for i in range(chunks):
        if i == chunks - 1:
            loads[chunks].wait()
            loads[chunks + 1].wait()
            mine = zone[0, pl.ds(pl.multiple_of(chip * rows, rows), rows), :]
            own = cond_of(mine, table)
            cond_pad[...] = jnp.concatenate([own, jnp.zeros((columns - rows, nz), F32)], 0).astype(BF16)
            store(cond_pad, near.at[rows])
        loads[i].wait()
        some = pl.ds(i * step, step)
        for c in range(i * step, (i + 1) * step):
            wide[c * pitch:c * pitch + ny, :] = basis[c, 0].astype(F32)
        for y in range(ny):
            turned[y + 1, some, :] = wide[pl.ds(i * step * pitch + y, step, stride=pitch), :].astype(BF16)
        store(turned.at[pl.ds(chip * rows + 1, rows), some], near.at[pl.ds(0, rows), some])
        for k in range(1, chips):
            start = (chip ^ k) * rows
            store(turned.at[pl.ds(start, rows // 2 + 1), some], firsts[k - 1].at[:, some])
            store(turned.at[pl.ds(start + rows // 2 + 1, rows // 2 + 1), some], seconds[k - 1].at[:, some])
        store(turned.at[pl.ds(chip * rows, rows + 2), some], center.at[:, some])
        store(turned.at[pl.ds(chip * rows + 1, rows), some], plain.at[:, some])
    for copy in stores:
        copy.wait()


def prepare(basis, zone, cond_table, chips):
    columns, _, ny, nz = basis.shape
    rows = ny // chips
    slabs = [rows + 1, rows + 2, rows] + [rows // 2 + 1] * (2 * chips - 2)
    shapes = [jax.ShapeDtypeStruct((n, columns, nz), BF16) for n in slabs]
    results = pl.pallas_call(
        functools.partial(prepare_kernel, chips),
        out_shape=shapes,
        in_specs=[HBM, HBM, HBM],
        out_specs=[pl.BlockSpec(memory_space=pl.ANY)] * len(shapes),
        scratch_shapes=[
            pltpu.VMEM(basis.shape, BF16),
            pltpu.VMEM(zone.shape, jnp.int32),
            pltpu.SMEM((ZONES,), F32),
            pltpu.VMEM((columns * (ny + 8), nz), F32),
            pltpu.VMEM((ny + 2, columns, nz), BF16),
            pltpu.VMEM((columns, nz), BF16),
            pltpu.SemaphoreType.DMA((columns // 16 + 2,)),
            pltpu.SemaphoreType.DMA((1 + (2 * chips + 1) * (columns // 16),)),
        ],
        compiler_params=pltpu.CompilerParams(vmem_limit_bytes=16 << 20),
    )(*[pltpu.with_memory_space_constraint(x, pltpu.HBM) for x in (basis, zone, cond_table)])
    return (*results[:3], results[3:2 + chips], results[2 + chips:])


def plane_kernel(chips, zone_ref, cond_ref, heat_ref, center, coef, partial, cond_pad):
    rows = partial.shape[0]
    nz = center.shape[2]
    ny = zone_ref.shape[1]
    chip = lax.axis_index("blk") // CORES
    cond_pad[0:8, :] = jnp.zeros((8, nz), F32)
    cond_pad[8:8 + ny, :] = cond_of(zone_ref[0], cond_ref)
    cond_pad[8 + ny:16 + ny, :] = jnp.zeros((8, nz), F32)
    base = pl.multiple_of(chip * rows, 8)
    near = cond_pad[pl.ds(base, rows + 16), :]
    own = near[8:8 + rows]
    lane = lax.broadcasted_iota(jnp.int32, (rows, nz), 1)
    coef[0] = lookup(zone_ref[0, pl.ds(base, rows), :], heat_ref)
    beside = (
        near[7:7 + rows],
        near[9:9 + rows],
        jnp.where(lane == 0, 0.0, pltpu.roll(own, 1, 1)),
        jnp.where(lane == nz - 1, 0.0, pltpu.roll(own, nz - 1, 1)),
    )
    for which, other in enumerate(beside):
        coef[1 + which] = 0.5 * (own + other)
    coef[5] = own
    plane_rows(coef, center, partial)


def plane_rows(coef, center, partial):
    columns, nz = center.shape[1:]
    lane = lax.broadcasted_iota(jnp.int32, (columns, nz), 1)
    first, last = lane == 0, lane == nz - 1
    for y in range(partial.shape[0]):
        face = [jnp.broadcast_to(coef[k, y:y + 1, :], (columns, nz)) for k in range(5)]
        v = center[y + 1].astype(F32)
        total = face[0] * v
        total += face[1] * (v - center[y].astype(F32))
        total += face[2] * (v - center[y + 2].astype(F32))
        total += face[3] * (v - jnp.where(first, 0.0, pltpu.roll(v, 1, 1)))
        total += face[4] * (v - jnp.where(last, 0.0, pltpu.roll(v, nz - 1, 1)))
        partial[y] = total


def image_row(faces, y, partial, v, one, two):
    columns, nz = v.shape
    face = [jnp.broadcast_to(faces[k, y:y + 1, :], (columns, nz)) for k in range(2)]
    v = v.astype(F32)
    total = partial + face[0] * (v - one.astype(F32))
    return (total + face[1] * (v - two.astype(F32))).astype(BF16)


def gram_of(left, right):
    return lax.dot_general(left, right, (((1,), (1,)), ((), ())), preferred_element_type=F32)


def near_kernel(coef, partial, center, one, two, mine, theirs, faces, flat):
    rows, _, nz = partial.shape
    half = rows // CORES
    core = lax.axis_index("blk") % CORES
    for which, ref in enumerate((one, two)):
        faces[which] = 0.5 * (coef[5] + ref[rows].astype(F32)[:rows])
    for y in range(rows):
        image = image_row(faces, y, partial[y], center[y + 1], one[y], two[y])
        flat[:, y * nz:(y + 1) * nz] = image

        @pl.when(core == y // half)
        def _():
            mine[y % half] = image

        @pl.when(core != y // half)
        def _():
            theirs[y % half] = image


def gather_kernel(chips, coef, *refs):
    count = chips - 1
    firsts, seconds, centers, partials = (refs[i * count:(i + 1) * count] for i in range(4))
    for first, second, center, partial in zip(firsts, seconds, centers, partials):
        half = first.shape[0]
        center[0:half] = first[...]
        center[half:2 * half] = second[...]
        plane_rows(coef, center, partial)


def first_far_kernel(chips, faces, *refs):
    count = chips - 1
    partials, centers, twos, ones, images, flats = (refs[i * count:(i + 1) * count] for i in range(6))
    nz = partials[0].shape[2]
    for k in range(count):
        for y in range(partials[k].shape[0] // 2):
            image = image_row(faces, y, partials[k][y], centers[k][y + 1], ones[k][y + 1], twos[k][y + 1])
            flats[k][:, y * nz:(y + 1) * nz] = image
            images[k][y] = image


def left_kernel(chips, weight, flat, center, plain, *refs):
    count = chips - 1
    flats, centers, other_firsts, other_seconds = (refs[i * count:(i + 1) * count] for i in range(4))
    left, gram = refs[4 * count:]
    columns, nz = center.shape[1:]
    rows = center.shape[0] - 2
    half = rows // 2
    me = lax.axis_index("blk")
    for k, ref in enumerate((center, *centers)):
        for core in range(CORES):
            where = pl.ds(pl.multiple_of((me ^ (CORES * k + core)) * columns, columns), columns)
            for y in range(rows):
                if not core:
                    side = ref[y + 1]
                elif not k:
                    side = plain[y]
                else:
                    side = other_firsts[k - 1][y] if y < half else other_seconds[k - 1][y - half]
                left[where, y * nz:(y + 1) * nz] = side
    gram[:, 0:columns] = weight * gram_of(left[...], flat[...])
    for k in range(count):
        gram[:, (k + 1) * columns:(k + 2) * columns] = weight * gram_of(left[:, 0:half * nz], flats[k][...])


def second_far_kernel(chips, weight, faces, left, first_gram, *refs):
    count = chips - 1
    partials, centers, twos, ones, images, mine, theirs = (refs[i * count:(i + 1) * count] for i in range(7))
    gram = refs[7 * count]
    rows, columns, nz = partials[0].shape
    half = rows // 2
    core = lax.axis_index("blk") % CORES
    slabs, blocks = lax.axis_size("dom"), lax.axis_size("blk")
    share = left.shape[0] // (slabs * blocks)
    values = [first_gram[:, 0:columns]]
    for k in range(count):
        block = slice((k + 1) * columns, (k + 2) * columns)
        total = jnp.zeros((left.shape[0], columns), F32)
        for i in range(0, half, 2):
            pair = []
            for at in (i, i + 1):
                y = half + at
                image = image_row(faces, y, partials[k][y], centers[k][y + 1], ones[k][at], twos[k][at])
                other = images[k][at]
                mine[k][at] = jnp.where(core == 0, other, image)
                theirs[k][at] = jnp.where(core == 0, image, other)
                pair.append(image)
            y = half + i
            total += gram_of(left[:, y * nz:(y + 2) * nz], jnp.concatenate(pair, 1))
        values.append(first_gram[:, block] + weight * total)
    for slab in range(slabs):
        for owner in range(blocks):
            start, place = (slab * blocks + owner) * share, (owner * slabs + slab) * share
            for k, value in enumerate(values):
                gram[place:place + share, k * columns:(k + 1) * columns] = value[start:start + share]


def turn_out(image, start, applied, wide, turned, sem):
    rows, columns, _ = image.shape
    for y in range(rows):
        wide[pl.ds(y, columns, stride=rows), :] = image[y].astype(F32)
    for c in range(columns):
        turned[c, 0] = wide[c * rows:(c + 1) * rows, :].astype(BF16)
    copy = pltpu.make_async_copy(turned, applied.at[pl.ds(start, columns)], sem)
    copy.start()
    return copy


def first_kernel(mine, theirs, applied, wide, turned, sems):
    me = lax.axis_index("blk")
    columns = mine.shape[1]
    copies = [
        turn_out(image, (me ^ s) * columns, applied, wide.at[s], turned.at[s], sems.at[s])
        for s, image in enumerate((mine, theirs))
    ]
    for copy in copies:
        copy.wait()


def last_kernel(blocks, applied_in, *refs):
    del applied_in
    images, (applied, wide, turned, sems) = refs[:blocks - CORES], refs[blocks - CORES:]
    me = lax.axis_index("blk")
    columns = images[0].shape[1]
    copies = [
        turn_out(image, (me ^ (s + CORES)) * columns, applied, wide.at[s], turned.at[s], sems.at[s])
        for s, image in enumerate(images)
    ]
    for copy in copies:
        copy.wait()


def sum_kernel(slabs, blocks, shares, reduced):
    chips = blocks // CORES
    columns = shares.shape[2] // chips
    for core in range(CORES):
        sums = []
        for chip in range(chips):
            total = shares[(CORES * chip + core) * slabs]
            for slab in range(1, slabs):
                total += shares[(CORES * chip + core) * slabs + slab]
            sums.append(total)
        for target in range(chips):
            parts = [sums[chip][:, (chip ^ target) * columns:((chip ^ target) + 1) * columns] for chip in range(chips)]
            start = (CORES * target + core) * columns
            reduced[:, start:start + columns] = functools.reduce(jnp.add, parts)


def per_device(basis, zone, cond_table, heat_table):
    blocks = lax.axis_size("blk")
    slabs = lax.axis_size("dom")
    chips = blocks // CORES
    count = chips - 1
    columns, planes, ny, nz = basis.shape
    rows = ny // chips
    half = ny // blocks
    total = columns * blocks
    weight = 1.0 / (slabs * planes * ny * nz)
    image = jax.ShapeDtypeStruct((half, columns, nz), BF16)
    center_shape = jax.ShapeDtypeStruct((rows + 2, columns, nz), BF16)
    partial = jax.ShapeDtypeStruct((rows, columns, nz), F32)
    whole = jax.ShapeDtypeStruct((total, 1, half, nz), BF16)
    params = pltpu.CompilerParams(vmem_limit_bytes=32 << 20)
    costly = pl.CostEstimate(flops=COST, bytes_accessed=COST // 8, transcendentals=0)
    cheap = pl.CostEstimate(flops=1, bytes_accessed=1, transcendentals=0)

    def call(kernel, out_shape, inputs, scratch=(), specs=None, out_specs=None, cost=cheap, aliases={}):
        return pl.pallas_call(
            kernel,
            out_shape=out_shape,
            in_specs=specs or [VMEM] * len(inputs),
            out_specs=out_specs or [VMEM] * len(out_shape),
            scratch_shapes=scratch,
            input_output_aliases=aliases,
            compiler_params=params,
            cost_estimate=cost,
        )(*inputs)

    def after(value, *others):
        return lax.optimization_barrier((value, *others))[0]

    def swap(array, s):
        return lax.ppermute(array, "blk", [(i, i ^ s) for i in range(blocks)])

    def exchange(array, offset):
        partner = [((d + offset) ^ 1) - offset for d in range(slabs)]
        return lax.ppermute(array, "dom", [(d, to) for d, to in enumerate(partner) if 0 <= to < slabs])

    def turning(n):
        return [
            pltpu.VMEM((n, columns * half, nz), F32),
            pltpu.VMEM((n, columns, 1, half, nz), BF16),
            pltpu.SemaphoreType.DMA((n,)),
        ]

    sent, center, plain, firsts, seconds = prepare(basis, zone, cond_table, chips)
    two = exchange(sent, 1)
    one = exchange(sent, 0)
    firsts = [swap(array, CORES * (k + 1)) for k, array in enumerate(firsts)]
    coef, near_partial = call(
        functools.partial(plane_kernel, chips),
        (jax.ShapeDtypeStruct((6, rows, nz), F32), partial),
        (zone, cond_table, heat_table, center),
        [pltpu.VMEM((ny + 16, nz), F32)],
        [VMEM, SMEM, SMEM, VMEM],
        cost=costly,
    )
    seconds = [swap(after(array, coef), CORES * (k + 1)) for k, array in enumerate(seconds)]
    firsts = [after(array, coef) for array in firsts]
    first_two = [exchange(array, 1) for array in firsts]
    first_one = [exchange(array, 0) for array in firsts]
    second_two = [exchange(array, 1) for array in seconds]
    second_one = [exchange(array, 0) for array in seconds]
    near_mine, near_theirs, faces, near_flat = call(
        near_kernel,
        (
            image,
            image,
            jax.ShapeDtypeStruct((2, rows, nz), F32),
            jax.ShapeDtypeStruct((columns, rows * nz), BF16),
        ),
        (coef, near_partial, center, one, two),
    )
    results = call(
        functools.partial(gather_kernel, chips), [center_shape] * count + [partial] * count, (coef, *firsts, *seconds)
    )
    centers, partials = results[:count], results[count:]
    plain = swap(after(plain, *seconds), 1)
    other_firsts = [swap(after(array, two)[1:], 1) for array in firsts]
    other_seconds = [swap(after(array, two)[:-1], 1) for array in seconds]
    half_flat = jax.ShapeDtypeStruct((columns, rows * nz // 2), BF16)
    results = call(
        functools.partial(first_far_kernel, chips),
        [image] * count + [half_flat] * count,
        (faces, *partials, *centers, *first_two, *first_one),
    )
    images, flats = results[:count], results[count:]
    applied, = call(
        first_kernel, (whole,), (near_mine, swap(near_theirs, 1)), turning(CORES), out_specs=[ANY]
    )
    gram_shape = jax.ShapeDtypeStruct((total, chips * columns), F32)
    left, first_gram = call(
        functools.partial(left_kernel, chips, weight),
        (jax.ShapeDtypeStruct((total, rows * nz), BF16), gram_shape),
        (near_flat, center, plain, *flats, *centers, *other_firsts, *other_seconds),
    )
    *images, gram = call(
        functools.partial(second_far_kernel, chips, weight),
        [image] * (2 * count) + [gram_shape],
        (faces, left, first_gram, *partials, *centers, *second_two, *second_one, *images),
    )
    parts = slabs * blocks
    shares = gram.reshape(parts, total // parts, chips * columns)
    shares = lax.all_to_all(shares, ("blk", "dom"), split_axis=0, concat_axis=0, tiled=True)
    pieces = []
    for k in range(count):
        pieces += [images[k], swap(images[count + k], 1)]
    applied, = call(
        functools.partial(last_kernel, blocks),
        (whole,),
        (applied, *pieces),
        turning(len(pieces)),
        [ANY] + [VMEM] * len(pieces),
        [ANY],
        aliases={0: 0},
    )
    reduced, = call(
        functools.partial(sum_kernel, slabs, blocks), (jax.ShapeDtypeStruct((total // parts, total), F32),), (after(shares, applied),)
    )
    return applied, reduced


def solution(mesh):
    placed = (P("blk", "dom", "roll", None), P("dom", "roll", None), P(), P())
    return jax.shard_map(
        per_device,
        mesh=mesh,
        in_specs=placed,
        out_specs=(P("roll", "dom", "blk", None), P(("dom", "blk"), "roll")),
        check_vma=False,
    )
```

```python
import functools

import jax
import jax.numpy as jnp
from jax import lax
from jax.experimental import pallas as pl
from jax.experimental.pallas import tpu as pltpu
from jax.sharding import PartitionSpec as P

ZONES = 16
CORES = 2
COST = 1 << 30
F32 = jnp.float32
BF16 = jnp.bfloat16
VMEM = pl.BlockSpec(memory_space=pltpu.VMEM)
SMEM = pl.BlockSpec(memory_space=pltpu.SMEM)
HBM = pl.BlockSpec(memory_space=pltpu.HBM)
ANY = pl.BlockSpec(memory_space=pl.ANY)


def lookup(zone, table_ref):
    result = jnp.zeros(zone.shape, F32)
    for which in range(ZONES):
        result = jnp.where(zone == which, table_ref[which], result)
    return result


def cond_of(zone, table_ref):
    return lookup(zone, table_ref).astype(BF16).astype(F32)


def prepare_kernel(chips, basis_hbm, zone_hbm, cond_hbm, *refs):
    near, center, plain, firsts, seconds = *refs[:3], refs[3:2 + chips], refs[2 + chips:2 * chips + 1]
    basis, zone, table, wide, turned, cond_pad, in_sems, out_sems = refs[2 * chips + 1:]
    columns, _, ny, nz = basis.shape
    rows = ny // chips
    chip = lax.axis_index("blk") // CORES
    step = 16
    chunks = columns // step
    pitch = wide.shape[0] // columns
    loads = [
        pltpu.make_async_copy(basis_hbm.at[pl.ds(i * step, step)], basis.at[pl.ds(i * step, step)], in_sems.at[i])
        for i in range(chunks)
    ]
    loads.append(pltpu.make_async_copy(zone_hbm, zone, in_sems.at[chunks]))
    loads.append(pltpu.make_async_copy(cond_hbm, table, in_sems.at[chunks + 1]))
    for load in loads:
        load.start()
    turned[0] = jnp.zeros((columns, nz), BF16)
    turned[ny + 1] = jnp.zeros((columns, nz), BF16)
    stores = []

    def store(source, target):
        copy = pltpu.make_async_copy(source, target, out_sems.at[len(stores)])
        copy.start()
        stores.append(copy)

    for i in range(chunks):
        if i == chunks - 1:
            loads[chunks].wait()
            loads[chunks + 1].wait()
            mine = zone[0, pl.ds(pl.multiple_of(chip * rows, rows), rows), :]
            own = cond_of(mine, table)
            cond_pad[...] = jnp.concatenate([own, jnp.zeros((columns - rows, nz), F32)], 0).astype(BF16)
            store(cond_pad, near.at[rows])
        loads[i].wait()
        some = pl.ds(i * step, step)
        for c in range(i * step, (i + 1) * step):
            wide[c * pitch:c * pitch + ny, :] = basis[c, 0].astype(F32)
        for y in range(ny):
            turned[y + 1, some, :] = wide[pl.ds(i * step * pitch + y, step, stride=pitch), :].astype(BF16)
        store(turned.at[pl.ds(chip * rows + 1, rows), some], near.at[pl.ds(0, rows), some])
        for k in range(1, chips):
            start = (chip ^ k) * rows
            store(turned.at[pl.ds(start, rows // 2 + 1), some], firsts[k - 1].at[:, some])
            store(turned.at[pl.ds(start + rows // 2 + 1, rows // 2 + 1), some], seconds[k - 1].at[:, some])
        store(turned.at[pl.ds(chip * rows, rows + 2), some], center.at[:, some])
        store(turned.at[pl.ds(chip * rows + 1, rows), some], plain.at[:, some])
    for copy in stores:
        copy.wait()


def prepare(basis, zone, cond_table, chips):
    columns, _, ny, nz = basis.shape
    rows = ny // chips
    slabs = [rows + 1, rows + 2, rows] + [rows // 2 + 1] * (2 * chips - 2)
    shapes = [jax.ShapeDtypeStruct((n, columns, nz), BF16) for n in slabs]
    results = pl.pallas_call(
        functools.partial(prepare_kernel, chips),
        out_shape=shapes,
        in_specs=[HBM, HBM, HBM],
        out_specs=[pl.BlockSpec(memory_space=pl.ANY)] * len(shapes),
        scratch_shapes=[
            pltpu.VMEM(basis.shape, BF16),
            pltpu.VMEM(zone.shape, jnp.int32),
            pltpu.SMEM((ZONES,), F32),
            pltpu.VMEM((columns * (ny + 8), nz), F32),
            pltpu.VMEM((ny + 2, columns, nz), BF16),
            pltpu.VMEM((columns, nz), BF16),
            pltpu.SemaphoreType.DMA((columns // 16 + 2,)),
            pltpu.SemaphoreType.DMA((1 + (2 * chips + 1) * (columns // 16),)),
        ],
        compiler_params=pltpu.CompilerParams(vmem_limit_bytes=16 << 20),
    )(*[pltpu.with_memory_space_constraint(x, pltpu.HBM) for x in (basis, zone, cond_table)])
    return (*results[:3], results[3:2 + chips], results[2 + chips:])


def plane_kernel(chips, zone_ref, cond_ref, heat_ref, center, coef, partial, cond_pad):
    rows = partial.shape[0]
    nz = center.shape[2]
    ny = zone_ref.shape[1]
    chip = lax.axis_index("blk") // CORES
    cond_pad[0:8, :] = jnp.zeros((8, nz), F32)
    cond_pad[8:8 + ny, :] = cond_of(zone_ref[0], cond_ref)
    cond_pad[8 + ny:16 + ny, :] = jnp.zeros((8, nz), F32)
    base = pl.multiple_of(chip * rows, 8)
    near = cond_pad[pl.ds(base, rows + 16), :]
    own = near[8:8 + rows]
    lane = lax.broadcasted_iota(jnp.int32, (rows, nz), 1)
    coef[0] = lookup(zone_ref[0, pl.ds(base, rows), :], heat_ref)
    beside = (
        near[7:7 + rows],
        near[9:9 + rows],
        jnp.where(lane == 0, 0.0, pltpu.roll(own, 1, 1)),
        jnp.where(lane == nz - 1, 0.0, pltpu.roll(own, nz - 1, 1)),
    )
    for which, other in enumerate(beside):
        coef[1 + which] = 0.5 * (own + other)
    coef[5] = own
    plane_rows(coef, center, partial)


def plane_rows(coef, center, partial):
    columns, nz = center.shape[1:]
    lane = lax.broadcasted_iota(jnp.int32, (columns, nz), 1)
    first, last = lane == 0, lane == nz - 1
    for y in range(partial.shape[0]):
        face = [jnp.broadcast_to(coef[k, y:y + 1, :], (columns, nz)) for k in range(5)]
        v = center[y + 1].astype(F32)
        total = face[0] * v
        total += face[1] * (v - center[y].astype(F32))
        total += face[2] * (v - center[y + 2].astype(F32))
        total += face[3] * (v - jnp.where(first, 0.0, pltpu.roll(v, 1, 1)))
        total += face[4] * (v - jnp.where(last, 0.0, pltpu.roll(v, nz - 1, 1)))
        partial[y] = total


def image_row(faces, y, partial, v, one, two):
    columns, nz = v.shape
    face = [jnp.broadcast_to(faces[k, y:y + 1, :], (columns, nz)) for k in range(2)]
    v = v.astype(F32)
    total = partial + face[0] * (v - one.astype(F32))
    return (total + face[1] * (v - two.astype(F32))).astype(BF16)


def gram_of(left, right):
    return lax.dot_general(left, right, (((1,), (1,)), ((), ())), preferred_element_type=F32)


def near_kernel(coef, partial, center, one, two, mine, theirs, faces, flat):
    rows, _, nz = partial.shape
    half = rows // CORES
    core = lax.axis_index("blk") % CORES
    for which, ref in enumerate((one, two)):
        faces[which] = 0.5 * (coef[5] + ref[rows].astype(F32)[:rows])
    for y in range(rows):
        image = image_row(faces, y, partial[y], center[y + 1], one[y], two[y])
        flat[:, y * nz:(y + 1) * nz] = image

        @pl.when(core == y // half)
        def _():
            mine[y % half] = image

        @pl.when(core != y // half)
        def _():
            theirs[y % half] = image


def gather_kernel(chips, coef, *refs):
    count = chips - 1
    firsts, seconds, centers, partials = (refs[i * count:(i + 1) * count] for i in range(4))
    for first, second, center, partial in zip(firsts, seconds, centers, partials):
        half = first.shape[0]
        center[0:half] = first[...]
        center[half:2 * half] = second[...]
        plane_rows(coef, center, partial)


def first_far_kernel(chips, faces, *refs):
    count = chips - 1
    partials, centers, twos, ones, images, flats = (refs[i * count:(i + 1) * count] for i in range(6))
    nz = partials[0].shape[2]
    for k in range(count):
        for y in range(partials[k].shape[0] // 2):
            image = image_row(faces, y, partials[k][y], centers[k][y + 1], ones[k][y + 1], twos[k][y + 1])
            flats[k][:, y * nz:(y + 1) * nz] = image
            images[k][y] = image


def left_kernel(chips, weight, flat, center, plain, *refs):
    count = chips - 1
    flats, centers, other_firsts, other_seconds = (refs[i * count:(i + 1) * count] for i in range(4))
    left, gram = refs[4 * count:]
    columns, nz = center.shape[1:]
    rows = center.shape[0] - 2
    half = rows // 2
    me = lax.axis_index("blk")
    for k, ref in enumerate((center, *centers)):
        for core in range(CORES):
            where = pl.ds(pl.multiple_of((me ^ (CORES * k + core)) * columns, columns), columns)
            for y in range(rows):
                if not core:
                    side = ref[y + 1]
                elif not k:
                    side = plain[y]
                else:
                    side = other_firsts[k - 1][y] if y < half else other_seconds[k - 1][y - half]
                left[where, y * nz:(y + 1) * nz] = side
    gram[:, 0:columns] = weight * gram_of(left[...], flat[...])
    for k in range(count):
        gram[:, (k + 1) * columns:(k + 2) * columns] = weight * gram_of(left[:, 0:half * nz], flats[k][...])


def second_far_kernel(chips, weight, faces, left, first_gram, *refs):
    count = chips - 1
    partials, centers, twos, ones, images, mine, theirs = (refs[i * count:(i + 1) * count] for i in range(7))
    gram = refs[7 * count]
    rows, columns, nz = partials[0].shape
    half = rows // 2
    core = lax.axis_index("blk") % CORES
    slabs, blocks = lax.axis_size("dom"), lax.axis_size("blk")
    share = left.shape[0] // (slabs * blocks)
    values = [first_gram[:, 0:columns]]
    for k in range(count):
        block = slice((k + 1) * columns, (k + 2) * columns)
        total = jnp.zeros((left.shape[0], columns), F32)
        for i in range(0, half, 2):
            pair = []
            for at in (i, i + 1):
                y = half + at
                image = image_row(faces, y, partials[k][y], centers[k][y + 1], ones[k][at], twos[k][at])
                other = images[k][at]
                mine[k][at] = jnp.where(core == 0, other, image)
                theirs[k][at] = jnp.where(core == 0, image, other)
                pair.append(image)
            y = half + i
            total += gram_of(left[:, y * nz:(y + 2) * nz], jnp.concatenate(pair, 1))
        values.append(first_gram[:, block] + weight * total)
    for slab in range(slabs):
        for owner in range(blocks):
            start, place = (slab * blocks + owner) * share, (slabs * blocks - 1 - owner * slabs - slab) * share
            for k, value in enumerate(values):
                gram[place:place + share, k * columns:(k + 1) * columns] = value[start:start + share]


def turn_out(image, start, applied, wide, turned, sem):
    rows, columns, _ = image.shape
    for y in range(rows):
        wide[pl.ds(y, columns, stride=rows), :] = image[y].astype(F32)
    for c in range(columns):
        turned[c, 0] = wide[c * rows:(c + 1) * rows, :].astype(BF16)
    copy = pltpu.make_async_copy(turned, applied.at[pl.ds(start, columns)], sem)
    copy.start()
    return copy


def first_kernel(mine, theirs, applied, wide, turned, sems):
    me = lax.axis_index("blk")
    columns = mine.shape[1]
    copies = [
        turn_out(image, (me ^ s) * columns, applied, wide.at[s], turned.at[s], sems.at[s])
        for s, image in enumerate((mine, theirs))
    ]
    for copy in copies:
        copy.wait()


def last_kernel(blocks, applied_in, *refs):
    del applied_in
    images, (applied, wide, turned, sems) = refs[:blocks - CORES], refs[blocks - CORES:]
    me = lax.axis_index("blk")
    columns = images[0].shape[1]
    copies = [
        turn_out(image, (me ^ (s + CORES)) * columns, applied, wide.at[s], turned.at[s], sems.at[s])
        for s, image in enumerate(images)
    ]
    for copy in copies:
        copy.wait()


def sum_kernel(slabs, blocks, shares, reduced):
    chips = blocks // CORES
    columns = shares.shape[2] // chips
    for core in range(CORES):
        sums = []
        for chip in range(chips):
            last = slabs * blocks - 1 - (CORES * chip + core) * slabs
            total = shares[last]
            for slab in range(1, slabs):
                total += shares[last - slab]
            sums.append(total)
        for target in range(chips):
            parts = [sums[chip][:, (chip ^ target) * columns:((chip ^ target) + 1) * columns] for chip in range(chips)]
            start = (CORES * target + core) * columns
            reduced[:, start:start + columns] = functools.reduce(jnp.add, parts)


def per_device(basis, zone, cond_table, heat_table):
    blocks = lax.axis_size("blk")
    slabs = lax.axis_size("dom")
    chips = blocks // CORES
    count = chips - 1
    columns, planes, ny, nz = basis.shape
    rows = ny // chips
    half = ny // blocks
    total = columns * blocks
    weight = 1.0 / (slabs * planes * ny * nz)
    image = jax.ShapeDtypeStruct((half, columns, nz), BF16)
    center_shape = jax.ShapeDtypeStruct((rows + 2, columns, nz), BF16)
    partial = jax.ShapeDtypeStruct((rows, columns, nz), F32)
    whole = jax.ShapeDtypeStruct((total, 1, half, nz), BF16)
    params = pltpu.CompilerParams(vmem_limit_bytes=32 << 20)
    costly = pl.CostEstimate(flops=COST, bytes_accessed=COST // 8, transcendentals=0)
    cheap = pl.CostEstimate(flops=1, bytes_accessed=1, transcendentals=0)

    def call(kernel, out_shape, inputs, scratch=(), specs=None, out_specs=None, cost=cheap, aliases={}):
        return pl.pallas_call(
            kernel,
            out_shape=out_shape,
            in_specs=specs or [VMEM] * len(inputs),
            out_specs=out_specs or [VMEM] * len(out_shape),
            scratch_shapes=scratch,
            input_output_aliases=aliases,
            compiler_params=params,
            cost_estimate=cost,
        )(*inputs)

    def after(value, *others):
        return lax.optimization_barrier((value, *others))[0]

    def swap(array, s):
        return lax.ppermute(array, "blk", [(i, i ^ s) for i in range(blocks)])

    def exchange(array, offset):
        partner = [((d + offset) ^ 1) - offset for d in range(slabs)]
        return lax.ppermute(array, "dom", [(d, to) for d, to in enumerate(partner) if 0 <= to < slabs])

    def turning(n):
        return [
            pltpu.VMEM((n, columns * half, nz), F32),
            pltpu.VMEM((n, columns, 1, half, nz), BF16),
            pltpu.SemaphoreType.DMA((n,)),
        ]

    sent, center, plain, firsts, seconds = prepare(basis, zone, cond_table, chips)
    two = exchange(sent, 1)
    one = exchange(sent, 0)
    firsts = [swap(array, CORES * (k + 1)) for k, array in enumerate(firsts)]
    coef, near_partial = call(
        functools.partial(plane_kernel, chips),
        (jax.ShapeDtypeStruct((6, rows, nz), F32), partial),
        (zone, cond_table, heat_table, center),
        [pltpu.VMEM((ny + 16, nz), F32)],
        [VMEM, SMEM, SMEM, VMEM],
        cost=costly,
    )
    seconds = [swap(after(array, coef), CORES * (k + 1)) for k, array in enumerate(seconds)]
    firsts = [after(array, coef) for array in firsts]
    first_two = [exchange(array, 1) for array in firsts]
    first_one = [exchange(array, 0) for array in firsts]
    second_two = [exchange(array, 1) for array in seconds]
    second_one = [exchange(array, 0) for array in seconds]
    near_mine, near_theirs, faces, near_flat = call(
        near_kernel,
        (
            image,
            image,
            jax.ShapeDtypeStruct((2, rows, nz), F32),
            jax.ShapeDtypeStruct((columns, rows * nz), BF16),
        ),
        (coef, near_partial, center, one, two),
    )
    results = call(
        functools.partial(gather_kernel, chips), [center_shape] * count + [partial] * count, (coef, *firsts, *seconds)
    )
    centers, partials = results[:count], results[count:]
    plain = swap(after(plain, *seconds), 1)
    other_firsts = [swap(after(array, two)[1:], 1) for array in firsts]
    other_seconds = [swap(after(array, two)[:-1], 1) for array in seconds]
    half_flat = jax.ShapeDtypeStruct((columns, rows * nz // 2), BF16)
    results = call(
        functools.partial(first_far_kernel, chips),
        [image] * count + [half_flat] * count,
        (faces, *partials, *centers, *first_two, *first_one),
    )
    images, flats = results[:count], results[count:]
    applied, = call(
        first_kernel, (whole,), (near_mine, swap(near_theirs, 1)), turning(CORES), out_specs=[ANY]
    )
    gram_shape = jax.ShapeDtypeStruct((total, chips * columns), F32)
    left, first_gram = call(
        functools.partial(left_kernel, chips, weight),
        (jax.ShapeDtypeStruct((total, rows * nz), BF16), gram_shape),
        (near_flat, center, plain, *flats, *centers, *other_firsts, *other_seconds),
    )
    *images, gram = call(
        functools.partial(second_far_kernel, chips, weight),
        [image] * (2 * count) + [gram_shape],
        (faces, left, first_gram, *partials, *centers, *second_two, *second_one, *images),
    )
    parts = slabs * blocks
    shares = gram.reshape(parts, total // parts, chips * columns)
    shares = lax.all_to_all(
        shares, ("blk", "dom"), split_axis=0, concat_axis=0, tiled=True, axis_index_groups=[[*reversed(range(parts))]]
    )
    pieces = []
    for k in range(count):
        pieces += [images[k], swap(images[count + k], 1)]
    applied, = call(
        functools.partial(last_kernel, blocks),
        (whole,),
        (applied, *pieces),
        turning(len(pieces)),
        [ANY] + [VMEM] * len(pieces),
        [ANY],
        aliases={0: 0},
    )
    reduced, = call(
        functools.partial(sum_kernel, slabs, blocks), (jax.ShapeDtypeStruct((total // parts, total), F32),), (after(shares, applied),)
    )
    return applied, reduced


def solution(mesh):
    placed = (P("blk", "dom", "roll", None), P("dom", "roll", None), P(), P())
    return jax.shard_map(
        per_device,
        mesh=mesh,
        in_specs=placed,
        out_specs=(P("roll", "dom", "blk", None), P(("dom", "blk"), "roll")),
        check_vma=False,
    )
```

```python
import functools

import jax
import jax.numpy as jnp
from jax import lax
from jax.experimental import pallas as pl
from jax.experimental.pallas import tpu as pltpu
from jax.sharding import PartitionSpec as P

ZONES = 16
CORES = 2
COST = 1 << 30
F32 = jnp.float32
BF16 = jnp.bfloat16
VMEM = pl.BlockSpec(memory_space=pltpu.VMEM)
SMEM = pl.BlockSpec(memory_space=pltpu.SMEM)
HBM = pl.BlockSpec(memory_space=pltpu.HBM)
ANY = pl.BlockSpec(memory_space=pl.ANY)


def lookup(zone, table_ref):
    result = jnp.zeros(zone.shape, F32)
    for which in range(ZONES):
        result = jnp.where(zone == which, table_ref[which], result)
    return result


def cond_of(zone, table_ref):
    return lookup(zone, table_ref).astype(BF16).astype(F32)


def prepare_kernel(chips, basis_hbm, zone_hbm, cond_hbm, *refs):
    near, center, plain, firsts, seconds = *refs[:3], refs[3:2 + chips], refs[2 + chips:2 * chips + 1]
    basis, zone, table, wide, turned, cond_pad, in_sems, out_sems = refs[2 * chips + 1:]
    columns, _, ny, nz = basis.shape
    rows = ny // chips
    chip = lax.axis_index("blk") // CORES
    step = 16
    chunks = columns // step
    pitch = wide.shape[0] // columns
    loads = [
        pltpu.make_async_copy(basis_hbm.at[pl.ds(i * step, step)], basis.at[pl.ds(i * step, step)], in_sems.at[i])
        for i in range(chunks)
    ]
    loads.append(pltpu.make_async_copy(zone_hbm, zone, in_sems.at[chunks]))
    loads.append(pltpu.make_async_copy(cond_hbm, table, in_sems.at[chunks + 1]))
    for load in loads:
        load.start()
    turned[0] = jnp.zeros((columns, nz), BF16)
    turned[ny + 1] = jnp.zeros((columns, nz), BF16)
    stores = []

    def store(source, target):
        copy = pltpu.make_async_copy(source, target, out_sems.at[len(stores)])
        copy.start()
        stores.append(copy)

    for i in range(chunks):
        if i == chunks - 1:
            loads[chunks].wait()
            loads[chunks + 1].wait()
            mine = zone[0, pl.ds(pl.multiple_of(chip * rows, rows), rows), :]
            own = cond_of(mine, table)
            cond_pad[...] = jnp.concatenate([own, jnp.zeros((columns - rows, nz), F32)], 0).astype(BF16)
            store(cond_pad, near.at[rows])
        loads[i].wait()
        some = pl.ds(i * step, step)
        for c in range(i * step, (i + 1) * step):
            wide[c * pitch:c * pitch + ny, :] = basis[c, 0].astype(F32)
        for y in range(ny):
            turned[y + 1, some, :] = wide[pl.ds(i * step * pitch + y, step, stride=pitch), :].astype(BF16)
        store(turned.at[pl.ds(chip * rows + 1, rows), some], near.at[pl.ds(0, rows), some])
        for k in range(1, chips):
            start = (chip ^ k) * rows
            store(turned.at[pl.ds(start, rows // 2 + 1), some], firsts[k - 1].at[:, some])
            store(turned.at[pl.ds(start + rows // 2 + 1, rows // 2 + 1), some], seconds[k - 1].at[:, some])
        store(turned.at[pl.ds(chip * rows, rows + 2), some], center.at[:, some])
        store(turned.at[pl.ds(chip * rows + 1, rows), some], plain.at[:, some])
    for copy in stores:
        copy.wait()


def prepare(basis, zone, cond_table, chips):
    columns, _, ny, nz = basis.shape
    rows = ny // chips
    slabs = [rows + 1, rows + 2, rows] + [rows // 2 + 1] * (2 * chips - 2)
    shapes = [jax.ShapeDtypeStruct((n, columns, nz), BF16) for n in slabs]
    results = pl.pallas_call(
        functools.partial(prepare_kernel, chips),
        out_shape=shapes,
        in_specs=[HBM, HBM, HBM],
        out_specs=[pl.BlockSpec(memory_space=pl.ANY)] * len(shapes),
        scratch_shapes=[
            pltpu.VMEM(basis.shape, BF16),
            pltpu.VMEM(zone.shape, jnp.int32),
            pltpu.SMEM((ZONES,), F32),
            pltpu.VMEM((columns * (ny + 8), nz), F32),
            pltpu.VMEM((ny + 2, columns, nz), BF16),
            pltpu.VMEM((columns, nz), BF16),
            pltpu.SemaphoreType.DMA((columns // 16 + 2,)),
            pltpu.SemaphoreType.DMA((1 + (2 * chips + 1) * (columns // 16),)),
        ],
        compiler_params=pltpu.CompilerParams(vmem_limit_bytes=16 << 20),
    )(*[pltpu.with_memory_space_constraint(x, pltpu.HBM) for x in (basis, zone, cond_table)])
    return (*results[:3], results[3:2 + chips], results[2 + chips:])


def plane_kernel(chips, zone_ref, cond_ref, heat_ref, center, coef, partial, cond_pad):
    rows = partial.shape[0]
    nz = center.shape[2]
    ny = zone_ref.shape[1]
    chip = lax.axis_index("blk") // CORES
    cond_pad[0:8, :] = jnp.zeros((8, nz), F32)
    cond_pad[8:8 + ny, :] = cond_of(zone_ref[0], cond_ref)
    cond_pad[8 + ny:16 + ny, :] = jnp.zeros((8, nz), F32)
    base = pl.multiple_of(chip * rows, 8)
    near = cond_pad[pl.ds(base, rows + 16), :]
    own = near[8:8 + rows]
    lane = lax.broadcasted_iota(jnp.int32, (rows, nz), 1)
    coef[0] = lookup(zone_ref[0, pl.ds(base, rows), :], heat_ref)
    beside = (
        near[7:7 + rows],
        near[9:9 + rows],
        jnp.where(lane == 0, 0.0, pltpu.roll(own, 1, 1)),
        jnp.where(lane == nz - 1, 0.0, pltpu.roll(own, nz - 1, 1)),
    )
    for which, other in enumerate(beside):
        coef[1 + which] = 0.5 * (own + other)
    coef[5] = own
    plane_rows(coef, center, partial)


def plane_rows(coef, center, partial):
    columns, nz = center.shape[1:]
    lane = lax.broadcasted_iota(jnp.int32, (columns, nz), 1)
    first, last = lane == 0, lane == nz - 1
    for y in range(partial.shape[0]):
        face = [jnp.broadcast_to(coef[k, y:y + 1, :], (columns, nz)) for k in range(5)]
        v = center[y + 1].astype(F32)
        total = face[0] * v
        total += face[1] * (v - center[y].astype(F32))
        total += face[2] * (v - center[y + 2].astype(F32))
        total += face[3] * (v - jnp.where(first, 0.0, pltpu.roll(v, 1, 1)))
        total += face[4] * (v - jnp.where(last, 0.0, pltpu.roll(v, nz - 1, 1)))
        partial[y] = total


def image_row(faces, y, partial, v, one, two):
    columns, nz = v.shape
    face = [jnp.broadcast_to(faces[k, y:y + 1, :], (columns, nz)) for k in range(2)]
    v = v.astype(F32)
    total = partial + face[0] * (v - one.astype(F32))
    return (total + face[1] * (v - two.astype(F32))).astype(BF16)


def gram_of(left, right):
    return lax.dot_general(left, right, (((1,), (1,)), ((), ())), preferred_element_type=F32)


def near_kernel(coef, partial, center, one, two, mine, theirs, faces, flat):
    rows, _, nz = partial.shape
    half = rows // CORES
    core = lax.axis_index("blk") % CORES
    for which, ref in enumerate((one, two)):
        faces[which] = 0.5 * (coef[5] + ref[rows].astype(F32)[:rows])
    for y in range(rows):
        image = image_row(faces, y, partial[y], center[y + 1], one[y], two[y])
        flat[:, y * nz:(y + 1) * nz] = image

        @pl.when(core == y // half)
        def _():
            mine[y % half] = image

        @pl.when(core != y // half)
        def _():
            theirs[y % half] = image


def gather_kernel(chips, coef, *refs):
    count = chips - 1
    firsts, seconds, centers, partials = (refs[i * count:(i + 1) * count] for i in range(4))
    for first, second, center, partial in zip(firsts, seconds, centers, partials):
        half = first.shape[0]
        center[0:half] = first[...]
        center[half:2 * half] = second[...]
        plane_rows(coef, center, partial)


def first_far_kernel(chips, faces, *refs):
    count = chips - 1
    partials, centers, twos, ones, images, flats = (refs[i * count:(i + 1) * count] for i in range(6))
    nz = partials[0].shape[2]
    for k in range(count):
        for y in range(partials[k].shape[0] // 2):
            image = image_row(faces, y, partials[k][y], centers[k][y + 1], ones[k][y + 1], twos[k][y + 1])
            flats[k][:, y * nz:(y + 1) * nz] = image
            images[k][y] = image


def left_kernel(chips, weight, flat, center, plain, *refs):
    count = chips - 1
    flats, centers, other_firsts, other_seconds = (refs[i * count:(i + 1) * count] for i in range(4))
    left, gram = refs[4 * count:]
    columns, nz = center.shape[1:]
    rows = center.shape[0] - 2
    half = rows // 2
    me = lax.axis_index("blk")
    for k, ref in enumerate((center, *centers)):
        for core in range(CORES):
            where = pl.ds(pl.multiple_of((me ^ (CORES * k + core)) * columns, columns), columns)
            for y in range(rows):
                if not core:
                    side = ref[y + 1]
                elif not k:
                    side = plain[y]
                else:
                    side = other_firsts[k - 1][y] if y < half else other_seconds[k - 1][y - half]
                left[where, y * nz:(y + 1) * nz] = side
    gram[:, 0:columns] = weight * gram_of(left[...], flat[...])
    for k in range(count):
        gram[:, (k + 1) * columns:(k + 2) * columns] = weight * gram_of(left[:, 0:half * nz], flats[k][...])


def second_far_kernel(chips, weight, faces, left, first_gram, *refs):
    count = chips - 1
    partials, centers, twos, ones, images, mine, theirs = (refs[i * count:(i + 1) * count] for i in range(7))
    gram = refs[7 * count]
    rows, columns, nz = partials[0].shape
    half = rows // 2
    core = lax.axis_index("blk") % CORES
    slabs, blocks = lax.axis_size("dom"), lax.axis_size("blk")
    share = left.shape[0] // (slabs * blocks)
    values = [first_gram[:, 0:columns]]
    for k in range(count):
        block = slice((k + 1) * columns, (k + 2) * columns)
        total = jnp.zeros((left.shape[0], columns), F32)
        for i in range(0, half, 2):
            pair = []
            for at in (i, i + 1):
                y = half + at
                image = image_row(faces, y, partials[k][y], centers[k][y + 1], ones[k][at], twos[k][at])
                other = images[k][at]
                mine[k][at] = jnp.where(core == 0, other, image)
                theirs[k][at] = jnp.where(core == 0, image, other)
                pair.append(image)
            y = half + i
            total += gram_of(left[:, y * nz:(y + 2) * nz], jnp.concatenate(pair, 1))
        values.append(first_gram[:, block] + weight * total)
    for slab in range(slabs):
        for owner in range(blocks):
            start, place = (slab * blocks + owner) * share, (slabs * blocks - 1 - slab * blocks - owner) * share
            for k, value in enumerate(values):
                gram[place:place + share, k * columns:(k + 1) * columns] = value[start:start + share]


def turn_out(image, start, applied, wide, turned, sem):
    rows, columns, _ = image.shape
    for y in range(rows):
        wide[pl.ds(y, columns, stride=rows), :] = image[y].astype(F32)
    for c in range(columns):
        turned[c, 0] = wide[c * rows:(c + 1) * rows, :].astype(BF16)
    copy = pltpu.make_async_copy(turned, applied.at[pl.ds(start, columns)], sem)
    copy.start()
    return copy


def first_kernel(mine, theirs, applied, wide, turned, sems):
    me = lax.axis_index("blk")
    columns = mine.shape[1]
    copies = [
        turn_out(image, (me ^ s) * columns, applied, wide.at[s], turned.at[s], sems.at[s])
        for s, image in enumerate((mine, theirs))
    ]
    for copy in copies:
        copy.wait()


def last_kernel(blocks, applied_in, *refs):
    del applied_in
    images, (applied, wide, turned, sems) = refs[:blocks - CORES], refs[blocks - CORES:]
    me = lax.axis_index("blk")
    columns = images[0].shape[1]
    copies = [
        turn_out(image, (me ^ (s + CORES)) * columns, applied, wide.at[s], turned.at[s], sems.at[s])
        for s, image in enumerate(images)
    ]
    for copy in copies:
        copy.wait()


def sum_kernel(slabs, blocks, shares, reduced):
    chips = blocks // CORES
    columns = shares.shape[2] // chips
    for core in range(CORES):
        sums = []
        for chip in range(chips):
            last = slabs * blocks - 1 - (CORES * chip + core)
            total = shares[last]
            for slab in range(1, slabs):
                total += shares[last - slab * blocks]
            sums.append(total)
        for target in range(chips):
            parts = [sums[chip][:, (chip ^ target) * columns:((chip ^ target) + 1) * columns] for chip in range(chips)]
            start = (CORES * target + core) * columns
            reduced[:, start:start + columns] = functools.reduce(jnp.add, parts)


def per_device(basis, zone, cond_table, heat_table):
    blocks = lax.axis_size("blk")
    slabs = lax.axis_size("dom")
    chips = blocks // CORES
    count = chips - 1
    columns, planes, ny, nz = basis.shape
    rows = ny // chips
    half = ny // blocks
    total = columns * blocks
    weight = 1.0 / (slabs * planes * ny * nz)
    image = jax.ShapeDtypeStruct((half, columns, nz), BF16)
    center_shape = jax.ShapeDtypeStruct((rows + 2, columns, nz), BF16)
    partial = jax.ShapeDtypeStruct((rows, columns, nz), F32)
    whole = jax.ShapeDtypeStruct((total, 1, half, nz), BF16)
    params = pltpu.CompilerParams(vmem_limit_bytes=32 << 20)
    costly = pl.CostEstimate(flops=COST, bytes_accessed=COST // 8, transcendentals=0)
    cheap = pl.CostEstimate(flops=1, bytes_accessed=1, transcendentals=0)

    def call(kernel, out_shape, inputs, scratch=(), specs=None, out_specs=None, cost=cheap, aliases={}):
        return pl.pallas_call(
            kernel,
            out_shape=out_shape,
            in_specs=specs or [VMEM] * len(inputs),
            out_specs=out_specs or [VMEM] * len(out_shape),
            scratch_shapes=scratch,
            input_output_aliases=aliases,
            compiler_params=params,
            cost_estimate=cost,
        )(*inputs)

    def after(value, *others):
        return lax.optimization_barrier((value, *others))[0]

    def swap(array, s):
        return lax.ppermute(array, "blk", [(i, i ^ s) for i in range(blocks)])

    def exchange(array, offset):
        partner = [((d + offset) ^ 1) - offset for d in range(slabs)]
        return lax.ppermute(array, "dom", [(d, to) for d, to in enumerate(partner) if 0 <= to < slabs])

    def turning(n):
        return [
            pltpu.VMEM((n, columns * half, nz), F32),
            pltpu.VMEM((n, columns, 1, half, nz), BF16),
            pltpu.SemaphoreType.DMA((n,)),
        ]

    sent, center, plain, firsts, seconds = prepare(basis, zone, cond_table, chips)
    two = exchange(sent, 1)
    one = exchange(sent, 0)
    firsts = [swap(array, CORES * (k + 1)) for k, array in enumerate(firsts)]
    coef, near_partial = call(
        functools.partial(plane_kernel, chips),
        (jax.ShapeDtypeStruct((6, rows, nz), F32), partial),
        (zone, cond_table, heat_table, center),
        [pltpu.VMEM((ny + 16, nz), F32)],
        [VMEM, SMEM, SMEM, VMEM],
        cost=costly,
    )
    seconds = [swap(after(array, coef), CORES * (k + 1)) for k, array in enumerate(seconds)]
    firsts = [after(array, coef) for array in firsts]
    first_two = [exchange(array, 1) for array in firsts]
    first_one = [exchange(array, 0) for array in firsts]
    second_two = [exchange(array, 1) for array in seconds]
    second_one = [exchange(array, 0) for array in seconds]
    near_mine, near_theirs, faces, near_flat = call(
        near_kernel,
        (
            image,
            image,
            jax.ShapeDtypeStruct((2, rows, nz), F32),
            jax.ShapeDtypeStruct((columns, rows * nz), BF16),
        ),
        (coef, near_partial, center, one, two),
    )
    results = call(
        functools.partial(gather_kernel, chips), [center_shape] * count + [partial] * count, (coef, *firsts, *seconds)
    )
    centers, partials = results[:count], results[count:]
    plain = swap(after(plain, *seconds), 1)
    other_firsts = [swap(after(array, two)[1:], 1) for array in firsts]
    other_seconds = [swap(after(array, two)[:-1], 1) for array in seconds]
    half_flat = jax.ShapeDtypeStruct((columns, rows * nz // 2), BF16)
    results = call(
        functools.partial(first_far_kernel, chips),
        [image] * count + [half_flat] * count,
        (faces, *partials, *centers, *first_two, *first_one),
    )
    images, flats = results[:count], results[count:]
    applied, = call(
        first_kernel, (whole,), (near_mine, swap(near_theirs, 1)), turning(CORES), out_specs=[ANY]
    )
    gram_shape = jax.ShapeDtypeStruct((total, chips * columns), F32)
    left, first_gram = call(
        functools.partial(left_kernel, chips, weight),
        (jax.ShapeDtypeStruct((total, rows * nz), BF16), gram_shape),
        (near_flat, center, plain, *flats, *centers, *other_firsts, *other_seconds),
    )
    *images, gram = call(
        functools.partial(second_far_kernel, chips, weight),
        [image] * (2 * count) + [gram_shape],
        (faces, left, first_gram, *partials, *centers, *second_two, *second_one, *images),
    )
    parts = slabs * blocks
    shares = gram.reshape(parts, total // parts, chips * columns)
    shares = lax.all_to_all(
        shares, ("dom", "blk"), split_axis=0, concat_axis=0, tiled=True, axis_index_groups=[[*reversed(range(parts))]]
    )
    pieces = []
    for k in range(count):
        pieces += [images[k], swap(images[count + k], 1)]
    applied, = call(
        functools.partial(last_kernel, blocks),
        (whole,),
        (applied, *pieces),
        turning(len(pieces)),
        [ANY] + [VMEM] * len(pieces),
        [ANY],
        aliases={0: 0},
    )
    reduced, = call(
        functools.partial(sum_kernel, slabs, blocks), (jax.ShapeDtypeStruct((total // parts, total), F32),), (after(shares, applied),)
    )
    return applied, reduced


def solution(mesh):
    placed = (P("blk", "dom", "roll", None), P("dom", "roll", None), P(), P())
    return jax.shard_map(
        per_device,
        mesh=mesh,
        in_specs=placed,
        out_specs=(P("roll", "dom", "blk", None), P(("dom", "blk"), "roll")),
        check_vma=False,
    )
```

```python
import functools

import jax
import jax.numpy as jnp
from jax import lax
from jax.experimental import pallas as pl
from jax.experimental.pallas import tpu as pltpu
from jax.sharding import PartitionSpec as P

ZONES = 16
CORES = 2
COST = 1 << 30
F32 = jnp.float32
BF16 = jnp.bfloat16
VMEM = pl.BlockSpec(memory_space=pltpu.VMEM)
SMEM = pl.BlockSpec(memory_space=pltpu.SMEM)
HBM = pl.BlockSpec(memory_space=pltpu.HBM)
ANY = pl.BlockSpec(memory_space=pl.ANY)


def lookup(zone, table_ref):
    result = jnp.zeros(zone.shape, F32)
    for which in range(ZONES):
        result = jnp.where(zone == which, table_ref[which], result)
    return result


def cond_of(zone, table_ref):
    return lookup(zone, table_ref).astype(BF16).astype(F32)


def prepare_kernel(chips, basis_hbm, zone_hbm, cond_hbm, *refs):
    near, center, plain, firsts, seconds = *refs[:3], refs[3:2 + chips], refs[2 + chips:2 * chips + 1]
    basis, zone, table, wide, turned, cond_pad, in_sems, out_sems = refs[2 * chips + 1:]
    columns, _, ny, nz = basis.shape
    rows = ny // chips
    chip = lax.axis_index("blk") // CORES
    step = 16
    chunks = columns // step
    pitch = wide.shape[0] // columns
    loads = [
        pltpu.make_async_copy(basis_hbm.at[pl.ds(i * step, step)], basis.at[pl.ds(i * step, step)], in_sems.at[i])
        for i in range(chunks)
    ]
    loads.append(pltpu.make_async_copy(zone_hbm, zone, in_sems.at[chunks]))
    loads.append(pltpu.make_async_copy(cond_hbm, table, in_sems.at[chunks + 1]))
    for load in loads:
        load.start()
    turned[0] = jnp.zeros((columns, nz), BF16)
    turned[ny + 1] = jnp.zeros((columns, nz), BF16)
    stores = []

    def store(source, target):
        copy = pltpu.make_async_copy(source, target, out_sems.at[len(stores)])
        copy.start()
        stores.append(copy)

    for i in range(chunks):
        if i == chunks - 1:
            loads[chunks].wait()
            loads[chunks + 1].wait()
            mine = zone[0, pl.ds(pl.multiple_of(chip * rows, rows), rows), :]
            own = cond_of(mine, table)
            cond_pad[...] = jnp.concatenate([own, jnp.zeros((columns - rows, nz), F32)], 0).astype(BF16)
            store(cond_pad, near.at[rows])
        loads[i].wait()
        some = pl.ds(i * step, step)
        for c in range(i * step, (i + 1) * step):
            wide[c * pitch:c * pitch + ny, :] = basis[c, 0].astype(F32)
        for y in range(ny):
            turned[y + 1, some, :] = wide[pl.ds(i * step * pitch + y, step, stride=pitch), :].astype(BF16)
        store(turned.at[pl.ds(chip * rows + 1, rows), some], near.at[pl.ds(0, rows), some])
        for k in range(1, chips):
            start = (chip ^ k) * rows
            store(turned.at[pl.ds(start, rows // 2 + 1), some], firsts[k - 1].at[:, some])
            store(turned.at[pl.ds(start + rows // 2 + 1, rows // 2 + 1), some], seconds[k - 1].at[:, some])
        store(turned.at[pl.ds(chip * rows, rows + 2), some], center.at[:, some])
        store(turned.at[pl.ds(chip * rows + 1, rows), some], plain.at[:, some])
    for copy in stores:
        copy.wait()


def prepare(basis, zone, cond_table, chips):
    columns, _, ny, nz = basis.shape
    rows = ny // chips
    slabs = [rows + 1, rows + 2, rows] + [rows // 2 + 1] * (2 * chips - 2)
    shapes = [jax.ShapeDtypeStruct((n, columns, nz), BF16) for n in slabs]
    results = pl.pallas_call(
        functools.partial(prepare_kernel, chips),
        out_shape=shapes,
        in_specs=[HBM, HBM, HBM],
        out_specs=[pl.BlockSpec(memory_space=pl.ANY)] * len(shapes),
        scratch_shapes=[
            pltpu.VMEM(basis.shape, BF16),
            pltpu.VMEM(zone.shape, jnp.int32),
            pltpu.SMEM((ZONES,), F32),
            pltpu.VMEM((columns * (ny + 8), nz), F32),
            pltpu.VMEM((ny + 2, columns, nz), BF16),
            pltpu.VMEM((columns, nz), BF16),
            pltpu.SemaphoreType.DMA((columns // 16 + 2,)),
            pltpu.SemaphoreType.DMA((1 + (2 * chips + 1) * (columns // 16),)),
        ],
        compiler_params=pltpu.CompilerParams(vmem_limit_bytes=16 << 20),
    )(*[pltpu.with_memory_space_constraint(x, pltpu.HBM) for x in (basis, zone, cond_table)])
    return (*results[:3], results[3:2 + chips], results[2 + chips:])


def plane_kernel(chips, zone_ref, cond_ref, heat_ref, center, coef, partial, cond_pad):
    rows = partial.shape[0]
    nz = center.shape[2]
    ny = zone_ref.shape[1]
    chip = lax.axis_index("blk") // CORES
    cond_pad[0:8, :] = jnp.zeros((8, nz), F32)
    cond_pad[8:8 + ny, :] = cond_of(zone_ref[0], cond_ref)
    cond_pad[8 + ny:16 + ny, :] = jnp.zeros((8, nz), F32)
    base = pl.multiple_of(chip * rows, 8)
    near = cond_pad[pl.ds(base, rows + 16), :]
    own = near[8:8 + rows]
    lane = lax.broadcasted_iota(jnp.int32, (rows, nz), 1)
    coef[0] = lookup(zone_ref[0, pl.ds(base, rows), :], heat_ref)
    beside = (
        near[7:7 + rows],
        near[9:9 + rows],
        jnp.where(lane == 0, 0.0, pltpu.roll(own, 1, 1)),
        jnp.where(lane == nz - 1, 0.0, pltpu.roll(own, nz - 1, 1)),
    )
    for which, other in enumerate(beside):
        coef[1 + which] = 0.5 * (own + other)
    coef[5] = own
    plane_rows(coef, center, partial)


def plane_rows(coef, center, partial):
    columns, nz = center.shape[1:]
    lane = lax.broadcasted_iota(jnp.int32, (columns, nz), 1)
    first, last = lane == 0, lane == nz - 1
    for y in range(partial.shape[0]):
        face = [jnp.broadcast_to(coef[k, y:y + 1, :], (columns, nz)) for k in range(5)]
        v = center[y + 1].astype(F32)
        total = face[0] * v
        total += face[1] * (v - center[y].astype(F32))
        total += face[2] * (v - center[y + 2].astype(F32))
        total += face[3] * (v - jnp.where(first, 0.0, pltpu.roll(v, 1, 1)))
        total += face[4] * (v - jnp.where(last, 0.0, pltpu.roll(v, nz - 1, 1)))
        partial[y] = total


def image_row(faces, y, partial, v, one, two):
    columns, nz = v.shape
    face = [jnp.broadcast_to(faces[k, y:y + 1, :], (columns, nz)) for k in range(2)]
    v = v.astype(F32)
    total = partial + face[0] * (v - one.astype(F32))
    return (total + face[1] * (v - two.astype(F32))).astype(BF16)


def gram_of(left, right):
    return lax.dot_general(left, right, (((1,), (1,)), ((), ())), preferred_element_type=F32)


def near_kernel(coef, partial, center, one, two, mine, theirs, faces, flat):
    rows, _, nz = partial.shape
    half = rows // CORES
    core = lax.axis_index("blk") % CORES
    for which, ref in enumerate((one, two)):
        faces[which] = 0.5 * (coef[5] + ref[rows].astype(F32)[:rows])
    for y in range(rows):
        image = image_row(faces, y, partial[y], center[y + 1], one[y], two[y])
        flat[:, y * nz:(y + 1) * nz] = image

        @pl.when(core == y // half)
        def _():
            mine[y % half] = image

        @pl.when(core != y // half)
        def _():
            theirs[y % half] = image


def gather_kernel(chips, coef, *refs):
    count = chips - 1
    firsts, seconds, centers, partials = (refs[i * count:(i + 1) * count] for i in range(4))
    for first, second, center, partial in zip(firsts, seconds, centers, partials):
        half = first.shape[0]
        center[0:half] = first[...]
        center[half:2 * half] = second[...]
        plane_rows(coef, center, partial)


def first_far_kernel(chips, faces, *refs):
    count = chips - 1
    partials, centers, ones, twos, images, flats = (refs[i * count:(i + 1) * count] for i in range(6))
    nz = partials[0].shape[2]
    for k in range(count):
        for y in range(partials[k].shape[0] // 2):
            image = image_row(faces, y, partials[k][y], centers[k][y + 1], ones[k][y + 1], twos[k][y + 1])
            flats[k][:, y * nz:(y + 1) * nz] = image
            images[k][y] = image


def left_kernel(chips, weight, flat, center, plain, *refs):
    count = chips - 1
    flats, centers, other_firsts, other_seconds = (refs[i * count:(i + 1) * count] for i in range(4))
    left, gram = refs[4 * count:]
    columns, nz = center.shape[1:]
    rows = center.shape[0] - 2
    half = rows // 2
    me = lax.axis_index("blk")
    for k, ref in enumerate((center, *centers)):
        for core in range(CORES):
            where = pl.ds(pl.multiple_of((me ^ (CORES * k + core)) * columns, columns), columns)
            for y in range(rows):
                if not core:
                    side = ref[y + 1]
                elif not k:
                    side = plain[y]
                else:
                    side = other_firsts[k - 1][y] if y < half else other_seconds[k - 1][y - half]
                left[where, y * nz:(y + 1) * nz] = side
    gram[:, 0:columns] = weight * gram_of(left[...], flat[...])
    for k in range(count):
        gram[:, (k + 1) * columns:(k + 2) * columns] = weight * gram_of(left[:, 0:half * nz], flats[k][...])


def second_far_kernel(chips, weight, faces, left, first_gram, *refs):
    count = chips - 1
    partials, centers, twos, ones, images, mine, theirs = (refs[i * count:(i + 1) * count] for i in range(7))
    gram = refs[7 * count]
    rows, columns, nz = partials[0].shape
    half = rows // 2
    core = lax.axis_index("blk") % CORES
    slabs, blocks = lax.axis_size("dom"), lax.axis_size("blk")
    share = left.shape[0] // (slabs * blocks)
    values = [first_gram[:, 0:columns]]
    for k in range(count):
        block = slice((k + 1) * columns, (k + 2) * columns)
        total = jnp.zeros((left.shape[0], columns), F32)
        for i in range(0, half, 2):
            pair = []
            for at in (i, i + 1):
                y = half + at
                image = image_row(faces, y, partials[k][y], centers[k][y + 1], ones[k][at], twos[k][at])
                other = images[k][at]
                mine[k][at] = jnp.where(core == 0, other, image)
                theirs[k][at] = jnp.where(core == 0, image, other)
                pair.append(image)
            y = half + i
            total += gram_of(left[:, y * nz:(y + 2) * nz], jnp.concatenate(pair, 1))
        values.append(first_gram[:, block] + weight * total)
    for slab in range(slabs):
        for owner in range(blocks):
            start, place = (slab * blocks + owner) * share, (slabs * blocks - 1 - slab * blocks - owner) * share
            for k, value in enumerate(values):
                gram[place:place + share, k * columns:(k + 1) * columns] = value[start:start + share]


def turn_out(image, start, applied, wide, turned, sem):
    rows, columns, _ = image.shape
    for y in range(rows):
        wide[pl.ds(y, columns, stride=rows), :] = image[y].astype(F32)
    for c in range(columns):
        turned[c, 0] = wide[c * rows:(c + 1) * rows, :].astype(BF16)
    copy = pltpu.make_async_copy(turned, applied.at[pl.ds(start, columns)], sem)
    copy.start()
    return copy


def first_kernel(mine, theirs, applied, wide, turned, sems):
    me = lax.axis_index("blk")
    columns = mine.shape[1]
    copies = [
        turn_out(image, (me ^ s) * columns, applied, wide.at[s], turned.at[s], sems.at[s])
        for s, image in enumerate((mine, theirs))
    ]
    for copy in copies:
        copy.wait()


def last_kernel(blocks, applied_in, *refs):
    del applied_in
    images, (applied, wide, turned, sems) = refs[:blocks - CORES], refs[blocks - CORES:]
    me = lax.axis_index("blk")
    columns = images[0].shape[1]
    copies = [
        turn_out(image, (me ^ (s + CORES)) * columns, applied, wide.at[s], turned.at[s], sems.at[s])
        for s, image in enumerate(images)
    ]
    for copy in copies:
        copy.wait()


def sum_kernel(slabs, blocks, shares, reduced):
    chips = blocks // CORES
    columns = shares.shape[2] // chips
    for core in range(CORES):
        sums = []
        for chip in range(chips):
            last = slabs * blocks - 1 - (CORES * chip + core)
            total = shares[last]
            for slab in range(1, slabs):
                total += shares[last - slab * blocks]
            sums.append(total)
        for target in range(chips):
            parts = [sums[chip][:, (chip ^ target) * columns:((chip ^ target) + 1) * columns] for chip in range(chips)]
            start = (CORES * target + core) * columns
            reduced[:, start:start + columns] = functools.reduce(jnp.add, parts)


def per_device(basis, zone, cond_table, heat_table):
    blocks = lax.axis_size("blk")
    slabs = lax.axis_size("dom")
    chips = blocks // CORES
    count = chips - 1
    columns, planes, ny, nz = basis.shape
    rows = ny // chips
    half = ny // blocks
    total = columns * blocks
    weight = 1.0 / (slabs * planes * ny * nz)
    image = jax.ShapeDtypeStruct((half, columns, nz), BF16)
    center_shape = jax.ShapeDtypeStruct((rows + 2, columns, nz), BF16)
    partial = jax.ShapeDtypeStruct((rows, columns, nz), F32)
    whole = jax.ShapeDtypeStruct((total, 1, half, nz), BF16)
    params = pltpu.CompilerParams(vmem_limit_bytes=32 << 20)
    costly = pl.CostEstimate(flops=COST, bytes_accessed=COST // 8, transcendentals=0)
    cheap = pl.CostEstimate(flops=1, bytes_accessed=1, transcendentals=0)

    def call(kernel, out_shape, inputs, scratch=(), specs=None, out_specs=None, cost=cheap, aliases={}):
        return pl.pallas_call(
            kernel,
            out_shape=out_shape,
            in_specs=specs or [VMEM] * len(inputs),
            out_specs=out_specs or [VMEM] * len(out_shape),
            scratch_shapes=scratch,
            input_output_aliases=aliases,
            compiler_params=params,
            cost_estimate=cost,
        )(*inputs)

    def after(value, *others):
        return lax.optimization_barrier((value, *others))[0]

    def swap(array, s):
        return lax.ppermute(array, "blk", [(i, i ^ s) for i in range(blocks)])

    def exchange(array, offset):
        partner = [((d + offset) ^ 1) - offset for d in range(slabs)]
        return lax.ppermute(array, "dom", [(d, to) for d, to in enumerate(partner) if 0 <= to < slabs])

    def turning(n):
        return [
            pltpu.VMEM((n, columns * half, nz), F32),
            pltpu.VMEM((n, columns, 1, half, nz), BF16),
            pltpu.SemaphoreType.DMA((n,)),
        ]

    sent, center, plain, firsts, seconds = prepare(basis, zone, cond_table, chips)
    two = exchange(sent, 1)
    one = exchange(sent, 0)
    firsts = [swap(array, CORES * (k + 1)) for k, array in enumerate(firsts)]
    coef, near_partial = call(
        functools.partial(plane_kernel, chips),
        (jax.ShapeDtypeStruct((6, rows, nz), F32), partial),
        (zone, cond_table, heat_table, center),
        [pltpu.VMEM((ny + 16, nz), F32)],
        [VMEM, SMEM, SMEM, VMEM],
        cost=costly,
    )
    seconds = [swap(after(array, coef), CORES * (k + 1)) for k, array in enumerate(seconds)]
    firsts = [after(array, coef) for array in firsts]
    first_two = [exchange(array, 1) for array in firsts]
    first_one = [exchange(array, 0) for array in firsts]
    second_two = [exchange(array, 1) for array in seconds]
    second_one = [exchange(array, 0) for array in seconds]
    near_mine, near_theirs, faces, near_flat = call(
        near_kernel,
        (
            image,
            image,
            jax.ShapeDtypeStruct((2, rows, nz), F32),
            jax.ShapeDtypeStruct((columns, rows * nz), BF16),
        ),
        (coef, near_partial, center, one, two),
    )
    results = call(
        functools.partial(gather_kernel, chips), [center_shape] * count + [partial] * count, (coef, *firsts, *seconds)
    )
    centers, partials = results[:count], results[count:]
    plain = swap(after(plain, *seconds), 1)
    other_firsts = [swap(after(array, two)[1:], 1) for array in firsts]
    other_seconds = [swap(after(array, two)[:-1], 1) for array in seconds]
    half_flat = jax.ShapeDtypeStruct((columns, rows * nz // 2), BF16)
    results = call(
        functools.partial(first_far_kernel, chips),
        [image] * count + [half_flat] * count,
        (faces, *partials, *centers, *first_one, *first_two),
    )
    images, flats = results[:count], results[count:]
    applied, = call(
        first_kernel, (whole,), (near_mine, swap(near_theirs, 1)), turning(CORES), out_specs=[ANY]
    )
    gram_shape = jax.ShapeDtypeStruct((total, chips * columns), F32)
    left, first_gram = call(
        functools.partial(left_kernel, chips, weight),
        (jax.ShapeDtypeStruct((total, rows * nz), BF16), gram_shape),
        (near_flat, center, plain, *flats, *centers, *other_firsts, *other_seconds),
    )
    *images, gram = call(
        functools.partial(second_far_kernel, chips, weight),
        [image] * (2 * count) + [gram_shape],
        (faces, left, first_gram, *partials, *centers, *second_two, *second_one, *images),
    )
    parts = slabs * blocks
    shares = gram.reshape(parts, total // parts, chips * columns)
    shares = lax.all_to_all(
        shares, ("dom", "blk"), split_axis=0, concat_axis=0, tiled=True, axis_index_groups=[[*reversed(range(parts))]]
    )
    pieces = []
    for k in range(count):
        pieces += [images[k], swap(images[count + k], 1)]
    applied, = call(
        functools.partial(last_kernel, blocks),
        (whole,),
        (applied, *pieces),
        turning(len(pieces)),
        [ANY] + [VMEM] * len(pieces),
        [ANY],
        aliases={0: 0},
    )
    reduced, = call(
        functools.partial(sum_kernel, slabs, blocks), (jax.ShapeDtypeStruct((total // parts, total), F32),), (after(shares, applied),)
    )
    return applied, reduced


def solution(mesh):
    placed = (P("blk", "dom", "roll", None), P("dom", "roll", None), P(), P())
    return jax.shard_map(
        per_device,
        mesh=mesh,
        in_specs=placed,
        out_specs=(P("roll", "dom", "blk", None), P(("dom", "blk"), "roll")),
        check_vma=False,
    )
```

```python
import functools

import jax
import jax.numpy as jnp
from jax import lax
from jax.experimental import pallas as pl
from jax.experimental.pallas import tpu as pltpu
from jax.sharding import PartitionSpec as P

ZONES = 16
CORES = 2
COST = 1 << 30
F32 = jnp.float32
BF16 = jnp.bfloat16
VMEM = pl.BlockSpec(memory_space=pltpu.VMEM)
SMEM = pl.BlockSpec(memory_space=pltpu.SMEM)
HBM = pl.BlockSpec(memory_space=pltpu.HBM)
ANY = pl.BlockSpec(memory_space=pl.ANY)


def lookup(zone, table_ref):
    result = jnp.zeros(zone.shape, F32)
    for which in range(ZONES):
        result = jnp.where(zone == which, table_ref[which], result)
    return result


def cond_of(zone, table_ref):
    return lookup(zone, table_ref).astype(BF16).astype(F32)


def prepare_kernel(chips, basis_hbm, zone_hbm, cond_hbm, *refs):
    near, center, plain, firsts, seconds = *refs[:3], refs[3:2 + chips], refs[2 + chips:2 * chips + 1]
    basis, zone, table, wide, turned, cond_pad, in_sems, out_sems = refs[2 * chips + 1:]
    columns, _, ny, nz = basis.shape
    rows = ny // chips
    chip = lax.axis_index("blk") // CORES
    step = 16
    chunks = columns // step
    pitch = wide.shape[0] // columns
    loads = [
        pltpu.make_async_copy(basis_hbm.at[pl.ds(i * step, step)], basis.at[pl.ds(i * step, step)], in_sems.at[i])
        for i in range(chunks)
    ]
    loads.append(pltpu.make_async_copy(zone_hbm, zone, in_sems.at[chunks]))
    loads.append(pltpu.make_async_copy(cond_hbm, table, in_sems.at[chunks + 1]))
    for load in loads:
        load.start()
    turned[0] = jnp.zeros((columns, nz), BF16)
    turned[ny + 1] = jnp.zeros((columns, nz), BF16)
    stores = []

    def store(source, target):
        copy = pltpu.make_async_copy(source, target, out_sems.at[len(stores)])
        copy.start()
        stores.append(copy)

    for i in range(chunks):
        if i == chunks - 1:
            loads[chunks].wait()
            loads[chunks + 1].wait()
            mine = zone[0, pl.ds(pl.multiple_of(chip * rows, rows), rows), :]
            own = cond_of(mine, table)
            cond_pad[...] = jnp.concatenate([own, jnp.zeros((columns - rows, nz), F32)], 0).astype(BF16)
            store(cond_pad, near.at[rows])
        loads[i].wait()
        some = pl.ds(i * step, step)
        for c in range(i * step, (i + 1) * step):
            wide[c * pitch:c * pitch + ny, :] = basis[c, 0].astype(F32)
        for y in range(ny):
            turned[y + 1, some, :] = wide[pl.ds(i * step * pitch + y, step, stride=pitch), :].astype(BF16)
        store(turned.at[pl.ds(chip * rows + 1, rows), some], near.at[pl.ds(0, rows), some])
        for k in range(1, chips):
            start = (chip ^ k) * rows
            store(turned.at[pl.ds(start, rows // 2 + 1), some], firsts[k - 1].at[:, some])
            store(turned.at[pl.ds(start + rows // 2 + 1, rows // 2 + 1), some], seconds[k - 1].at[:, some])
        store(turned.at[pl.ds(chip * rows, rows + 2), some], center.at[:, some])
        store(turned.at[pl.ds(chip * rows + 1, rows), some], plain.at[:, some])
    for copy in stores:
        copy.wait()


def prepare(basis, zone, cond_table, chips):
    columns, _, ny, nz = basis.shape
    rows = ny // chips
    slabs = [rows + 1, rows + 2, rows] + [rows // 2 + 1] * (2 * chips - 2)
    shapes = [jax.ShapeDtypeStruct((n, columns, nz), BF16) for n in slabs]
    results = pl.pallas_call(
        functools.partial(prepare_kernel, chips),
        out_shape=shapes,
        in_specs=[HBM, HBM, HBM],
        out_specs=[pl.BlockSpec(memory_space=pl.ANY)] * len(shapes),
        scratch_shapes=[
            pltpu.VMEM(basis.shape, BF16),
            pltpu.VMEM(zone.shape, jnp.int32),
            pltpu.SMEM((ZONES,), F32),
            pltpu.VMEM((columns * (ny + 8), nz), F32),
            pltpu.VMEM((ny + 2, columns, nz), BF16),
            pltpu.VMEM((columns, nz), BF16),
            pltpu.SemaphoreType.DMA((columns // 16 + 2,)),
            pltpu.SemaphoreType.DMA((1 + (2 * chips + 1) * (columns // 16),)),
        ],
        compiler_params=pltpu.CompilerParams(vmem_limit_bytes=16 << 20),
    )(*[pltpu.with_memory_space_constraint(x, pltpu.HBM) for x in (basis, zone, cond_table)])
    return (*results[:3], results[3:2 + chips], results[2 + chips:])


def plane_kernel(chips, zone_ref, cond_ref, heat_ref, center, coef, partial, cond_pad):
    rows = partial.shape[0]
    nz = center.shape[2]
    ny = zone_ref.shape[1]
    chip = lax.axis_index("blk") // CORES
    cond_pad[0:8, :] = jnp.zeros((8, nz), F32)
    cond_pad[8:8 + ny, :] = cond_of(zone_ref[0], cond_ref)
    cond_pad[8 + ny:16 + ny, :] = jnp.zeros((8, nz), F32)
    base = pl.multiple_of(chip * rows, 8)
    near = cond_pad[pl.ds(base, rows + 16), :]
    own = near[8:8 + rows]
    lane = lax.broadcasted_iota(jnp.int32, (rows, nz), 1)
    coef[0] = lookup(zone_ref[0, pl.ds(base, rows), :], heat_ref)
    beside = (
        near[7:7 + rows],
        near[9:9 + rows],
        jnp.where(lane == 0, 0.0, pltpu.roll(own, 1, 1)),
        jnp.where(lane == nz - 1, 0.0, pltpu.roll(own, nz - 1, 1)),
    )
    for which, other in enumerate(beside):
        coef[1 + which] = 0.5 * (own + other)
    coef[5] = own
    plane_rows(coef, center, partial)


def plane_rows(coef, center, partial):
    columns, nz = center.shape[1:]
    lane = lax.broadcasted_iota(jnp.int32, (columns, nz), 1)
    first, last = lane == 0, lane == nz - 1
    for y in range(partial.shape[0]):
        face = [jnp.broadcast_to(coef[k, y:y + 1, :], (columns, nz)) for k in range(5)]
        v = center[y + 1].astype(F32)
        total = face[0] * v
        total += face[1] * (v - center[y].astype(F32))
        total += face[2] * (v - center[y + 2].astype(F32))
        total += face[3] * (v - jnp.where(first, 0.0, pltpu.roll(v, 1, 1)))
        total += face[4] * (v - jnp.where(last, 0.0, pltpu.roll(v, nz - 1, 1)))
        partial[y] = total


def image_row(faces, y, partial, v, one, two):
    columns, nz = v.shape
    face = [jnp.broadcast_to(faces[k, y:y + 1, :], (columns, nz)) for k in range(2)]
    v = v.astype(F32)
    total = partial + face[0] * (v - one.astype(F32))
    return (total + face[1] * (v - two.astype(F32))).astype(BF16)


def gram_of(left, right):
    return lax.dot_general(left, right, (((1,), (1,)), ((), ())), preferred_element_type=F32)


def near_kernel(coef, partial, center, one, two, mine, theirs, faces, flat):
    rows, _, nz = partial.shape
    half = rows // CORES
    core = lax.axis_index("blk") % CORES
    for which, ref in enumerate((one, two)):
        faces[which] = 0.5 * (coef[5] + ref[rows].astype(F32)[:rows])
    for y in range(rows):
        image = image_row(faces, y, partial[y], center[y + 1], one[y], two[y])
        flat[:, y * nz:(y + 1) * nz] = image

        @pl.when(core == y // half)
        def _():
            mine[y % half] = image

        @pl.when(core != y // half)
        def _():
            theirs[y % half] = image


def gather_kernel(chips, coef, *refs):
    count = chips - 1
    firsts, seconds, centers, partials = (refs[i * count:(i + 1) * count] for i in range(4))
    for first, second, center, partial in zip(firsts, seconds, centers, partials):
        half = first.shape[0]
        center[0:half] = first[...]
        center[half:2 * half] = second[...]
        plane_rows(coef, center, partial)


def first_far_kernel(chips, faces, *refs):
    count = chips - 1
    partials, centers, twos, ones, images, flats = (refs[i * count:(i + 1) * count] for i in range(6))
    nz = partials[0].shape[2]
    for k in range(count):
        for y in range(partials[k].shape[0] // 2):
            image = image_row(faces, y, partials[k][y], centers[k][y + 1], ones[k][y + 1], twos[k][y + 1])
            flats[k][:, y * nz:(y + 1) * nz] = image
            images[k][y] = image


def left_kernel(chips, weight, flat, center, plain, *refs):
    count = chips - 1
    flats, centers, other_firsts, other_seconds = (refs[i * count:(i + 1) * count] for i in range(4))
    left, gram = refs[4 * count:]
    columns, nz = center.shape[1:]
    rows = center.shape[0] - 2
    half = rows // 2
    me = lax.axis_index("blk")
    for k, ref in enumerate((center, *centers)):
        for core in range(CORES):
            where = pl.ds(pl.multiple_of((me ^ (CORES * k + core)) * columns, columns), columns)
            for y in range(rows):
                if not core:
                    side = ref[y + 1]
                elif not k:
                    side = plain[y]
                else:
                    side = other_firsts[k - 1][y] if y < half else other_seconds[k - 1][y - half]
                left[where, y * nz:(y + 1) * nz] = side
    gram[:, 0:columns] = weight * gram_of(left[...], flat[...])
    for k in range(count):
        gram[:, (k + 1) * columns:(k + 2) * columns] = weight * gram_of(left[:, 0:half * nz], flats[k][...])


def second_far_kernel(chips, weight, faces, left, first_gram, *refs):
    count = chips - 1
    partials, centers, twos, ones, images, mine, theirs = (refs[i * count:(i + 1) * count] for i in range(7))
    gram = refs[7 * count]
    rows, columns, nz = partials[0].shape
    half = rows // 2
    core = lax.axis_index("blk") % CORES
    slabs, blocks = lax.axis_size("dom"), lax.axis_size("blk")
    share = left.shape[0] // (slabs * blocks)
    values = [first_gram[:, 0:columns]]
    for k in range(count):
        block = slice((k + 1) * columns, (k + 2) * columns)
        total = jnp.zeros((left.shape[0], columns), F32)
        for i in range(0, half, 2):
            pair = []
            for at in (i, i + 1):
                y = half + at
                image = image_row(faces, y, partials[k][y], centers[k][y + 1], ones[k][at], twos[k][at])
                other = images[k][at]
                mine[k][at] = jnp.where(core == 0, other, image)
                theirs[k][at] = jnp.where(core == 0, image, other)
                pair.append(image)
            y = half + i
            total += gram_of(left[:, y * nz:(y + 2) * nz], jnp.concatenate(pair, 1))
        values.append(first_gram[:, block] + weight * total)
    for slab in range(slabs):
        for owner in range(blocks):
            start, place = (slab * blocks + owner) * share, ((slabs - 1 - slab) * blocks + owner) * share
            for k, value in enumerate(values):
                gram[place:place + share, k * columns:(k + 1) * columns] = value[start:start + share]


def turn_out(image, start, applied, wide, turned, sem):
    rows, columns, _ = image.shape
    for y in range(rows):
        wide[pl.ds(y, columns, stride=rows), :] = image[y].astype(F32)
    for c in range(columns):
        turned[c, 0] = wide[c * rows:(c + 1) * rows, :].astype(BF16)
    copy = pltpu.make_async_copy(turned, applied.at[pl.ds(start, columns)], sem)
    copy.start()
    return copy


def first_kernel(mine, theirs, applied, wide, turned, sems):
    me = lax.axis_index("blk")
    columns = mine.shape[1]
    copies = [
        turn_out(image, (me ^ s) * columns, applied, wide.at[s], turned.at[s], sems.at[s])
        for s, image in enumerate((mine, theirs))
    ]
    for copy in copies:
        copy.wait()


def last_kernel(blocks, applied_in, *refs):
    del applied_in
    images, (applied, wide, turned, sems) = refs[:blocks - CORES], refs[blocks - CORES:]
    me = lax.axis_index("blk")
    columns = images[0].shape[1]
    copies = [
        turn_out(image, (me ^ (s + CORES)) * columns, applied, wide.at[s], turned.at[s], sems.at[s])
        for s, image in enumerate(images)
    ]
    for copy in copies:
        copy.wait()


def sum_kernel(slabs, blocks, shares, reduced):
    chips = blocks // CORES
    columns = shares.shape[2] // chips
    for core in range(CORES):
        sums = []
        for chip in range(chips):
            last = (slabs - 1) * blocks + CORES * chip + core
            total = shares[last]
            for slab in range(1, slabs):
                total += shares[last - slab * blocks]
            sums.append(total)
        for target in range(chips):
            parts = [sums[chip][:, (chip ^ target) * columns:((chip ^ target) + 1) * columns] for chip in range(chips)]
            start = (CORES * target + core) * columns
            reduced[:, start:start + columns] = functools.reduce(jnp.add, parts)


def per_device(basis, zone, cond_table, heat_table):
    blocks = lax.axis_size("blk")
    slabs = lax.axis_size("dom")
    chips = blocks // CORES
    count = chips - 1
    columns, planes, ny, nz = basis.shape
    rows = ny // chips
    half = ny // blocks
    total = columns * blocks
    weight = 1.0 / (slabs * planes * ny * nz)
    image = jax.ShapeDtypeStruct((half, columns, nz), BF16)
    center_shape = jax.ShapeDtypeStruct((rows + 2, columns, nz), BF16)
    partial = jax.ShapeDtypeStruct((rows, columns, nz), F32)
    whole = jax.ShapeDtypeStruct((total, 1, half, nz), BF16)
    params = pltpu.CompilerParams(vmem_limit_bytes=32 << 20)
    costly = pl.CostEstimate(flops=COST, bytes_accessed=COST // 8, transcendentals=0)
    cheap = pl.CostEstimate(flops=1, bytes_accessed=1, transcendentals=0)

    def call(kernel, out_shape, inputs, scratch=(), specs=None, out_specs=None, cost=cheap, aliases={}):
        return pl.pallas_call(
            kernel,
            out_shape=out_shape,
            in_specs=specs or [VMEM] * len(inputs),
            out_specs=out_specs or [VMEM] * len(out_shape),
            scratch_shapes=scratch,
            input_output_aliases=aliases,
            compiler_params=params,
            cost_estimate=cost,
        )(*inputs)

    def after(value, *others):
        return lax.optimization_barrier((value, *others))[0]

    def swap(array, s):
        return lax.ppermute(array, "blk", [(i, i ^ s) for i in range(blocks)])

    def exchange(array, offset):
        partner = [((d + offset) ^ 1) - offset for d in range(slabs)]
        return lax.ppermute(array, "dom", [(d, to) for d, to in enumerate(partner) if 0 <= to < slabs])

    def turning(n):
        return [
            pltpu.VMEM((n, columns * half, nz), F32),
            pltpu.VMEM((n, columns, 1, half, nz), BF16),
            pltpu.SemaphoreType.DMA((n,)),
        ]

    sent, center, plain, firsts, seconds = prepare(basis, zone, cond_table, chips)
    two = exchange(sent, 1)
    one = exchange(sent, 0)
    firsts = [swap(array, CORES * (k + 1)) for k, array in enumerate(firsts)]
    coef, near_partial = call(
        functools.partial(plane_kernel, chips),
        (jax.ShapeDtypeStruct((6, rows, nz), F32), partial),
        (zone, cond_table, heat_table, center),
        [pltpu.VMEM((ny + 16, nz), F32)],
        [VMEM, SMEM, SMEM, VMEM],
        cost=costly,
    )
    seconds = [swap(after(array, coef), CORES * (k + 1)) for k, array in enumerate(seconds)]
    firsts = [after(array, coef) for array in firsts]
    first_two = [exchange(array, 1) for array in firsts]
    first_one = [exchange(array, 0) for array in firsts]
    second_two = [exchange(array, 1) for array in seconds]
    second_one = [exchange(array, 0) for array in seconds]
    near_mine, near_theirs, faces, near_flat = call(
        near_kernel,
        (
            image,
            image,
            jax.ShapeDtypeStruct((2, rows, nz), F32),
            jax.ShapeDtypeStruct((columns, rows * nz), BF16),
        ),
        (coef, near_partial, center, one, two),
    )
    results = call(
        functools.partial(gather_kernel, chips), [center_shape] * count + [partial] * count, (coef, *firsts, *seconds)
    )
    centers, partials = results[:count], results[count:]
    plain = swap(after(plain, *seconds), 1)
    other_firsts = [swap(after(array, two)[1:], 1) for array in firsts]
    other_seconds = [swap(after(array, two)[:-1], 1) for array in seconds]
    half_flat = jax.ShapeDtypeStruct((columns, rows * nz // 2), BF16)
    results = call(
        functools.partial(first_far_kernel, chips),
        [image] * count + [half_flat] * count,
        (faces, *partials, *centers, *first_two, *first_one),
    )
    images, flats = results[:count], results[count:]
    applied, = call(
        first_kernel, (whole,), (near_mine, swap(near_theirs, 1)), turning(CORES), out_specs=[ANY]
    )
    gram_shape = jax.ShapeDtypeStruct((total, chips * columns), F32)
    left, first_gram = call(
        functools.partial(left_kernel, chips, weight),
        (jax.ShapeDtypeStruct((total, rows * nz), BF16), gram_shape),
        (near_flat, center, plain, *flats, *centers, *other_firsts, *other_seconds),
    )
    *images, gram = call(
        functools.partial(second_far_kernel, chips, weight),
        [image] * (2 * count) + [gram_shape],
        (faces, left, first_gram, *partials, *centers, *second_two, *second_one, *images),
    )
    parts = slabs * blocks
    order = [[slab * blocks + b for slab in reversed(range(slabs)) for b in range(blocks)]]
    shares = gram.reshape(parts, total // parts, chips * columns)
    shares = lax.all_to_all(
        shares, ("dom", "blk"), split_axis=0, concat_axis=0, tiled=True, axis_index_groups=order
    )
    pieces = []
    for k in range(count):
        pieces += [images[k], swap(images[count + k], 1)]
    applied, = call(
        functools.partial(last_kernel, blocks),
        (whole,),
        (applied, *pieces),
        turning(len(pieces)),
        [ANY] + [VMEM] * len(pieces),
        [ANY],
        aliases={0: 0},
    )
    reduced, = call(
        functools.partial(sum_kernel, slabs, blocks), (jax.ShapeDtypeStruct((total // parts, total), F32),), (after(shares, applied),)
    )
    return applied, reduced


def solution(mesh):
    placed = (P("blk", "dom", "roll", None), P("dom", "roll", None), P(), P())
    return jax.shard_map(
        per_device,
        mesh=mesh,
        in_specs=placed,
        out_specs=(P("roll", "dom", "blk", None), P(("dom", "blk"), "roll")),
        check_vma=False,
    )
```

```python
import functools

import jax
import jax.numpy as jnp
from jax import lax
from jax.experimental import pallas as pl
from jax.experimental.pallas import tpu as pltpu
from jax.sharding import PartitionSpec as P

ZONES = 16
CORES = 2
COST = 1 << 30
F32 = jnp.float32
BF16 = jnp.bfloat16
VMEM = pl.BlockSpec(memory_space=pltpu.VMEM)
SMEM = pl.BlockSpec(memory_space=pltpu.SMEM)
HBM = pl.BlockSpec(memory_space=pltpu.HBM)
ANY = pl.BlockSpec(memory_space=pl.ANY)


def lookup(zone, table_ref):
    result = jnp.zeros(zone.shape, F32)
    for which in range(ZONES):
        result = jnp.where(zone == which, table_ref[which], result)
    return result


def cond_of(zone, table_ref):
    return lookup(zone, table_ref).astype(BF16).astype(F32)


def prepare_kernel(chips, basis_hbm, zone_hbm, cond_hbm, *refs):
    near, center, plain, firsts, seconds = *refs[:3], refs[3:2 + chips], refs[2 + chips:2 * chips + 1]
    basis, zone, table, wide, turned, cond_pad, in_sems, out_sems = refs[2 * chips + 1:]
    columns, _, ny, nz = basis.shape
    rows = ny // chips
    chip = lax.axis_index("blk") // CORES
    step = 16
    chunks = columns // step
    pitch = wide.shape[0] // columns
    loads = [
        pltpu.make_async_copy(basis_hbm.at[pl.ds(i * step, step)], basis.at[pl.ds(i * step, step)], in_sems.at[i])
        for i in range(chunks)
    ]
    loads.append(pltpu.make_async_copy(zone_hbm, zone, in_sems.at[chunks]))
    loads.append(pltpu.make_async_copy(cond_hbm, table, in_sems.at[chunks + 1]))
    for load in loads:
        load.start()
    turned[0] = jnp.zeros((columns, nz), BF16)
    turned[ny + 1] = jnp.zeros((columns, nz), BF16)
    stores = []

    def store(source, target):
        copy = pltpu.make_async_copy(source, target, out_sems.at[len(stores)])
        copy.start()
        stores.append(copy)

    for i in range(chunks):
        if i == chunks - 1:
            loads[chunks].wait()
            loads[chunks + 1].wait()
            mine = zone[0, pl.ds(pl.multiple_of(chip * rows, rows), rows), :]
            own = cond_of(mine, table)
            cond_pad[...] = jnp.concatenate([own, jnp.zeros((columns - rows, nz), F32)], 0).astype(BF16)
            store(cond_pad, near.at[rows])
        loads[i].wait()
        some = pl.ds(i * step, step)
        for c in range(i * step, (i + 1) * step):
            wide[c * pitch:c * pitch + ny, :] = basis[c, 0].astype(F32)
        for y in range(ny):
            turned[y + 1, some, :] = wide[pl.ds(i * step * pitch + y, step, stride=pitch), :].astype(BF16)
        store(turned.at[pl.ds(chip * rows + 1, rows), some], near.at[pl.ds(0, rows), some])
        for k in range(1, chips):
            start = (chip ^ k) * rows
            store(turned.at[pl.ds(start, rows // 2 + 1), some], firsts[k - 1].at[:, some])
            store(turned.at[pl.ds(start + rows // 2 + 1, rows // 2 + 1), some], seconds[k - 1].at[:, some])
        store(turned.at[pl.ds(chip * rows, rows + 2), some], center.at[:, some])
        store(turned.at[pl.ds(chip * rows + 1, rows), some], plain.at[:, some])
    for copy in stores:
        copy.wait()


def prepare(basis, zone, cond_table, chips):
    columns, _, ny, nz = basis.shape
    rows = ny // chips
    slabs = [rows + 1, rows + 2, rows] + [rows // 2 + 1] * (2 * chips - 2)
    shapes = [jax.ShapeDtypeStruct((n, columns, nz), BF16) for n in slabs]
    results = pl.pallas_call(
        functools.partial(prepare_kernel, chips),
        out_shape=shapes,
        in_specs=[HBM, HBM, HBM],
        out_specs=[pl.BlockSpec(memory_space=pl.ANY)] * len(shapes),
        scratch_shapes=[
            pltpu.VMEM(basis.shape, BF16),
            pltpu.VMEM(zone.shape, jnp.int32),
            pltpu.SMEM((ZONES,), F32),
            pltpu.VMEM((columns * (ny + 8), nz), F32),
            pltpu.VMEM((ny + 2, columns, nz), BF16),
            pltpu.VMEM((columns, nz), BF16),
            pltpu.SemaphoreType.DMA((columns // 16 + 2,)),
            pltpu.SemaphoreType.DMA((1 + (2 * chips + 1) * (columns // 16),)),
        ],
        compiler_params=pltpu.CompilerParams(vmem_limit_bytes=16 << 20),
    )(*[pltpu.with_memory_space_constraint(x, pltpu.HBM) for x in (basis, zone, cond_table)])
    return (*results[:3], results[3:2 + chips], results[2 + chips:])


def plane_kernel(chips, zone_ref, cond_ref, heat_ref, center, coef, partial, cond_pad):
    rows = partial.shape[0]
    nz = center.shape[2]
    ny = zone_ref.shape[1]
    chip = lax.axis_index("blk") // CORES
    cond_pad[0:8, :] = jnp.zeros((8, nz), F32)
    cond_pad[8:8 + ny, :] = cond_of(zone_ref[0], cond_ref)
    cond_pad[8 + ny:16 + ny, :] = jnp.zeros((8, nz), F32)
    base = pl.multiple_of(chip * rows, 8)
    near = cond_pad[pl.ds(base, rows + 16), :]
    own = near[8:8 + rows]
    lane = lax.broadcasted_iota(jnp.int32, (rows, nz), 1)
    coef[0] = lookup(zone_ref[0, pl.ds(base, rows), :], heat_ref)
    beside = (
        near[7:7 + rows],
        near[9:9 + rows],
        jnp.where(lane == 0, 0.0, pltpu.roll(own, 1, 1)),
        jnp.where(lane == nz - 1, 0.0, pltpu.roll(own, nz - 1, 1)),
    )
    for which, other in enumerate(beside):
        coef[1 + which] = 0.5 * (own + other)
    coef[5] = own
    plane_rows(coef, center, partial)


def plane_rows(coef, center, partial):
    columns, nz = center.shape[1:]
    lane = lax.broadcasted_iota(jnp.int32, (columns, nz), 1)
    first, last = lane == 0, lane == nz - 1
    for y in range(partial.shape[0]):
        face = [jnp.broadcast_to(coef[k, y:y + 1, :], (columns, nz)) for k in range(5)]
        v = center[y + 1].astype(F32)
        total = face[0] * v
        total += face[1] * (v - center[y].astype(F32))
        total += face[2] * (v - center[y + 2].astype(F32))
        total += face[3] * (v - jnp.where(first, 0.0, pltpu.roll(v, 1, 1)))
        total += face[4] * (v - jnp.where(last, 0.0, pltpu.roll(v, nz - 1, 1)))
        partial[y] = total


def image_row(faces, y, partial, v, one, two):
    columns, nz = v.shape
    face = [jnp.broadcast_to(faces[k, y:y + 1, :], (columns, nz)) for k in range(2)]
    v = v.astype(F32)
    total = partial + face[0] * (v - one.astype(F32))
    return (total + face[1] * (v - two.astype(F32))).astype(BF16)


def gram_of(left, right):
    return lax.dot_general(left, right, (((1,), (1,)), ((), ())), preferred_element_type=F32)


def near_kernel(coef, partial, center, one, two, mine, theirs, faces, flat):
    rows, _, nz = partial.shape
    half = rows // CORES
    core = lax.axis_index("blk") % CORES
    for which, ref in enumerate((one, two)):
        faces[which] = 0.5 * (coef[5] + ref[rows].astype(F32)[:rows])
    for y in range(rows):
        image = image_row(faces, y, partial[y], center[y + 1], one[y], two[y])
        flat[:, y * nz:(y + 1) * nz] = image

        @pl.when(core == y // half)
        def _():
            mine[y % half] = image

        @pl.when(core != y // half)
        def _():
            theirs[y % half] = image


def gather_kernel(chips, coef, *refs):
    count = chips - 1
    firsts, seconds, centers, partials = (refs[i * count:(i + 1) * count] for i in range(4))
    for first, second, center, partial in zip(firsts, seconds, centers, partials):
        half = first.shape[0]
        center[0:half] = first[...]
        center[half:2 * half] = second[...]
        plane_rows(coef, center, partial)


def first_far_kernel(chips, faces, *refs):
    count = chips - 1
    partials, centers, twos, ones, images, flats = (refs[i * count:(i + 1) * count] for i in range(6))
    nz = partials[0].shape[2]
    for k in range(count):
        for y in range(partials[k].shape[0] // 2):
            image = image_row(faces, y, partials[k][y], centers[k][y + 1], ones[k][y + 1], twos[k][y + 1])
            flats[k][:, y * nz:(y + 1) * nz] = image
            images[k][y] = image


def left_kernel(chips, weight, flat, center, plain, *refs):
    count = chips - 1
    flats, centers, other_firsts, other_seconds = (refs[i * count:(i + 1) * count] for i in range(4))
    left, gram = refs[4 * count:]
    columns, nz = center.shape[1:]
    rows = center.shape[0] - 2
    half = rows // 2
    me = lax.axis_index("blk")
    for k, ref in enumerate((center, *centers)):
        for core in range(CORES):
            where = pl.ds(pl.multiple_of((me ^ (CORES * k + core)) * columns, columns), columns)
            for y in range(rows):
                if not core:
                    side = ref[y + 1]
                elif not k:
                    side = plain[y]
                else:
                    side = other_firsts[k - 1][y] if y < half else other_seconds[k - 1][y - half]
                left[where, y * nz:(y + 1) * nz] = side
    gram[:, 0:columns] = weight * gram_of(left[...], flat[...])
    for k in range(count):
        gram[:, (k + 1) * columns:(k + 2) * columns] = weight * gram_of(left[:, 0:half * nz], flats[k][...])


def second_far_kernel(chips, weight, faces, left, first_gram, *refs):
    count = chips - 1
    partials, centers, twos, ones, images, mine, theirs = (refs[i * count:(i + 1) * count] for i in range(7))
    gram = refs[7 * count]
    rows, columns, nz = partials[0].shape
    half = rows // 2
    core = lax.axis_index("blk") % CORES
    slabs, blocks = lax.axis_size("dom"), lax.axis_size("blk")
    share = left.shape[0] // (slabs * blocks)
    values = [first_gram[:, 0:columns]]
    for k in range(count):
        block = slice((k + 1) * columns, (k + 2) * columns)
        total = jnp.zeros((left.shape[0], columns), F32)
        for i in range(0, half, 2):
            pair = []
            for at in (i, i + 1):
                y = half + at
                image = image_row(faces, y, partials[k][y], centers[k][y + 1], ones[k][at], twos[k][at])
                other = images[k][at]
                mine[k][at] = jnp.where(core == 0, other, image)
                theirs[k][at] = jnp.where(core == 0, image, other)
                pair.append(image)
            y = half + i
            total += gram_of(left[:, y * nz:(y + 2) * nz], jnp.concatenate(pair, 1))
        values.append(first_gram[:, block] + weight * total)
    for slab in range(slabs):
        for owner in range(blocks):
            start, place = (slab * blocks + owner) * share, (slabs * blocks - 1 - slab * blocks - owner) * share
            for k, value in enumerate(values):
                gram[place:place + share, k * columns:(k + 1) * columns] = value[start:start + share]


def turn_out(image, start, applied, wide, turned, sem):
    rows, columns, _ = image.shape
    for y in range(rows):
        wide[pl.ds(y, columns, stride=rows + 8), :] = image[y].astype(F32)
    for c in range(columns):
        turned[c, 0] = wide[c * (rows + 8):c * (rows + 8) + rows, :].astype(BF16)
    copy = pltpu.make_async_copy(turned, applied.at[pl.ds(start, columns)], sem)
    copy.start()
    return copy


def first_kernel(mine, theirs, applied, wide, turned, sems):
    me = lax.axis_index("blk")
    columns = mine.shape[1]
    copies = [
        turn_out(image, (me ^ s) * columns, applied, wide.at[s], turned.at[s], sems.at[s])
        for s, image in enumerate((mine, theirs))
    ]
    for copy in copies:
        copy.wait()


def last_kernel(blocks, applied_in, *refs):
    del applied_in
    images, (applied, wide, turned, sems) = refs[:blocks - CORES], refs[blocks - CORES:]
    me = lax.axis_index("blk")
    columns = images[0].shape[1]
    copies = [
        turn_out(image, (me ^ (s + CORES)) * columns, applied, wide.at[s], turned.at[s], sems.at[s])
        for s, image in enumerate(images)
    ]
    for copy in copies:
        copy.wait()


def sum_kernel(slabs, blocks, shares, reduced):
    chips = blocks // CORES
    columns = shares.shape[2] // chips
    for core in range(CORES):
        sums = []
        for chip in range(chips):
            last = slabs * blocks - 1 - (CORES * chip + core)
            total = shares[last]
            for slab in range(1, slabs):
                total += shares[last - slab * blocks]
            sums.append(total)
        for target in range(chips):
            parts = [sums[chip][:, (chip ^ target) * columns:((chip ^ target) + 1) * columns] for chip in range(chips)]
            start = (CORES * target + core) * columns
            reduced[:, start:start + columns] = functools.reduce(jnp.add, parts)


def per_device(basis, zone, cond_table, heat_table):
    blocks = lax.axis_size("blk")
    slabs = lax.axis_size("dom")
    chips = blocks // CORES
    count = chips - 1
    columns, planes, ny, nz = basis.shape
    rows = ny // chips
    half = ny // blocks
    total = columns * blocks
    weight = 1.0 / (slabs * planes * ny * nz)
    image = jax.ShapeDtypeStruct((half, columns, nz), BF16)
    center_shape = jax.ShapeDtypeStruct((rows + 2, columns, nz), BF16)
    partial = jax.ShapeDtypeStruct((rows, columns, nz), F32)
    whole = jax.ShapeDtypeStruct((total, 1, half, nz), BF16)
    params = pltpu.CompilerParams(vmem_limit_bytes=32 << 20)
    costly = pl.CostEstimate(flops=COST, bytes_accessed=COST // 8, transcendentals=0)
    cheap = pl.CostEstimate(flops=1, bytes_accessed=1, transcendentals=0)

    def call(kernel, out_shape, inputs, scratch=(), specs=None, out_specs=None, cost=cheap, aliases={}):
        return pl.pallas_call(
            kernel,
            out_shape=out_shape,
            in_specs=specs or [VMEM] * len(inputs),
            out_specs=out_specs or [VMEM] * len(out_shape),
            scratch_shapes=scratch,
            input_output_aliases=aliases,
            compiler_params=params,
            cost_estimate=cost,
        )(*inputs)

    def after(value, *others):
        return lax.optimization_barrier((value, *others))[0]

    def swap(array, s):
        return lax.ppermute(array, "blk", [(i, i ^ s) for i in range(blocks)])

    def exchange(array, offset):
        partner = [((d + offset) ^ 1) - offset for d in range(slabs)]
        return lax.ppermute(array, "dom", [(d, to) for d, to in enumerate(partner) if 0 <= to < slabs])

    def turning(n):
        return [
            pltpu.VMEM((n, columns * (half + 8), nz), F32),
            pltpu.VMEM((n, columns, 1, half, nz), BF16),
            pltpu.SemaphoreType.DMA((n,)),
        ]

    sent, center, plain, firsts, seconds = prepare(basis, zone, cond_table, chips)
    two = exchange(sent, 1)
    one = exchange(sent, 0)
    firsts = [swap(array, CORES * (k + 1)) for k, array in enumerate(firsts)]
    coef, near_partial = call(
        functools.partial(plane_kernel, chips),
        (jax.ShapeDtypeStruct((6, rows, nz), F32), partial),
        (zone, cond_table, heat_table, center),
        [pltpu.VMEM((ny + 16, nz), F32)],
        [VMEM, SMEM, SMEM, VMEM],
        cost=costly,
    )
    seconds = [swap(after(array, coef), CORES * (k + 1)) for k, array in enumerate(seconds)]
    firsts = [after(array, coef) for array in firsts]
    first_two = [exchange(array, 1) for array in firsts]
    first_one = [exchange(array, 0) for array in firsts]
    second_two = [exchange(array, 1) for array in seconds]
    second_one = [exchange(array, 0) for array in seconds]
    near_mine, near_theirs, faces, near_flat = call(
        near_kernel,
        (
            image,
            image,
            jax.ShapeDtypeStruct((2, rows, nz), F32),
            jax.ShapeDtypeStruct((columns, rows * nz), BF16),
        ),
        (coef, near_partial, center, one, two),
    )
    results = call(
        functools.partial(gather_kernel, chips), [center_shape] * count + [partial] * count, (coef, *firsts, *seconds)
    )
    centers, partials = results[:count], results[count:]
    plain = swap(after(plain, *seconds), 1)
    other_firsts = [swap(after(array, two)[1:], 1) for array in firsts]
    other_seconds = [swap(after(array, two)[:-1], 1) for array in seconds]
    half_flat = jax.ShapeDtypeStruct((columns, rows * nz // 2), BF16)
    results = call(
        functools.partial(first_far_kernel, chips),
        [image] * count + [half_flat] * count,
        (faces, *partials, *centers, *first_two, *first_one),
    )
    images, flats = results[:count], results[count:]
    applied, = call(
        first_kernel, (whole,), (near_mine, swap(near_theirs, 1)), turning(CORES), out_specs=[ANY]
    )
    gram_shape = jax.ShapeDtypeStruct((total, chips * columns), F32)
    left, first_gram = call(
        functools.partial(left_kernel, chips, weight),
        (jax.ShapeDtypeStruct((total, rows * nz), BF16), gram_shape),
        (near_flat, center, plain, *flats, *centers, *other_firsts, *other_seconds),
    )
    *images, gram = call(
        functools.partial(second_far_kernel, chips, weight),
        [image] * (2 * count) + [gram_shape],
        (faces, left, first_gram, *partials, *centers, *second_two, *second_one, *images),
    )
    parts = slabs * blocks
    shares = gram.reshape(parts, total // parts, chips * columns)
    shares = lax.all_to_all(
        shares, ("dom", "blk"), split_axis=0, concat_axis=0, tiled=True, axis_index_groups=[[*reversed(range(parts))]]
    )
    pieces = []
    for k in range(count):
        pieces += [images[k], swap(images[count + k], 1)]
    applied, = call(
        functools.partial(last_kernel, blocks),
        (whole,),
        (applied, *pieces),
        turning(len(pieces)),
        [ANY] + [VMEM] * len(pieces),
        [ANY],
        aliases={0: 0},
    )
    reduced, = call(
        functools.partial(sum_kernel, slabs, blocks), (jax.ShapeDtypeStruct((total // parts, total), F32),), (after(shares, applied),)
    )
    return applied, reduced


def solution(mesh):
    placed = (P("blk", "dom", "roll", None), P("dom", "roll", None), P(), P())
    return jax.shard_map(
        per_device,
        mesh=mesh,
        in_specs=placed,
        out_specs=(P("roll", "dom", "blk", None), P(("dom", "blk"), "roll")),
        check_vma=False,
    )
```
